32 devices in a mesh: blk: 8 (over y, x, core), layer: 4 (over z).
Axes of the slice: x: 2, y: 2, z: 4, core: 2. Of those that a mesh axis runs over, the one named last changes fastest.
Arguments:
- flow_t: bfloat16 [8, 8192, 1536], P('blk', 'layer'), may hold values from 0.1 to 100, as said below
- graph: bfloat16 [8, 8192, 1536], P('blk', 'layer'), may hold values from 0.1 to 100, as said below
- a_pattern: int32 [8, 32, 6], P('blk'), may hold values 0 or 1
- b_pattern: int32 [8, 32, 6], P('blk'), may hold values 0 or 1
- c_pattern: int32 [8, 6, 2], P('blk'), may hold values 0 or 1
Outputs:
- next_flow: float32 [8, 1536, 512], P('blk', 'layer')
The draws below stay inside these ranges and needn't reach their ends.
Inputs may be any that keep to these rules, and one draw needn't show every extreme that they name: `flow_t`: positive entries. `graph`: positive entries.
All inputs are finite; a program needn't handle non-finite values. No bound on the sum of `a_pattern` or of `b_pattern` or of `c_pattern` on one device may be relied on, other than what follows from the above.
Results may differ from the reference program's by a relative error of at most 0.0003.
Values may be sent and summed in bfloat16 or wider, within the bound.
No kernel may reach another device: no remote copies, remote signals or barrier semaphores. Data moves between devices by JAX's collectives and lax.ppermute only.
A program may use at most 64 MiB of HBM per device.

```python
import math
import jax
import jax.numpy as jnp
from jax import lax

BS = 256
PB = 2
KB = 32
N_BLK = 8


def scaled_entries(key, inner_dim, outer_dim):
    keys = jax.random.split(key, 3)
    shape = (N_BLK, inner_dim, outer_dim)
    base = jax.random.uniform(keys[0], shape, jnp.float32, 0.1, 1.0)
    inner_scale = jnp.exp(jax.random.uniform(keys[1], (N_BLK, inner_dim, 1), jnp.float32, 0.0, math.log(10.0)))
    outer_scale = jnp.exp(jax.random.uniform(keys[2], (N_BLK, 1, outer_dim), jnp.float32, 0.0, math.log(10.0)))
    return (base * inner_scale * outer_scale).astype(jnp.bfloat16)


def draw_flow_t(key, part):
    return scaled_entries(jax.random.fold_in(key, 11), KB * BS, 3 * PB * BS)


def draw_graph(key, part):
    return scaled_entries(jax.random.fold_in(key, 23), KB * BS, 3 * PB * BS)


def place_ends(values, rng, least, largest):
    dims = values.shape
    index_at = [jax.random.randint(jax.random.fold_in(rng, axis), (), 0, dims[axis]) for axis in range(len(dims))]
    values = values.at[tuple(index_at)].set(least)
    longest = dims.index(max(dims))
    index_at[longest] = (index_at[longest] + 1) % dims[longest]
    return values.at[tuple(index_at)].set(largest)


def setup_inputs(seed: int = 0) -> dict:
    streams_of = jax.random.split(jax.random.key(seed), 6)
    flow_t = draw_flow_t(jax.random.fold_in(streams_of[5], 71), 0)
    graph = draw_graph(jax.random.fold_in(streams_of[5], 71), 0)
    a_pattern = place_ends((jax.random.randint(streams_of[2], (N_BLK, KB, 3 * PB), 0, 4) < 3).astype(jnp.int32), jax.random.fold_in(streams_of[2], 1), 0, 1)
    b_pattern = place_ends((jax.random.randint(streams_of[3], (N_BLK, KB, 3 * PB), 0, 4) < 3).astype(jnp.int32), jax.random.fold_in(streams_of[3], 1), 0, 1)
    c_pattern = place_ends((jax.random.randint(streams_of[4], (N_BLK, 3 * PB, PB), 0, 4) < 3).astype(jnp.int32), jax.random.fold_in(streams_of[4], 1), 0, 1)
    return dict(flow_t=flow_t, graph=graph, a_pattern=a_pattern, b_pattern=b_pattern, c_pattern=c_pattern)


def expand(pattern):
    wide = jnp.repeat(jnp.repeat(pattern, BS, axis=1), BS, axis=2)
    return wide.astype(jnp.float32)


def reference(flow_t, graph, a_pattern, b_pattern, c_pattern):
    panel_cols = PB * BS
    highest = lax.Precision.HIGHEST
    flow_masked = (flow_t.astype(jnp.float32) * expand(a_pattern)).astype(jnp.bfloat16).astype(jnp.float32)
    graph_masked = (graph.astype(jnp.float32) * expand(b_pattern)).astype(jnp.bfloat16).astype(jnp.float32)
    own_part = jnp.einsum("pkr,pkc->prc", flow_masked, graph_masked[:, :, panel_cols:2 * panel_cols], precision=highest)
    left_part = jnp.einsum("pkr,pkc->prc", flow_masked[:, :, :2 * panel_cols], graph_masked[:, :, :panel_cols], precision=highest)
    right_part = jnp.einsum("pkr,pkc->prc", flow_masked[:, :, panel_cols:], graph_masked[:, :, 2 * panel_cols:], precision=highest)
    from_above = jnp.roll(left_part, -1, axis=0)
    from_below = jnp.roll(right_part, 1, axis=0)
    product = own_part + jnp.pad(from_above, ((0, 0), (panel_cols, 0), (0, 0)))
    product = product + jnp.pad(from_below, ((0, 0), (0, panel_cols), (0, 0)))
    kept_blocks = product * expand(c_pattern)
    squared = kept_blocks * kept_blocks
    col_mean = jnp.sum(squared, axis=1, keepdims=True) / (3.0 * panel_cols)
    return squared / (col_mean + 1e-6)
```

```python
import functools

import jax
import jax.numpy as jnp
from jax import lax
from jax.experimental import pallas as pl
from jax.experimental.pallas import tpu as pltpu
from jax.sharding import PartitionSpec as P

BS = 256
LANES = 128
HEAD = 16
STEPS = 256.0
TOP = 65534.0
LN2 = 0.6931471805599453
VMEM_LIMIT = 40 * 1024 * 1024
SMEM = pltpu.SMEM
VMEM = pltpu.VMEM


def from_behind(block, axis, distance):
    devices = range(lax.axis_size(axis))
    route = [((i - distance) % len(devices), i) for i in devices]
    return lax.ppermute(block, axis, route)


def from_partner(block, axis, bit):
    return lax.ppermute(block, axis, [(i ^ bit, i) for i in range(lax.axis_size(axis))])


def store_coded(ref, values, group):
    rows, width = values.shape
    line = lax.broadcasted_iota(jnp.int32, (HEAD, width), 0)
    head = jnp.zeros((HEAD, width), jnp.float32)
    for g in range(rows // group):
        part = values[g * group : (g + 1) * group]
        largest = jnp.maximum(jnp.max(part, axis=0, keepdims=True), 1e-3)
        power = jnp.floor(jnp.log(largest) * (STEPS / LN2)) + 2.0
        head = jnp.where(line == g, power, head)
        codes = (part * (TOP * jnp.exp(power * (-LN2 / STEPS))) + 0.5).astype(jnp.int32) - 32767
        ref[HEAD + g * group : HEAD + (g + 1) * group, :] = codes.astype(jnp.int16)
    ref[0:HEAD, :] = head.astype(jnp.int32).astype(jnp.int16)


def load_coded(ref, group):
    rows = ref.shape[0] - HEAD
    scales = jnp.exp(ref[0:HEAD, :].astype(jnp.int32).astype(jnp.float32) * (LN2 / STEPS)) * (1.0 / TOP)
    parts = []
    for g in range(rows // group):
        codes = ref[HEAD + g * group : HEAD + (g + 1) * group, :].astype(jnp.int32) + 32767
        parts.append(codes.astype(jnp.float32) * scales[g : g + 1])
    return parts


def mask_row(pattern, inner, first, count):
    column = lax.broadcasted_iota(jnp.int32, (1, count * BS), 1) // BS
    line = jnp.zeros((1, count * BS), jnp.float32)
    for v in range(count):
        line = jnp.where(column == v, pattern[first + v, 0, inner].astype(jnp.float32), line)
    return line.astype(jnp.bfloat16)


def masked(ref, pattern, inner, first):
    depth, width = ref.shape
    return jnp.concatenate(
        [
            ref[t * BS : (t + 1) * BS, :] * mask_row(pattern, inner + t, first, width // BS)
            for t in range(depth // BS)
        ],
        axis=0,
    )


def contract(left_side, right_side):
    return lax.dot_general(
        left_side, right_side, (((0,), (0,)), ((), ())), preferred_element_type=jnp.float32
    )


def side_kernel(inner_blocks, half, panel, a_ref, b_ref, flow_ref, left_ref, right_ref, *rest):
    outs, (right_sum, left_sum) = rest[:-2], rest[-2:]
    step = pl.program_id(0)
    depth = flow_ref.shape[0]
    inner = lax.axis_index("layer") * inner_blocks + step * (depth // BS)
    last_side = 2 * panel // BS
    flow = masked(flow_ref, a_ref, inner, 0)
    to_right = contract(flow[:, panel:], masked(right_ref, b_ref, inner, last_side + half))
    to_left = contract(flow[:, : 2 * panel], masked(left_ref, b_ref, inner, half))

    @pl.when(step == 0)
    def _():
        right_sum[...] = to_right
        left_sum[...] = to_left

    @pl.when(step > 0)
    def _():
        right_sum[...] += to_right
        left_sum[...] += to_left

    @pl.when(step == pl.num_programs(0) - 1)
    def _():
        chunks = len(outs) // 2
        for c in range(chunks):
            store_coded(outs[2 * c], right_sum[:, c * LANES : (c + 1) * LANES], BS)
            store_coded(outs[2 * c + 1], left_sum[:, c * LANES : (c + 1) * LANES], BS)


def side_products(flow_t, graph, a_lines, b_lines, half, depth):
    inner, width = flow_t.shape[1:]
    panel = width // 3
    per_half = BS // LANES
    coded = jax.ShapeDtypeStruct((HEAD + 2 * panel, LANES), jnp.int16)
    whole = pl.BlockSpec(coded.shape, lambda k, *_: (0, 0))
    last_side = 2 * panel // BS
    return pl.pallas_call(
        functools.partial(side_kernel, inner // BS, half, panel),
        out_shape=[coded] * (2 * per_half),
        grid_spec=pltpu.PrefetchScalarGridSpec(
            num_scalar_prefetch=2,
            grid=(inner // depth,),
            in_specs=[
                pl.BlockSpec((None, depth, width), lambda k, *_: (0, k, 0)),
                pl.BlockSpec((None, depth, BS), lambda k, *_: (0, k, half)),
                pl.BlockSpec((None, depth, BS), lambda k, *_: (0, k, last_side + half)),
            ],
            out_specs=[whole] * (2 * per_half),
            scratch_shapes=[pltpu.VMEM((2 * panel, BS), jnp.float32)] * 2,
        ),
        compiler_params=pltpu.CompilerParams(vmem_limit_bytes=VMEM_LIMIT),
        cost_estimate=pl.CostEstimate(
            flops=2 * inner * 4 * panel * BS, bytes_accessed=2 * inner * (width + 2 * BS), transcendentals=0
        ),
        name=f"side_products_{half}",
    )(a_lines, b_lines, flow_t, graph, graph)


def own_kernel(inner_blocks, panel, a_ref, b_ref, flow_ref, mid_ref, out_ref):
    step = pl.program_id(0)
    inner = lax.axis_index("layer") * inner_blocks + step * (flow_ref.shape[0] // BS)
    part = contract(masked(flow_ref, a_ref, inner, 0), masked(mid_ref, b_ref, inner, panel // BS))

    @pl.when(step == 0)
    def _():
        out_ref[...] = part

    @pl.when(step > 0)
    def _():
        out_ref[...] += part


def own_product(flow_t, graph, a_lines, b_lines, depth):
    inner, width = flow_t.shape[1:]
    panel = width // 3
    return pl.pallas_call(
        functools.partial(own_kernel, inner // BS, panel),
        out_shape=jax.ShapeDtypeStruct((width, panel), jnp.float32),
        grid_spec=pltpu.PrefetchScalarGridSpec(
            num_scalar_prefetch=2,
            grid=(inner // depth,),
            in_specs=[
                pl.BlockSpec((None, depth, width), lambda k, *_: (0, k, 0)),
                pl.BlockSpec((None, depth, panel), lambda k, *_: (0, k, 1)),
            ],
            out_specs=pl.BlockSpec((width, panel), lambda k, *_: (0, 0)),
        ),
        compiler_params=pltpu.CompilerParams(vmem_limit_bytes=VMEM_LIMIT),
        cost_estimate=pl.CostEstimate(
            flops=2 * inner * width * panel, bytes_accessed=2 * inner * (width + panel), transcendentals=0
        ),
        name="own_product",
    )(a_lines, b_lines, flow_t, graph)


def whole_call(kernel, name, out_shape, in_specs, operands, scratch_shapes=(), moved=0):
    return pl.pallas_call(
        kernel,
        out_shape=out_shape,
        in_specs=in_specs,
        out_specs=jax.tree.map(lambda _: pl.BlockSpec(memory_space=VMEM), out_shape),
        scratch_shapes=list(scratch_shapes),
        compiler_params=pltpu.CompilerParams(vmem_limit_bytes=VMEM_LIMIT),
        cost_estimate=pl.CostEstimate(flops=moved, bytes_accessed=moved, transcendentals=0),
        name=name,
    )(*operands)


def split_strips(total, rows, position, keep_ref, send_ref):
    bit = lax.rem(lax.axis_index("layer") // position, 2)
    pairs = keep_ref.shape[0]
    for j in range(pairs):
        keep_ref[j] = total[pl.ds((2 * j + bit) * rows, rows), :]
    away = [total[pl.ds((2 * j + 1 - bit) * rows, rows), :] for j in range(pairs)]
    store_coded(send_ref, jnp.concatenate(away, axis=0), pairs * rows)


def join_kernel(rows, chunk, c_ref, own_ref, below_ref, above_ref, keep_ref, send_ref, total):
    panel_blocks = own_ref.shape[0] // BS // 3
    below = load_coded(below_ref, BS)
    above = load_coded(above_ref, BS)
    for v in range(3 * panel_blocks):
        block = own_ref[v * BS : (v + 1) * BS, :]
        if v < 2 * panel_blocks:
            block = block + below[v]
        if v >= panel_blocks:
            block = block + above[v - panel_blocks]
        kept = c_ref[0, chunk * LANES // BS, v].astype(jnp.float32)
        total[v * BS : (v + 1) * BS, :] = block * kept
    split_strips(total, rows, 1, keep_ref, send_ref)


def join(own, below, above, c_lines, chunk, layers):
    height = own.shape[0]
    rows = height // layers
    pairs = layers // 2
    return pl.pallas_call(
        functools.partial(join_kernel, rows, chunk),
        out_shape=[
            jax.ShapeDtypeStruct((pairs, rows, LANES), jnp.float32),
            jax.ShapeDtypeStruct((HEAD + pairs * rows, LANES), jnp.int16),
        ],
        grid=(1,),
        in_specs=[
            pl.BlockSpec(memory_space=SMEM),
            pl.BlockSpec((height, LANES), lambda i: (0, chunk)),
            pl.BlockSpec(below.shape, lambda i: (0, 0)),
            pl.BlockSpec(above.shape, lambda i: (0, 0)),
        ],
        out_specs=[
            pl.BlockSpec((pairs, rows, LANES), lambda i: (0, 0, 0)),
            pl.BlockSpec((HEAD + pairs * rows, LANES), lambda i: (0, 0)),
        ],
        scratch_shapes=[pltpu.VMEM((height, LANES), jnp.float32)],
        compiler_params=pltpu.CompilerParams(vmem_limit_bytes=VMEM_LIMIT),
        cost_estimate=pl.CostEstimate(flops=8 * height * LANES, bytes_accessed=8 * height * LANES, transcendentals=0),
        name=f"join_{chunk}",
    )(c_lines, own, below, above)


def halve_kernel(rows, position, kept_ref, got_ref, keep_ref, send_ref, total):
    strips = kept_ref.shape[0]
    (got,) = load_coded(got_ref, strips * rows)
    for j in range(strips):
        total[j * rows : (j + 1) * rows, :] = kept_ref[j] + got[j * rows : (j + 1) * rows]
    split_strips(total, rows, position, keep_ref, send_ref)


def halve(kept, got, position, chunk):
    strips, rows, _ = kept.shape
    pairs = strips // 2
    return whole_call(
        functools.partial(halve_kernel, rows, position),
        f"halve_{position}_{chunk}",
        [
            jax.ShapeDtypeStruct((pairs, rows, LANES), jnp.float32),
            jax.ShapeDtypeStruct((HEAD + pairs * rows, LANES), jnp.int16),
        ],
        [pl.BlockSpec(memory_space=VMEM)] * 2,
        (kept, got),
        [pltpu.VMEM((strips * rows, LANES), jnp.float32)],
        moved=8 * kept.size,
    )


def square_kernel(kept_ref, got_ref, *rest):
    earlier, (square_ref, sums_ref) = rest[:-2], rest[-2:]
    rows = kept_ref.shape[1]
    (got,) = load_coded(got_ref, rows)
    value = kept_ref[0] + got
    square = value * value
    square_ref[...] = square
    sums = jnp.broadcast_to(jnp.sum(square, axis=0, keepdims=True), (8, LANES))
    sums_ref[...] = jnp.concatenate([ref[...] for ref in earlier] + [sums], axis=1)


def square(kept, got, earlier, chunk):
    rows = kept.shape[1]
    return whole_call(
        square_kernel,
        f"square_{chunk}",
        [
            jax.ShapeDtypeStruct((rows, LANES), jnp.float32),
            jax.ShapeDtypeStruct((8, LANES * (len(earlier) + 1)), jnp.float32),
        ],
        [pl.BlockSpec(memory_space=VMEM)] * (2 + len(earlier)),
        (kept, got, *earlier),
        moved=8 * kept.size,
    )


def rescale_kernel(count, height, *refs):
    squares, sums, out_ref = refs[:count], refs[count:-1], refs[-1]
    total = sums[0][0:1, :]
    for ref in sums[1:]:
        total = total + ref[0:1, :]
    divisor = total / height + 1e-6
    for c, ref in enumerate(squares):
        columns = slice(c * LANES, (c + 1) * LANES)
        out_ref[0, :, columns] = ref[...] / divisor[:, columns]


def rescale(squares, sums, height):
    rows = squares[0].shape[0]
    width = LANES * len(squares)
    return whole_call(
        functools.partial(rescale_kernel, len(squares), float(height)),
        "rescale",
        jax.ShapeDtypeStruct((1, rows, width), jnp.float32),
        [pl.BlockSpec(memory_space=VMEM)] * (len(squares) + len(sums)),
        (*squares, *sums),
        moved=8 * rows * width,
    )


def shards(flow_t, graph, a_pattern, b_pattern, c_pattern):
    layers = lax.axis_size("layer")
    inner, width = flow_t.shape[1:]
    panel = width // 3
    depth = min(512, inner)
    a_lines = a_pattern.transpose(2, 0, 1)
    b_lines = b_pattern.transpose(2, 0, 1)
    c_lines = c_pattern.transpose(0, 2, 1)
    per_half = BS // LANES
    chunks = panel // LANES

    below, above = [], []
    for half in range(panel // BS):
        parts = side_products(flow_t, graph, a_lines, b_lines, half, depth)
        for c in range(per_half):
            below.append(from_behind(parts[2 * c], "blk", 1))
            above.append(from_behind(parts[2 * c + 1], "blk", -1))
    own = own_product(flow_t, graph, a_lines, b_lines, depth)

    squares, sums = [], []
    for chunk in range(chunks):
        kept, send = join(own, below[chunk], above[chunk], c_lines, chunk, layers)
        position = 1
        while kept.shape[0] > 1:
            got = from_partner(send, "layer", position)
            position *= 2
            kept, send = halve(kept, got, position, chunk)
        got = from_partner(send, "layer", position)
        last = chunk == chunks - 1
        squared, summed = square(kept, got, sums if last else [], chunk)
        squares.append(squared)
        sums.append(summed)
    own_sums = sums[-1]
    all_sums = [own_sums] + [from_behind(own_sums, "layer", i) for i in range(1, layers)]
    return rescale(squares, all_sums, width)


def solution(mesh):
    placed = (
        P("blk", "layer", None),
        P("blk", "layer", None),
        P("blk", None, None),
        P("blk", None, None),
        P("blk", None, None),
    )
    return jax.shard_map(
        shards, mesh=mesh, in_specs=placed, out_specs=P("blk", "layer", None), check_vma=False
    )
```

```python
import functools

import jax
import jax.numpy as jnp
from jax import lax
from jax.experimental import pallas as pl
from jax.experimental.pallas import tpu as pltpu
from jax.sharding import PartitionSpec as P

BS = 256
LANES = 128
HEAD = 16
STEPS = 256.0
TOP = 65534.0
LN2 = 0.6931471805599453
VMEM_LIMIT = 57500000
SMALL_LIMIT = 8 * 1024 * 1024
IN_SMEM = pl.BlockSpec(memory_space=pltpu.SMEM)
IN_VMEM = pl.BlockSpec(memory_space=pltpu.VMEM)
IN_HBM = pl.BlockSpec(memory_space=pltpu.HBM)


def swap(block, axis, partner):
    return lax.ppermute(block, axis, [(partner(i), i) for i in range(lax.axis_size(axis))])


def after(value, *others):
    return lax.optimization_barrier((value, *others))[0]


def call(kernel, name, operands, in_specs, out_shape, scratch_shapes=(), flops=0, moved=0, limit=SMALL_LIMIT):
    return pl.pallas_call(
        kernel,
        out_shape=out_shape,
        in_specs=in_specs,
        out_specs=jax.tree.map(lambda _: IN_VMEM, out_shape),
        scratch_shapes=list(scratch_shapes),
        compiler_params=pltpu.CompilerParams(vmem_limit_bytes=limit),
        cost_estimate=pl.CostEstimate(flops=flops, bytes_accessed=moved, transcendentals=0),
        name=name,
    )(*operands)


def powers(values):
    largest = jnp.maximum(jnp.max(values, axis=0, keepdims=True), 1e-3)
    return jnp.floor(jnp.log(largest) * (STEPS / LN2)) + 2.0


def code(values, power):
    scaled = values * (TOP * jnp.exp(power * (-LN2 / STEPS)))
    return ((scaled + 0.5).astype(jnp.int32) - 32767).astype(jnp.int16)


def scales(head):
    return jnp.exp(head.astype(jnp.int32).astype(jnp.float32) * (LN2 / STEPS)) * (1.0 / TOP)


def decode(codes, scale):
    return (codes.astype(jnp.int32) + 32767).astype(jnp.float32) * scale


def masked(values, pattern, column, first):
    parts = []
    for u in range(values.shape[0] // BS):
        factor = jnp.full((1, values.shape[1]), pattern[column, 0, first + u].astype(jnp.float32))
        parts.append(values[u * BS : (u + 1) * BS] * factor.astype(values.dtype))
    return jnp.concatenate(parts, axis=0) if len(parts) > 1 else parts[0]


def contract(left_side, right_side):
    return lax.dot_general(
        left_side, right_side, (((0,), (0,)), ((), ())), preferred_element_type=jnp.float32
    )


def column_block(ref, block):
    return ref.at[0, :, pl.ds(pl.multiple_of(block * BS, BS), BS)]


def product_kernel(half, wanted, a_ref, b_ref, flow_ref, graph_ref, *rest):
    outs, (flow_buf, graph_buf, sems) = rest[:-3], rest[-3:]
    outs = iter(outs)
    count, inner = flow_buf.shape[:2]
    panel = flow_ref.shape[2] // BS // 3
    odd = lax.rem(lax.axis_index("blk"), 2)
    first = lax.axis_index("layer") * (inner // BS)
    ext_side, int_side = odd * (2 * panel), (1 - odd) * (2 * panel)
    columns = {"ext": ext_side + half, "own": panel + half, "int": int_side + half}
    starts = {"ext": odd * panel, "own": 0, "int": (1 - odd) * panel}
    users = [(panel, ("ext", "own", "int")), (ext_side, ("ext", "own")), (int_side, ("own", "int"))]
    parts = [part for part in ("ext", "own", "int") if part in wanted]
    refs = {part: [next(outs) for _ in wanted[part]] for part in parts}
    blocks = []
    for side, names in users:
        used = [part for part in parts if part in names]
        blocks += [(side + i, used) for i in range(panel) if used]

    graph_copies = [
        pltpu.make_async_copy(column_block(graph_ref, columns[part]), graph_buf.at[j], sems.at[count + j])
        for j, part in enumerate(parts)
    ]
    flow_copies = [
        pltpu.make_async_copy(column_block(flow_ref, block), flow_buf.at[i], sems.at[i])
        for i, (block, _) in enumerate(blocks)
    ]
    for copy in graph_copies + flow_copies:
        copy.start()
    sides = []
    for j, part in enumerate(parts):
        graph_copies[j].wait()
        sides.append(masked(graph_buf[j], b_ref, columns[part], first))
    sides = jnp.concatenate(sides, axis=1) if len(sides) > 1 else sides[0]

    heads = {part: [jnp.zeros((HEAD, ref.shape[1]), jnp.float32) for ref in refs[part]] for part in parts}
    for i, (block, used) in enumerate(blocks):
        flow_copies[i].wait()
        low = parts.index(used[0]) * BS
        product = contract(masked(flow_buf[i], a_ref, block, first), sides[:, low : low + len(used) * BS])
        for j, part in enumerate(used):
            place = block - starts[part]
            column = j * BS
            for c, ref in enumerate(refs[part]):
                chunk = product[:, column : column + ref.shape[1]]
                column += ref.shape[1]
                if part == "own":
                    ref[pl.ds(pl.multiple_of(place * BS, BS), BS), :] = chunk
                else:
                    power = powers(chunk)
                    ref[pl.ds(pl.multiple_of(HEAD + place * BS, HEAD), BS), :] = code(chunk, power)
                    line = lax.broadcasted_iota(jnp.int32, heads[part][c].shape, 0)
                    heads[part][c] = jnp.where(line == place, power, heads[part][c])
    for part in parts:
        for ref, head in zip(refs[part], heads[part]):
            if part != "own":
                ref[0:HEAD, :] = head.astype(jnp.int32).astype(jnp.int16)


def products(flow_t, graph, a_lines, b_lines, half, wanted):
    inner, width = flow_t.shape[1:]
    panel = width // 3
    rows = width if "own" in wanted or len(wanted) > 1 else 2 * panel
    count = rows // BS
    outs = []
    for part in ("ext", "own", "int"):
        for w in wanted.get(part, ()):
            if part == "own":
                outs.append(jax.ShapeDtypeStruct((width, w), jnp.float32))
            else:
                outs.append(jax.ShapeDtypeStruct((HEAD + 2 * panel, w), jnp.int16))
    return call(
        functools.partial(product_kernel, half, wanted),
        "_".join(wanted) + f"_products_{half}",
        (a_lines, b_lines, flow_t, graph),
        [IN_SMEM, IN_SMEM, IN_HBM, IN_HBM],
        outs,
        [
            pltpu.VMEM((count, inner, BS), flow_t.dtype),
            pltpu.VMEM((len(wanted), inner, BS), graph.dtype),
            pltpu.SemaphoreType.DMA((count + len(wanted),)),
        ],
        flops=2 * inner * BS * sum(width if part == "own" else 2 * panel for part in wanted),
        moved=2 * inner * (rows + len(wanted) * BS),
        limit=VMEM_LIMIT,
    )


def split_strips(total, rows, position, keep_ref, send_ref):
    bit = lax.rem(lax.axis_index("layer") // position, 2)
    pairs = keep_ref.shape[0]
    for j in range(pairs):
        keep_ref[j] = total[pl.ds((2 * j + bit) * rows, rows), :]
    away = [total[pl.ds((2 * j + 1 - bit) * rows, rows), :] for j in range(pairs)]
    power = functools.reduce(jnp.maximum, [powers(strip) for strip in away])
    for j, strip in enumerate(away):
        send_ref[HEAD + j * rows : HEAD + (j + 1) * rows, :] = code(strip, power)
    send_ref[0:HEAD, :] = jnp.broadcast_to(power, (HEAD, power.shape[1])).astype(jnp.int32).astype(jnp.int16)


def join_kernel(rows, half, lane, c_ref, own_ref, ext_ref, int_ref, keep_ref, send_ref, total):
    odd = lax.rem(lax.axis_index("blk"), 2)
    blocks = own_ref.shape[0] // BS
    panel = blocks // 3
    lanes = slice(lane, lane + ext_ref.shape[1])
    for v in range(blocks):
        kept = c_ref[0, half, v].astype(jnp.float32)
        total[v * BS : (v + 1) * BS, :] = own_ref[v * BS : (v + 1) * BS, lanes] * kept
    for ref, part, start in ((ext_ref, slice(None), odd * panel), (int_ref, lanes, (1 - odd) * panel)):
        scale = scales(ref[0:HEAD, part])
        for i in range(2 * panel):
            kept = c_ref[0, half, start + i].astype(jnp.float32)
            place = pl.ds(pl.multiple_of((start + i) * BS, BS), BS)
            codes = ref[HEAD + i * BS : HEAD + (i + 1) * BS, part]
            total[place, :] += decode(codes, scale[i : i + 1] * kept)
    split_strips(total, rows, 1, keep_ref, send_ref)


def strips_shapes(pairs, rows, width):
    return [
        jax.ShapeDtypeStruct((pairs, rows, width), jnp.float32),
        jax.ShapeDtypeStruct((HEAD + pairs * rows, width), jnp.int16),
    ]


def join(own, ext_part, int_part, c_lines, half, lane, layers):
    height = own.shape[0]
    width = ext_part.shape[1]
    rows = height // layers
    return call(
        functools.partial(join_kernel, rows, half, lane),
        f"join_{half}_{lane}",
        (c_lines, own, ext_part, int_part),
        [IN_SMEM] + [IN_VMEM] * 3,
        strips_shapes(layers // 2, rows, width),
        [pltpu.VMEM((height, width), jnp.float32)],
        moved=8 * height * width,
    )


def halve_kernel(rows, position, kept_ref, got_ref, keep_ref, send_ref, total):
    scale = scales(got_ref[0:HEAD, :])[0:1]
    for j in range(kept_ref.shape[0]):
        codes = got_ref[HEAD + j * rows : HEAD + (j + 1) * rows, :]
        total[j * rows : (j + 1) * rows, :] = kept_ref[j] + decode(codes, scale)
    split_strips(total, rows, position, keep_ref, send_ref)


def halve(kept, got, position, chunk):
    strips, rows, width = kept.shape
    return call(
        functools.partial(halve_kernel, rows, position),
        f"halve_{position}_{chunk}",
        (kept, got),
        [IN_VMEM] * 2,
        strips_shapes(strips // 2, rows, width),
        [pltpu.VMEM((strips * rows, width), jnp.float32)],
        moved=8 * kept.size,
    )


def square_kernel(kept_ref, got_ref, *rest):
    earlier, (square_ref, sums_ref) = rest[:-2], rest[-2:]
    value = kept_ref[0] + decode(got_ref[HEAD:, :], scales(got_ref[0:HEAD, :])[0:1])
    square = value * value
    square_ref[...] = square
    sums = jnp.broadcast_to(jnp.sum(square, axis=0, keepdims=True), (8, square.shape[1]))
    sums_ref[...] = jnp.concatenate([ref[...] for ref in earlier] + [sums], axis=1)


def square(kept, got, earlier, chunk):
    _, rows, width = kept.shape
    return call(
        square_kernel,
        f"square_{chunk}",
        (kept, got, *earlier),
        [IN_VMEM] * (2 + len(earlier)),
        [
            jax.ShapeDtypeStruct((rows, width), jnp.float32),
            jax.ShapeDtypeStruct((8, width + sum(sums.shape[1] for sums in earlier)), jnp.float32),
        ],
        moved=8 * kept.size,
    )


def rescale_kernel(height, *refs):
    squares, (mine_ref, other_ref, out_ref) = refs[:-3], refs[-3:]
    divisor = (mine_ref[0:1, :] + other_ref[0:1, :]) / height + 1e-6
    column = 0
    for ref in squares:
        columns = slice(column, column + ref.shape[1])
        column += ref.shape[1]
        out_ref[0, :, columns] = ref[...] / divisor[:, columns]


def rescale(squares, mine, other, height):
    rows = squares[0].shape[0]
    width = mine.shape[1]
    return call(
        functools.partial(rescale_kernel, float(height)),
        "rescale",
        (*squares, mine, other),
        [IN_VMEM] * (len(squares) + 2),
        jax.ShapeDtypeStruct((1, rows, width), jnp.float32),
        moved=8 * rows * width,
    )


def shards(flow_t, graph, a_pattern, b_pattern, c_pattern):
    layers = lax.axis_size("layer")
    blks = lax.axis_size("blk")
    width = flow_t.shape[2]
    panel = width // 3
    a_lines = a_pattern.transpose(2, 0, 1)
    b_lines = b_pattern.transpose(2, 0, 1)
    c_lines = c_pattern.transpose(0, 2, 1)

    def other_chip(i):
        return (i + 1 if i % 2 else i - 1) % blks

    def same_chip(i):
        return i ^ 1

    halved = []

    def scatter(kept, send):
        position = 1
        while kept.shape[0] > 1:
            got = swap(send, "layer", lambda i: i ^ position)
            position *= 2
            kept, send = halve(kept, got, position, len(halved))
        halved.append((kept, send))

    def join_all(own, ext_parts, int_part, half):
        lane = 0
        sent = []
        for part in ext_parts:
            kept, send = join(own, part, int_part, c_lines, half, lane, layers)
            scatter(kept, send)
            sent.append(send)
            lane += part.shape[1]
        return sent

    halves = panel // BS
    fine = (LANES,) * (BS // LANES)
    (ext_part,) = products(flow_t, graph, a_lines, b_lines, 0, {"ext": (BS,)})
    got_ext = swap(ext_part, "blk", other_chip)
    own, int_part = products(flow_t, graph, after(a_lines, ext_part), b_lines, 0, {"own": (BS,), "int": (BS,)})
    got_int = swap(int_part, "blk", same_chip)
    a_next = after(a_lines, int_part)
    for half in range(1, halves):
        widths = fine if half == halves - 1 else (BS,)
        *ext_parts, int_part = products(flow_t, graph, a_next, b_lines, half, {"ext": widths, "int": (BS,)})
        next_ext = [swap(part, "blk", other_chip) for part in ext_parts]
        next_int = swap(int_part, "blk", same_chip)
        got_ext = got_ext if half > 1 else [got_ext]
        sent = join_all(own, got_ext, got_int, half - 1)
        (own,) = products(flow_t, graph, after(a_lines, sent[-1]), b_lines, half, {"own": (BS,)})
        a_next = after(a_lines, own)
        got_ext, got_int = next_ext, next_int
    join_all(own, got_ext, got_int, halves - 1)

    squares, sums = [], []
    for chunk, (kept, send) in enumerate(halved):
        got = swap(send, "layer", lambda i: i ^ (layers // 2))
        squared, summed = square(kept, got, sums if chunk == len(halved) - 1 else [], chunk)
        squares.append(squared)
        sums.append(summed)

    total = sums[-1]
    position = 1
    while 2 * position < layers:
        total = total + swap(total, "layer", lambda i: i ^ position)
        position *= 2
    return rescale(squares, total, swap(total, "layer", lambda i: i ^ position), width)


def solution(mesh):
    placed = (
        P("blk", "layer", None),
        P("blk", "layer", None),
        P("blk", None, None),
        P("blk", None, None),
        P("blk", None, None),
    )
    return jax.shard_map(
        shards, mesh=mesh, in_specs=placed, out_specs=P("blk", "layer", None), check_vma=False
    )
```

```python
import functools

import jax
import jax.numpy as jnp
from jax import lax
from jax.experimental import pallas as pl
from jax.experimental.pallas import tpu as pltpu
from jax.sharding import PartitionSpec as P

BS = 256
LANES = 128
HEAD = 16
STEPS = 256.0
TOP = 65534.0
LN2 = 0.6931471805599453
FIRST_LIMIT = 48000000
PRODUCT_LIMIT = 48000000
SMALL_LIMIT = 8 * 1024 * 1024
IN_SMEM = pl.BlockSpec(memory_space=pltpu.SMEM)
IN_VMEM = pl.BlockSpec(memory_space=pltpu.VMEM)
IN_HBM = pl.BlockSpec(memory_space=pltpu.HBM)


def swap(block, axis, partner):
    return lax.ppermute(block, axis, [(partner(i), i) for i in range(lax.axis_size(axis))])


def after(value, *others):
    return lax.optimization_barrier((value, *others))[0]


def call(kernel, name, operands, in_specs, out_shape, scratch_shapes=(), flops=0, moved=0, limit=SMALL_LIMIT):
    return pl.pallas_call(
        kernel,
        out_shape=out_shape,
        in_specs=in_specs,
        out_specs=jax.tree.map(lambda _: IN_VMEM, out_shape),
        scratch_shapes=list(scratch_shapes),
        compiler_params=pltpu.CompilerParams(vmem_limit_bytes=limit),
        cost_estimate=pl.CostEstimate(flops=flops, bytes_accessed=moved, transcendentals=0),
        name=name,
    )(*operands)


def powers(values):
    largest = jnp.maximum(jnp.max(values, axis=0, keepdims=True), 1e-3)
    return jnp.floor(jnp.log(largest) * (STEPS / LN2)) + 2.0


def code(values, power):
    scaled = values * (TOP * jnp.exp(power * (-LN2 / STEPS)))
    return ((scaled + 0.5).astype(jnp.int32) - 32767).astype(jnp.int16)


def scales(head):
    return jnp.exp(head.astype(jnp.int32).astype(jnp.float32) * (LN2 / STEPS)) * (1.0 / TOP)


def decode(codes, scale):
    return (codes.astype(jnp.int32) + 32767).astype(jnp.float32) * scale


def masked(values, pattern, column, first):
    depth, width = values.shape
    place = lax.broadcasted_iota(jnp.int32, (1, width), 1) // BS
    parts = []
    for u in range(depth // BS):
        factor = jnp.zeros((1, width), jnp.float32)
        for v in range(width // BS):
            factor = jnp.where(place == v, pattern[column + v, 0, first + u].astype(jnp.float32), factor)
        parts.append(values[u * BS : (u + 1) * BS] * factor.astype(values.dtype))
    return jnp.concatenate(parts, axis=0) if len(parts) > 1 else parts[0]


def dot(left_side, right_side):
    return lax.dot_general(
        left_side, right_side, (((1,), (0,)), ((), ())), preferred_element_type=jnp.float32
    )


def blocks(ref, start, count):
    return ref.at[0, :, pl.ds(pl.multiple_of(start * BS, BS), count * BS)]


def product_kernel(half, wanted, depth, known, a_ref, b_ref, flow_ref, graph_ref, *rest):
    refs = list(rest)
    held = {name: refs.pop(0) for name in known}
    inner = flow_ref.shape[1]
    panel = flow_ref.shape[2] // BS // 3
    odd = lax.rem(lax.axis_index("blk"), 2)
    first = lax.axis_index("layer") * (inner // BS)
    ext_side, int_side = odd * (2 * panel), (1 - odd) * (2 * panel)
    columns = {"ext": ext_side + half, "own": panel + half, "int": int_side + half}
    starts = {"ext": odd * panel, "own": 0, "int": (1 - odd) * panel}
    parts = [part for part in ("ext", "own", "int") if part in wanted]
    outs = {part: [refs.pop(0) for _ in wanted[part]] for part in parts}
    makes = None
    if len(known) < 2:
        makes = ("ext", "int")[len(known)]
        held[makes] = refs.pop(0)
        flow_buf = refs.pop(0)
    graph_buf, sems = refs
    turned_start = {"ext": odd * panel, "int": int_side}

    graph_copies = [
        pltpu.make_async_copy(blocks(graph_ref, columns[part], 1), graph_buf.at[j], sems.at[j])
        for j, part in enumerate(parts)
    ]
    flow_copies = []
    if makes:
        source = blocks(flow_ref, turned_start[makes], held[makes].shape[0] // BS)
        for t in range(inner // depth):
            rows = slice(t * depth, (t + 1) * depth)
            flow_copies.append(
                pltpu.make_async_copy(source.at[rows], flow_buf.at[rows], sems.at[len(parts) + t])
            )
    for copy in graph_copies + flow_copies:
        copy.start()

    sides = []
    for j, part in enumerate(parts):
        graph_copies[j].wait()
        sides.append(masked(graph_buf[j], b_ref, columns[part], first))
    sides = jnp.concatenate(sides, axis=1) if len(sides) > 1 else sides[0]

    def turn():
        for t, copy in enumerate(flow_copies):
            rows = slice(t * depth, (t + 1) * depth)
            copy.wait()
            chunk = masked(flow_buf[rows, :], a_ref, turned_start[makes], first + t * (depth // BS))
            held[makes][:, rows] = chunk.T

    heads = {part: [jnp.zeros((HEAD, ref.shape[1]), jnp.float32) for ref in outs[part]] for part in parts}

    def multiply(side, names):
        used = [part for part in parts if part in names]
        if not used:
            return
        low = parts.index(used[0]) * BS
        for i in range(panel):
            block = side + i
            source = "int" if side is int_side else "ext"
            at = pl.ds(pl.multiple_of((block - turned_start[source]) * BS, BS), BS)
            product = dot(held[source][at, :], sides[:, low : low + len(used) * BS])
            for j, part in enumerate(used):
                place = block - starts[part]
                column = j * BS
                for c, ref in enumerate(outs[part]):
                    chunk = product[:, column : column + ref.shape[1]]
                    column += ref.shape[1]
                    if part == "own":
                        ref[pl.ds(pl.multiple_of(place * BS, BS), BS), :] = chunk
                    else:
                        power = powers(chunk)
                        ref[pl.ds(pl.multiple_of(HEAD + place * BS, HEAD), BS), :] = code(chunk, power)
                        line = lax.broadcasted_iota(jnp.int32, heads[part][c].shape, 0)
                        heads[part][c] = jnp.where(line == place, power, heads[part][c])

    if makes == "ext":
        turn()
    multiply(panel, ("ext", "own", "int"))
    multiply(ext_side, ("ext", "own"))
    if makes == "int":
        turn()
    multiply(int_side, ("own", "int"))
    for part in parts:
        for ref, head in zip(outs[part], heads[part]):
            if part != "own":
                ref[0:HEAD, :] = head.astype(jnp.int32).astype(jnp.int16)


def products(flow_t, graph, a_lines, b_lines, half, wanted, turned, limit):
    inner, width = flow_t.shape[1:]
    panel = width // 3
    depth = min(512, inner)
    known = tuple(turned)
    outs = []
    for part in ("ext", "own", "int"):
        for w in wanted.get(part, ()):
            if part == "own":
                outs.append(jax.ShapeDtypeStruct((width, w), jnp.float32))
            else:
                outs.append(jax.ShapeDtypeStruct((HEAD + 2 * panel, w), jnp.int16))
    scratch = []
    if len(known) < 2:
        rows = (2 * panel, panel)[len(known)]
        outs.append(jax.ShapeDtypeStruct((rows, inner), flow_t.dtype))
        scratch.append(pltpu.VMEM((inner, rows), flow_t.dtype))
    results = list(call(
        functools.partial(product_kernel, half, wanted, depth, known),
        "_".join(wanted) + f"_products_{half}",
        (a_lines, b_lines, flow_t, graph, *turned.values()),
        [IN_SMEM, IN_SMEM, IN_HBM, IN_HBM] + [IN_VMEM] * len(known),
        outs,
        scratch
        + [
            pltpu.VMEM((len(wanted), inner, BS), graph.dtype),
            pltpu.SemaphoreType.DMA((len(wanted) + inner // depth,)),
        ],
        flops=2 * inner * BS * sum(width if part == "own" else 2 * panel for part in wanted),
        moved=2 * inner * (width + len(wanted) * BS),
        limit=limit,
    ))
    if len(known) < 2:
        turned[("ext", "int")[len(known)]] = results.pop()
    return results


def split_strips(total, rows, position, keep_ref, send_ref):
    bit = lax.rem(lax.axis_index("layer") // position, 2)
    pairs = keep_ref.shape[0]
    for j in range(pairs):
        keep_ref[j] = total[pl.ds((2 * j + bit) * rows, rows), :]
    away = [total[pl.ds((2 * j + 1 - bit) * rows, rows), :] for j in range(pairs)]
    power = functools.reduce(jnp.maximum, [powers(strip) for strip in away])
    for j, strip in enumerate(away):
        send_ref[HEAD + j * rows : HEAD + (j + 1) * rows, :] = code(strip, power)
    send_ref[0:HEAD, :] = jnp.broadcast_to(power, (HEAD, power.shape[1])).astype(jnp.int32).astype(jnp.int16)


def join_kernel(rows, half, lane, c_ref, own_ref, ext_ref, int_ref, keep_ref, send_ref, total):
    odd = lax.rem(lax.axis_index("blk"), 2)
    blocks = own_ref.shape[0] // BS
    panel = blocks // 3
    lanes = slice(lane, lane + ext_ref.shape[1])
    for v in range(blocks):
        kept = c_ref[0, half, v].astype(jnp.float32)
        total[v * BS : (v + 1) * BS, :] = own_ref[v * BS : (v + 1) * BS, lanes] * kept
    for ref, part, start in ((ext_ref, slice(None), odd * panel), (int_ref, lanes, (1 - odd) * panel)):
        scale = scales(ref[0:HEAD, part])
        for i in range(2 * panel):
            kept = c_ref[0, half, start + i].astype(jnp.float32)
            place = pl.ds(pl.multiple_of((start + i) * BS, BS), BS)
            codes = ref[HEAD + i * BS : HEAD + (i + 1) * BS, part]
            total[place, :] += decode(codes, scale[i : i + 1] * kept)
    split_strips(total, rows, 1, keep_ref, send_ref)


def strips_shapes(pairs, rows, width):
    return [
        jax.ShapeDtypeStruct((pairs, rows, width), jnp.float32),
        jax.ShapeDtypeStruct((HEAD + pairs * rows, width), jnp.int16),
    ]


def join(own, ext_part, int_part, c_lines, half, lane, layers):
    height = own.shape[0]
    width = ext_part.shape[1]
    rows = height // layers
    return call(
        functools.partial(join_kernel, rows, half, lane),
        f"join_{half}_{lane}",
        (c_lines, own, ext_part, int_part),
        [IN_SMEM] + [IN_VMEM] * 3,
        strips_shapes(layers // 2, rows, width),
        [pltpu.VMEM((height, width), jnp.float32)],
        moved=8 * height * width,
    )


def halve_kernel(rows, position, kept_ref, got_ref, keep_ref, send_ref, total):
    scale = scales(got_ref[0:HEAD, :])[0:1]
    for j in range(kept_ref.shape[0]):
        codes = got_ref[HEAD + j * rows : HEAD + (j + 1) * rows, :]
        total[j * rows : (j + 1) * rows, :] = kept_ref[j] + decode(codes, scale)
    split_strips(total, rows, position, keep_ref, send_ref)


def halve(kept, got, position, chunk):
    strips, rows, width = kept.shape
    return call(
        functools.partial(halve_kernel, rows, position),
        f"halve_{position}_{chunk}",
        (kept, got),
        [IN_VMEM] * 2,
        strips_shapes(strips // 2, rows, width),
        [pltpu.VMEM((strips * rows, width), jnp.float32)],
        moved=8 * kept.size,
    )


def square_kernel(kept_ref, got_ref, *rest):
    earlier, (square_ref, sums_ref) = rest[:-2], rest[-2:]
    value = kept_ref[0] + decode(got_ref[HEAD:, :], scales(got_ref[0:HEAD, :])[0:1])
    square = value * value
    square_ref[...] = square
    sums = jnp.broadcast_to(jnp.sum(square, axis=0, keepdims=True), (8, square.shape[1]))
    sums_ref[...] = jnp.concatenate([ref[...] for ref in earlier] + [sums], axis=1)


def square(kept, got, earlier, chunk):
    _, rows, width = kept.shape
    return call(
        square_kernel,
        f"square_{chunk}",
        (kept, got, *earlier),
        [IN_VMEM] * (2 + len(earlier)),
        [
            jax.ShapeDtypeStruct((rows, width), jnp.float32),
            jax.ShapeDtypeStruct((8, width + sum(sums.shape[1] for sums in earlier)), jnp.float32),
        ],
        moved=8 * kept.size,
    )


def rescale_kernel(height, count, *refs):
    squares, sums, out_ref = refs[:count], refs[count:-1], refs[-1]
    total = functools.reduce(jnp.add, [ref[0:1, :] for ref in sums])
    divisor = total / height + 1e-6
    column = 0
    for ref in squares:
        columns = slice(column, column + ref.shape[1])
        column += ref.shape[1]
        out_ref[0, :, columns] = ref[...] / divisor[:, columns]


def rescale(squares, sums, height):
    rows = squares[0].shape[0]
    width = sums[0].shape[1]
    return call(
        functools.partial(rescale_kernel, float(height), len(squares)),
        "rescale",
        (*squares, *sums),
        [IN_VMEM] * (len(squares) + len(sums)),
        jax.ShapeDtypeStruct((1, rows, width), jnp.float32),
        moved=8 * rows * width,
    )


def shards(flow_t, graph, a_pattern, b_pattern, c_pattern):
    layers = lax.axis_size("layer")
    blks = lax.axis_size("blk")
    width = flow_t.shape[2]
    panel = width // 3
    a_lines = a_pattern.transpose(2, 0, 1)
    b_lines = b_pattern.transpose(2, 0, 1)
    c_lines = c_pattern.transpose(0, 2, 1)

    def other_chip(i):
        return (i + 1 if i % 2 else i - 1) % blks

    def same_chip(i):
        return i ^ 1

    halved = []

    def scatter(kept, send):
        position = 1
        while kept.shape[0] > 1:
            got = swap(send, "layer", lambda i: i ^ position)
            position *= 2
            kept, send = halve(kept, got, position, len(halved))
        halved.append((kept, send))

    def join_all(own, ext_parts, int_part, half):
        lane = 0
        sent = []
        for part in ext_parts:
            kept, send = join(own, part, int_part, c_lines, half, lane, layers)
            scatter(kept, send)
            sent.append(send)
            lane += part.shape[1]
        return sent

    halves = panel // BS
    fine = (LANES,) * (BS // LANES)
    turned = {}
    (ext_part,) = products(flow_t, graph, a_lines, b_lines, 0, {"ext": (BS,)}, turned, FIRST_LIMIT)
    got_ext = swap(ext_part, "blk", other_chip)
    wanted = {"own": (BS,), "int": (BS,)}
    own, int_part = products(flow_t, graph, a_lines, b_lines, 0, wanted, turned, PRODUCT_LIMIT)
    got_int = swap(int_part, "blk", same_chip)
    a_next = after(a_lines, int_part)
    for half in range(1, halves):
        widths = fine if half == halves - 1 else (BS,)
        wanted = {"ext": widths, "int": (BS,)}
        *ext_parts, int_part = products(flow_t, graph, a_next, b_lines, half, wanted, turned, PRODUCT_LIMIT)
        next_ext = [swap(part, "blk", other_chip) for part in ext_parts]
        next_int = swap(int_part, "blk", same_chip)
        got_ext = got_ext if half > 1 else [got_ext]
        sent = join_all(own, got_ext, got_int, half - 1)
        wanted = {"own": (BS,)}
        (own,) = products(flow_t, graph, after(a_lines, sent[-1]), b_lines, half, wanted, turned, PRODUCT_LIMIT)
        a_next = after(a_lines, own)
        got_ext, got_int = next_ext, next_int
    join_all(own, got_ext, got_int, halves - 1)

    squares, sums = [], []
    for chunk, (kept, send) in enumerate(halved):
        got = swap(send, "layer", lambda i: i ^ (layers // 2))
        squared, summed = square(kept, got, sums if chunk == len(halved) - 1 else [], chunk)
        squares.append(squared)
        sums.append(summed)

    mine = sums[-1]
    others = [swap(mine, "layer", lambda i: i ^ other) for other in range(1, layers)]
    return rescale(squares, [mine, *others], width)


def solution(mesh):
    placed = (
        P("blk", "layer", None),
        P("blk", "layer", None),
        P("blk", None, None),
        P("blk", None, None),
        P("blk", None, None),
    )
    return jax.shard_map(
        shards, mesh=mesh, in_specs=placed, out_specs=P("blk", "layer", None), check_vma=False
    )
```

```python
import functools

import jax
import jax.numpy as jnp
from jax import lax
from jax.experimental import pallas as pl
from jax.experimental.pallas import tpu as pltpu
from jax.sharding import PartitionSpec as P

BS = 256
LANES = 128
HEAD = 16
STEPS = 256.0
TOP = 65534.0
LN2 = 0.6931471805599453
PRODUCT_LIMIT = 24000000
SMALL_LIMIT = 8 * 1024 * 1024
IN_SMEM = pl.BlockSpec(memory_space=pltpu.SMEM)
IN_VMEM = pl.BlockSpec(memory_space=pltpu.VMEM)
IN_HBM = pl.BlockSpec(memory_space=pltpu.HBM)


def swap(block, axis, partner):
    return lax.ppermute(block, axis, [(partner(i), i) for i in range(lax.axis_size(axis))])


def after(value, *others):
    return lax.optimization_barrier((value, *others))[0]


def call(kernel, name, operands, in_specs, out_shape, scratch_shapes=(), flops=0, moved=0, limit=SMALL_LIMIT):
    return pl.pallas_call(
        kernel,
        out_shape=out_shape,
        in_specs=in_specs,
        out_specs=jax.tree.map(lambda _: IN_VMEM, out_shape),
        scratch_shapes=list(scratch_shapes),
        compiler_params=pltpu.CompilerParams(vmem_limit_bytes=limit),
        cost_estimate=pl.CostEstimate(flops=1, bytes_accessed=1, transcendentals=0),
        name=name,
    )(*operands)


def powers(values):
    largest = jnp.maximum(jnp.max(values, axis=0, keepdims=True), 1e-3)
    return jnp.floor(jnp.log(largest) * (STEPS / LN2)) + 2.0


def code(values, power):
    scaled = values * (TOP * jnp.exp(power * (-LN2 / STEPS)))
    return ((scaled + 0.5).astype(jnp.int32) - 32767).astype(jnp.int16)


def scales(head):
    return jnp.exp(head.astype(jnp.int32).astype(jnp.float32) * (LN2 / STEPS)) * (1.0 / TOP)


def decode(codes, scale):
    return (codes.astype(jnp.int32) + 32767).astype(jnp.float32) * scale


def masked(values, pattern, column, first):
    depth, width = values.shape
    place = lax.broadcasted_iota(jnp.int32, (1, width), 1) // BS
    parts = []
    for u in range(depth // BS):
        factor = jnp.zeros((1, width), jnp.float32)
        for v in range(width // BS):
            factor = jnp.where(place == v, pattern[column + v, 0, first + u].astype(jnp.float32), factor)
        parts.append(values[u * BS : (u + 1) * BS] * factor.astype(values.dtype))
    return jnp.concatenate(parts, axis=0) if len(parts) > 1 else parts[0]


def dot(left_side, right_side):
    return lax.dot_general(
        left_side, right_side, (((1,), (0,)), ((), ())), preferred_element_type=jnp.float32
    )


def columns_of(ref, start, count):
    return ref.at[0, :, pl.ds(pl.multiple_of(start * BS, BS), count * BS)]


def rows_at(block, first=0):
    return pl.ds(pl.multiple_of(first + block * BS, HEAD), BS)


class Sides:
    def __init__(self, inner, panel):
        odd = lax.rem(lax.axis_index("blk"), 2)
        self.panel = panel
        self.first = lax.axis_index("layer") * (inner // BS)
        self.ext_side, self.int_side = odd * (2 * panel), (1 - odd) * (2 * panel)
        self.columns = {"ext": self.ext_side, "own": panel, "int": self.int_side}
        self.starts = {"ext": odd * panel, "own": 0, "int": (1 - odd) * panel}


class Coded:
    def __init__(self, refs):
        self.refs = refs
        self.heads = [jnp.zeros((HEAD, ref.shape[1]), jnp.float32) for ref in refs]

    def write(self, product, place):
        column = 0
        for c, ref in enumerate(self.refs):
            chunk = product[:, column : column + ref.shape[1]]
            column += ref.shape[1]
            power = powers(chunk)
            ref[rows_at(place, HEAD), :] = code(chunk, power)
            line = lax.broadcasted_iota(jnp.int32, self.heads[c].shape, 0)
            self.heads[c] = jnp.where(line == place, power, self.heads[c])

    def finish(self):
        for ref, head in zip(self.refs, self.heads):
            ref[0:HEAD, :] = head.astype(jnp.int32).astype(jnp.int16)


def turn(chunk, a_ref, start, first, turned_ref, rows):
    turned_ref[:, rows] = masked(chunk, a_ref, start, first).T


def first_kernel(depth, a_hbm, b_hbm, flow_hbm, graph_hbm, *rest):
    out_refs, (turned_ref, graph_ref, flow_ref, flow_buf, a_ref, b_ref, sems) = rest[:-7], rest[-7:]
    inner, panel = flow_ref.shape[0], flow_ref.shape[1] // BS
    at = Sides(inner, panel)
    steps = inner // depth
    small = [pltpu.make_async_copy(a_hbm, a_ref, sems.at[0]), pltpu.make_async_copy(b_hbm, b_ref, sems.at[1])]
    side = pl.ds(pl.multiple_of(at.ext_side * BS, BS), panel * BS)
    rest_start = (panel * BS) - at.ext_side // 2 * BS
    others = pl.ds(pl.multiple_of(rest_start, BS), 2 * panel * BS)
    early = pltpu.make_async_copy(graph_hbm.at[0, :, side], graph_ref.at[:, side], sems.at[2])
    late = [
        pltpu.make_async_copy(graph_hbm.at[0, :, others], graph_ref.at[:, others], sems.at[3]),
        pltpu.make_async_copy(columns_of(flow_hbm, at.int_side, panel), flow_ref, sems.at[4]),
    ]
    source = columns_of(flow_hbm, at.starts["ext"], 2 * panel)
    flows = []
    for t in range(steps):
        rows = slice(t * depth, (t + 1) * depth)
        flows.append(pltpu.make_async_copy(source.at[rows], flow_buf.at[rows], sems.at[5 + t]))
    for copy in small + flows[:1] + [early] + flows[1:] + late:
        copy.start()
    for copy in small:
        copy.wait()
    for t in range(steps):
        rows = slice(t * depth, (t + 1) * depth)
        flows[t].wait()
        turn(flow_buf[rows, :], a_ref, at.starts["ext"], at.first + t * (depth // BS), turned_ref, rows)
    early.wait()
    right = masked(graph_ref[:, rows_at(at.ext_side)], b_ref, at.ext_side, at.first)
    coded = Coded(out_refs)
    for i in range(2 * panel):
        coded.write(dot(turned_ref[i * BS : (i + 1) * BS, :], right), i)
    coded.finish()
    for copy in late:
        copy.wait()


def first_products(flow_t, graph, a_lines, b_lines, widths):
    inner, width = flow_t.shape[1:]
    panel = width // 3
    depth = min(512, inner)
    operands = [pltpu.with_memory_space_constraint(x, pltpu.HBM) for x in (a_lines, b_lines, flow_t, graph)]
    return call(
        functools.partial(first_kernel, depth),
        "first_products",
        operands,
        [IN_HBM] * 4,
        [jax.ShapeDtypeStruct((HEAD + 2 * panel, w), jnp.int16) for w in widths]
        + [
            pltpu.VMEM((2 * panel, inner), flow_t.dtype),
            pltpu.VMEM((inner, width), graph.dtype),
            pltpu.VMEM((inner, panel), flow_t.dtype),
        ],
        [
            pltpu.VMEM((inner, 2 * panel), flow_t.dtype),
            pltpu.SMEM(a_lines.shape, a_lines.dtype),
            pltpu.SMEM(b_lines.shape, b_lines.dtype),
            pltpu.SemaphoreType.DMA((5 + inner // depth,)),
        ],
        flops=2 * inner * BS * 2 * panel,
        moved=4 * inner * width,
        limit=PRODUCT_LIMIT,
    )


def product_kernel(half, wanted, turns, a_ref, b_ref, graph_ref, ext_rows_ref, int_rows_ref, *rest):
    refs = list(rest)
    inner, panel = graph_ref.shape[0], graph_ref.shape[1] // BS // 3
    at = Sides(inner, panel)
    parts = [part for part in ("ext", "own", "int") if part in wanted]
    outs = {part: [refs.pop(0) for _ in wanted[part]] for part in parts}
    turned_ref = refs.pop(0) if turns else int_rows_ref
    coded = {part: Coded(outs[part]) for part in parts if part != "own"}
    right = []
    for part in parts:
        column = at.columns[part] + half
        right.append(masked(graph_ref[:, rows_at(column)], b_ref, column, at.first))
    right = jnp.concatenate(right, axis=1) if len(right) > 1 else right[0]

    def multiply(side, start, source, names):
        used = [part for part in parts if part in names]
        if not used:
            return
        low = parts.index(used[0]) * BS
        for i in range(panel):
            block = side + i
            product = dot(source[rows_at(block - start), :], right[:, low : low + len(used) * BS])
            for j, part in enumerate(used):
                piece = product[:, j * BS : (j + 1) * BS]
                if part == "own":
                    outs[part][0][rows_at(block), :] = piece
                else:
                    coded[part].write(piece, block - at.starts[part])

    if turns:
        turn(int_rows_ref[...], a_ref, at.int_side, at.first, turned_ref, slice(None))
    multiply(panel, at.starts["ext"], ext_rows_ref, ("ext", "own", "int"))
    multiply(at.ext_side, at.starts["ext"], ext_rows_ref, ("ext", "own"))
    multiply(at.int_side, at.int_side, turned_ref, ("own", "int"))
    for part in coded:
        coded[part].finish()


def products(a_lines, b_lines, graph, ext_rows, int_rows, half, wanted, turns=False):
    inner, width = graph.shape
    panel = width // 3
    outs = []
    for part in ("ext", "own", "int"):
        for w in wanted.get(part, ()):
            if part == "own":
                outs.append(jax.ShapeDtypeStruct((width, w), jnp.float32))
            else:
                outs.append(jax.ShapeDtypeStruct((HEAD + 2 * panel, w), jnp.int16))
    if turns:
        outs.append(pltpu.VMEM((panel, inner), graph.dtype))
    return call(
        functools.partial(product_kernel, half, wanted, turns),
        "_".join(wanted) + f"_products_{half}",
        (a_lines, b_lines, graph, ext_rows, int_rows),
        [IN_SMEM, IN_SMEM] + [IN_VMEM] * 3,
        outs,
        flops=2 * inner * BS * sum(width if part == "own" else 2 * panel for part in wanted),
        moved=2 * inner * BS,
        limit=PRODUCT_LIMIT,
    )


def split_strips(total, rows, position, keep_ref, send_ref):
    bit = lax.rem(lax.axis_index("layer") // position, 2)
    pairs = keep_ref.shape[0]
    for j in range(pairs):
        keep_ref[j] = total[pl.ds((2 * j + bit) * rows, rows), :]
    away = [total[pl.ds((2 * j + 1 - bit) * rows, rows), :] for j in range(pairs)]
    power = functools.reduce(jnp.maximum, [powers(strip) for strip in away])
    for j, strip in enumerate(away):
        send_ref[HEAD + j * rows : HEAD + (j + 1) * rows, :] = code(strip, power)
    send_ref[0:HEAD, :] = jnp.broadcast_to(power, (HEAD, power.shape[1])).astype(jnp.int32).astype(jnp.int16)


def join_kernel(rows, half, lane, c_ref, own_ref, ext_ref, int_ref, keep_ref, send_ref, total):
    odd = lax.rem(lax.axis_index("blk"), 2)
    blocks = own_ref.shape[0] // BS
    panel = blocks // 3
    lanes = slice(lane, lane + ext_ref.shape[1])

    def add(below_ref, above_ref):
        below_scale = scales(below_ref[0:HEAD, :])
        above_scale = scales(above_ref[0:HEAD, :])
        for v in range(blocks):
            kept = c_ref[0, half, v].astype(jnp.float32)
            block = own_ref[v * BS : (v + 1) * BS, lanes] * kept
            if v < 2 * panel:
                codes = below_ref[HEAD + v * BS : HEAD + (v + 1) * BS, :]
                block += decode(codes, below_scale[v : v + 1] * kept)
            if v >= panel:
                i = v - panel
                codes = above_ref[HEAD + i * BS : HEAD + (i + 1) * BS, :]
                block += decode(codes, above_scale[i : i + 1] * kept)
            total[v * BS : (v + 1) * BS, :] = block

    @pl.when(odd == 1)
    def _():
        add(int_ref, ext_ref)

    @pl.when(odd == 0)
    def _():
        add(ext_ref, int_ref)

    split_strips(total, rows, 1, keep_ref, send_ref)


def strips_shapes(pairs, rows, width):
    return [
        jax.ShapeDtypeStruct((pairs, rows, width), jnp.float32),
        jax.ShapeDtypeStruct((HEAD + pairs * rows, width), jnp.int16),
    ]


def join(own, ext_part, int_part, c_lines, half, lane, layers):
    height = own.shape[0]
    width = ext_part.shape[1]
    rows = height // layers
    return call(
        functools.partial(join_kernel, rows, half, lane),
        f"join_{half}_{lane}",
        (c_lines, own, ext_part, int_part),
        [IN_SMEM] + [IN_VMEM] * 3,
        strips_shapes(layers // 2, rows, width),
        [pltpu.VMEM((height, width), jnp.float32)],
        moved=8 * height * width,
    )


def halve_kernel(rows, position, kept_ref, got_ref, keep_ref, send_ref, total):
    scale = scales(got_ref[0:HEAD, :])[0:1]
    for j in range(kept_ref.shape[0]):
        codes = got_ref[HEAD + j * rows : HEAD + (j + 1) * rows, :]
        total[j * rows : (j + 1) * rows, :] = kept_ref[j] + decode(codes, scale)
    split_strips(total, rows, position, keep_ref, send_ref)


def halve(kept, got, position, chunk):
    strips, rows, width = kept.shape
    return call(
        functools.partial(halve_kernel, rows, position),
        f"halve_{position}_{chunk}",
        (kept, got),
        [IN_VMEM] * 2,
        strips_shapes(strips // 2, rows, width),
        [pltpu.VMEM((strips * rows, width), jnp.float32)],
        moved=8 * kept.size,
    )


def square_kernel(kept_ref, got_ref, *rest):
    earlier, (square_ref, sums_ref) = rest[:-2], rest[-2:]
    value = kept_ref[0] + decode(got_ref[HEAD:, :], scales(got_ref[0:HEAD, :])[0:1])
    square = value * value
    square_ref[...] = square
    sums = jnp.broadcast_to(jnp.sum(square, axis=0, keepdims=True), (8, square.shape[1]))
    sums_ref[...] = jnp.concatenate([ref[...] for ref in earlier] + [sums], axis=1)


def square(kept, got, earlier, chunk):
    _, rows, width = kept.shape
    return call(
        square_kernel,
        f"square_{chunk}",
        (kept, got, *earlier),
        [IN_VMEM] * (2 + len(earlier)),
        [
            jax.ShapeDtypeStruct((rows, width), jnp.float32),
            jax.ShapeDtypeStruct((8, width + sum(sums.shape[1] for sums in earlier)), jnp.float32),
        ],
        moved=8 * kept.size,
    )


def rescale_kernel(height, count, *refs):
    squares, sums, out_ref = refs[:count], refs[count:-1], refs[-1]
    total = functools.reduce(jnp.add, [ref[0:1, :] for ref in sums])
    divisor = total / height + 1e-6
    column = 0
    for ref in squares:
        columns = slice(column, column + ref.shape[1])
        column += ref.shape[1]
        out_ref[0, :, columns] = ref[...] / divisor[:, columns]


def rescale(squares, sums, height):
    rows = squares[0].shape[0]
    width = sums[0].shape[1]
    return call(
        functools.partial(rescale_kernel, float(height), len(squares)),
        "rescale",
        (*squares, *sums),
        [IN_VMEM] * (len(squares) + len(sums)),
        jax.ShapeDtypeStruct((1, rows, width), jnp.float32),
        moved=8 * rows * width,
    )


def shards(flow_t, graph, a_pattern, b_pattern, c_pattern):
    layers = lax.axis_size("layer")
    blks = lax.axis_size("blk")
    width = flow_t.shape[2]
    panel = width // 3
    a_lines = a_pattern.transpose(2, 0, 1)
    b_lines = b_pattern.transpose(2, 0, 1)
    c_lines = c_pattern.transpose(0, 2, 1)

    def other_chip(i):
        return (i + 1 if i % 2 else i - 1) % blks

    def same_chip(i):
        return i ^ 1

    halves = panel // BS
    chunks = panel // LANES
    fine = (LANES,) * (BS // LANES)
    per_half = len(fine)
    *ext_parts, ext_rows, graph, flow_rest = first_products(flow_t, graph, a_lines, b_lines, fine)
    ext = [swap(part, "blk", other_chip) for part in ext_parts]
    wanted = {"own": (BS,), "int": fine}
    own, *int_parts, int_rows = products(a_lines, b_lines, graph, ext_rows, flow_rest, 0, wanted, turns=True)
    owns = [own]
    int_ = [swap(part, "blk", same_chip) for part in int_parts]
    latest = [own]

    def ordered(value):
        return after(value, latest[-1])

    def more_products(half):
        parts = products(ordered(a_lines), b_lines, graph, ext_rows, int_rows, half, {"ext": fine, "int": fine})
        ext.extend(swap(part, "blk", other_chip) for part in parts[:per_half])
        int_.extend(swap(part, "blk", same_chip) for part in parts[per_half:])
        latest.append(parts[0])
        owns.extend(products(ordered(a_lines), b_lines, graph, ext_rows, int_rows, half, {"own": (BS,)}))
        latest.append(owns[-1])

    strips, squares, sums = [], [], []

    def add_up(chunk):
        half, lane = divmod(chunk, per_half)
        kept, send = join(owns[half], ext[chunk], int_[chunk], ordered(c_lines), half, lane * LANES, layers)
        latest.append(send)
        strips.append((kept, swap(send, "layer", lambda i: i ^ 1)))

    def scatter(chunk):
        kept, got = strips[chunk]
        position = 1
        while kept.shape[0] > 1:
            position *= 2
            kept, send = halve(ordered(kept), got, position, chunk)
            latest.append(send)
            got = swap(send, "layer", lambda i: i ^ position)
        strips[chunk] = kept, got

    def finish(chunk):
        kept, got = strips[chunk]
        squared, summed = square(ordered(kept), got, sums if chunk == chunks - 1 else [], chunk)
        latest.append(summed)
        squares.append(squared)
        sums.append(summed)

    for chunk in range(chunks + 2):
        if chunk < chunks:
            add_up(chunk)
        if 1 <= chunk <= chunks:
            scatter(chunk - 1)
        if chunk >= 2:
            finish(chunk - 2)
        if chunk % per_half == 0 and chunk // per_half + 1 < halves:
            more_products(chunk // per_half + 1)

    mine = sums[-1]
    others = [swap(mine, "layer", lambda i: i ^ other) for other in range(1, layers)]
    return rescale(squares, [mine, *others], width)


def solution(mesh):
    placed = (
        P("blk", "layer", None),
        P("blk", "layer", None),
        P("blk", None, None),
        P("blk", None, None),
        P("blk", None, None),
    )
    return jax.shard_map(
        shards, mesh=mesh, in_specs=placed, out_specs=P("blk", "layer", None), check_vma=False
    )
```

```python
import functools

import jax
import jax.numpy as jnp
from jax import lax
from jax.experimental import pallas as pl
from jax.experimental.pallas import tpu as pltpu
from jax.sharding import PartitionSpec as P

BS = 256
LANES = 128
HEAD = 16
STEPS = 256.0
TOP = 65534.0
LN2 = 0.6931471805599453
PRODUCT_LIMIT = 24000000
SMALL_LIMIT = 8 * 1024 * 1024
IN_SMEM = pl.BlockSpec(memory_space=pltpu.SMEM)
IN_VMEM = pl.BlockSpec(memory_space=pltpu.VMEM)
IN_HBM = pl.BlockSpec(memory_space=pltpu.HBM)


def swap(block, axis, partner):
    return lax.ppermute(block, axis, [(partner(i), i) for i in range(lax.axis_size(axis))])


def after(value, *others):
    return lax.optimization_barrier((value, *others))[0]


def call(kernel, name, operands, in_specs, out_shape, scratch_shapes=(), flops=0, moved=0, limit=SMALL_LIMIT):
    return pl.pallas_call(
        kernel,
        out_shape=out_shape,
        in_specs=in_specs,
        out_specs=jax.tree.map(lambda _: IN_VMEM, out_shape),
        scratch_shapes=list(scratch_shapes),
        compiler_params=pltpu.CompilerParams(vmem_limit_bytes=limit),
        cost_estimate=pl.CostEstimate(flops=1, bytes_accessed=1, transcendentals=0),
        name=name,
    )(*operands)


def powers(values):
    largest = jnp.maximum(jnp.max(values, axis=0, keepdims=True), 1e-3)
    return jnp.floor(jnp.log(largest) * (STEPS / LN2)) + 2.0


def code(values, power):
    scaled = values * (TOP * jnp.exp(power * (-LN2 / STEPS)))
    return ((scaled + 0.5).astype(jnp.int32) - 32767).astype(jnp.int16)


def scales(head):
    return jnp.exp(head.astype(jnp.int32).astype(jnp.float32) * (LN2 / STEPS)) * (1.0 / TOP)


def decode(codes, scale):
    return (codes.astype(jnp.int32) + 32767).astype(jnp.float32) * scale


def masked(values, pattern, column, first):
    depth, width = values.shape
    place = lax.broadcasted_iota(jnp.int32, (1, width), 1) // BS
    parts = []
    for u in range(depth // BS):
        factor = jnp.zeros((1, width), jnp.float32)
        for v in range(width // BS):
            factor = jnp.where(place == v, pattern[column + v, 0, first + u].astype(jnp.float32), factor)
        parts.append(values[u * BS : (u + 1) * BS] * factor.astype(values.dtype))
    return jnp.concatenate(parts, axis=0) if len(parts) > 1 else parts[0]


def dot(left_side, right_side):
    return lax.dot_general(
        left_side, right_side, (((1,), (0,)), ((), ())), preferred_element_type=jnp.float32
    )


def columns_of(ref, start, count):
    return ref.at[0, :, pl.ds(pl.multiple_of(start * BS, BS), count * BS)]


def rows_at(block, first=0):
    return pl.ds(pl.multiple_of(first + block * BS, HEAD), BS)


class Sides:
    def __init__(self, inner, panel):
        odd = lax.rem(lax.axis_index("blk"), 2)
        self.panel = panel
        self.first = lax.axis_index("layer") * (inner // BS)
        self.ext_side, self.int_side = odd * (2 * panel), (1 - odd) * (2 * panel)
        self.columns = {"ext": self.ext_side, "own": panel, "int": self.int_side}
        self.starts = {"ext": odd * panel, "own": 0, "int": (1 - odd) * panel}


class Coded:
    def __init__(self, refs):
        self.refs = refs
        self.heads = [jnp.zeros((HEAD, ref.shape[1]), jnp.float32) for ref in refs]

    def write(self, product, place):
        column = 0
        for c, ref in enumerate(self.refs):
            chunk = product[:, column : column + ref.shape[1]]
            column += ref.shape[1]
            power = powers(chunk)
            ref[rows_at(place, HEAD), :] = code(chunk, power)
            line = lax.broadcasted_iota(jnp.int32, self.heads[c].shape, 0)
            self.heads[c] = jnp.where(line == place, power, self.heads[c])

    def finish(self):
        for ref, head in zip(self.refs, self.heads):
            ref[0:HEAD, :] = head.astype(jnp.int32).astype(jnp.int16)


def turn(chunk, a_ref, start, first, turned_ref, rows):
    turned_ref[:, rows] = masked(chunk, a_ref, start, first).T


def first_kernel(depth, a_hbm, b_hbm, flow_hbm, graph_hbm, *rest):
    out_refs, (turned_ref, graph_ref, flow_ref, flow_buf, a_ref, b_ref, sems) = rest[:-7], rest[-7:]
    inner, panel = flow_ref.shape[0], flow_ref.shape[1] // BS
    at = Sides(inner, panel)
    steps = inner // depth
    small = [pltpu.make_async_copy(a_hbm, a_ref, sems.at[0]), pltpu.make_async_copy(b_hbm, b_ref, sems.at[1])]
    side = pl.ds(pl.multiple_of(at.ext_side * BS, BS), panel * BS)
    rest_start = (panel * BS) - at.ext_side // 2 * BS
    others = pl.ds(pl.multiple_of(rest_start, BS), 2 * panel * BS)
    early = pltpu.make_async_copy(graph_hbm.at[0, :, side], graph_ref.at[:, side], sems.at[2])
    late = [
        pltpu.make_async_copy(graph_hbm.at[0, :, others], graph_ref.at[:, others], sems.at[3]),
        pltpu.make_async_copy(columns_of(flow_hbm, at.int_side, panel), flow_ref, sems.at[4]),
    ]
    source = columns_of(flow_hbm, at.starts["ext"], 2 * panel)
    flows = []
    for t in range(steps):
        rows = slice(t * depth, (t + 1) * depth)
        flows.append(pltpu.make_async_copy(source.at[rows], flow_buf.at[rows], sems.at[5 + t]))
    for copy in small + flows[:1] + [early] + flows[1:] + late:
        copy.start()
    for copy in small:
        copy.wait()
    for t in range(steps):
        rows = slice(t * depth, (t + 1) * depth)
        flows[t].wait()
        turn(flow_buf[rows, :], a_ref, at.starts["ext"], at.first + t * (depth // BS), turned_ref, rows)
    early.wait()
    right = masked(graph_ref[:, rows_at(at.ext_side)], b_ref, at.ext_side, at.first)
    coded = Coded(out_refs)
    for i in range(2 * panel):
        coded.write(dot(turned_ref[i * BS : (i + 1) * BS, :], right), i)
    coded.finish()
    for copy in late:
        copy.wait()


def first_products(flow_t, graph, a_lines, b_lines, widths):
    inner, width = flow_t.shape[1:]
    panel = width // 3
    depth = min(512, inner)
    operands = [pltpu.with_memory_space_constraint(x, pltpu.HBM) for x in (a_lines, b_lines, flow_t, graph)]
    return call(
        functools.partial(first_kernel, depth),
        "first_products",
        operands,
        [IN_HBM] * 4,
        [jax.ShapeDtypeStruct((HEAD + 2 * panel, w), jnp.int16) for w in widths]
        + [
            pltpu.VMEM((2 * panel, inner), flow_t.dtype),
            pltpu.VMEM((inner, width), graph.dtype),
            pltpu.VMEM((inner, panel), flow_t.dtype),
        ],
        [
            pltpu.VMEM((inner, 2 * panel), flow_t.dtype),
            pltpu.SMEM(a_lines.shape, a_lines.dtype),
            pltpu.SMEM(b_lines.shape, b_lines.dtype),
            pltpu.SemaphoreType.DMA((5 + inner // depth,)),
        ],
        flops=2 * inner * BS * 2 * panel,
        moved=4 * inner * width,
        limit=PRODUCT_LIMIT,
    )


def product_kernel(half, wanted, turns, a_ref, b_ref, graph_ref, ext_rows_ref, int_rows_ref, *rest):
    refs = list(rest)
    inner, panel = graph_ref.shape[0], graph_ref.shape[1] // BS // 3
    at = Sides(inner, panel)
    parts = [part for part in ("ext", "own", "int") if part in wanted]
    outs = {part: [refs.pop(0) for _ in wanted[part]] for part in parts}
    turned_ref = refs.pop(0) if turns else int_rows_ref
    coded = {part: Coded(outs[part]) for part in parts if part != "own"}
    right = []
    for part in parts:
        column = at.columns[part] + half
        right.append(masked(graph_ref[:, rows_at(column)], b_ref, column, at.first))
    right = jnp.concatenate(right, axis=1) if len(right) > 1 else right[0]

    def multiply(side, start, source, names):
        used = [part for part in parts if part in names]
        if not used:
            return
        low = parts.index(used[0]) * BS
        for i in range(panel):
            block = side + i
            product = dot(source[rows_at(block - start), :], right[:, low : low + len(used) * BS])
            for j, part in enumerate(used):
                piece = product[:, j * BS : (j + 1) * BS]
                if part == "own":
                    outs[part][0][rows_at(block), :] = piece
                else:
                    coded[part].write(piece, block - at.starts[part])

    if turns:
        turn(int_rows_ref[...], a_ref, at.int_side, at.first, turned_ref, slice(None))
    multiply(panel, at.starts["ext"], ext_rows_ref, ("ext", "own", "int"))
    multiply(at.ext_side, at.starts["ext"], ext_rows_ref, ("ext", "own"))
    multiply(at.int_side, at.int_side, turned_ref, ("own", "int"))
    for part in coded:
        coded[part].finish()


def products(a_lines, b_lines, graph, ext_rows, int_rows, half, wanted, turns=False):
    inner, width = graph.shape
    panel = width // 3
    outs = []
    for part in ("ext", "own", "int"):
        for w in wanted.get(part, ()):
            if part == "own":
                outs.append(jax.ShapeDtypeStruct((width, w), jnp.float32))
            else:
                outs.append(jax.ShapeDtypeStruct((HEAD + 2 * panel, w), jnp.int16))
    if turns:
        outs.append(pltpu.VMEM((panel, inner), graph.dtype))
    return call(
        functools.partial(product_kernel, half, wanted, turns),
        "_".join(wanted) + f"_products_{half}",
        (a_lines, b_lines, graph, ext_rows, int_rows),
        [IN_SMEM, IN_SMEM] + [IN_VMEM] * 3,
        outs,
        flops=2 * inner * BS * sum(width if part == "own" else 2 * panel for part in wanted),
        moved=2 * inner * BS,
        limit=PRODUCT_LIMIT,
    )


def join_kernel(rows, half, lane, c_ref, own_ref, ext_ref, int_ref, keep_ref, send_ref, total):
    odd = lax.rem(lax.axis_index("blk"), 2)
    blocks = own_ref.shape[0] // BS
    panel = blocks // 3
    lanes = slice(lane, lane + ext_ref.shape[1])

    def add(below_ref, above_ref):
        below_scale = scales(below_ref[0:HEAD, :])
        above_scale = scales(above_ref[0:HEAD, :])
        for v in range(blocks):
            kept = c_ref[0, half, v].astype(jnp.float32)
            block = own_ref[v * BS : (v + 1) * BS, lanes] * kept
            if v < 2 * panel:
                codes = below_ref[HEAD + v * BS : HEAD + (v + 1) * BS, :]
                block += decode(codes, below_scale[v : v + 1] * kept)
            if v >= panel:
                i = v - panel
                codes = above_ref[HEAD + i * BS : HEAD + (i + 1) * BS, :]
                block += decode(codes, above_scale[i : i + 1] * kept)
            total[v * BS : (v + 1) * BS, :] = block

    @pl.when(odd == 1)
    def _():
        add(int_ref, ext_ref)

    @pl.when(odd == 0)
    def _():
        add(ext_ref, int_ref)

    for j in range(send_ref.shape[0]):
        strip = total[j * rows : (j + 1) * rows, :]
        power = powers(strip)
        send_ref[j, HEAD:, :] = code(strip, power)
        send_ref[j, 0:HEAD, :] = jnp.broadcast_to(power, (HEAD, power.shape[1])).astype(jnp.int32).astype(jnp.int16)
    keep_ref[...] = total[pl.ds(lax.axis_index("layer") * rows, rows), :]


def join(own, ext_part, int_part, c_lines, half, lane, layers):
    height = own.shape[0]
    width = ext_part.shape[1]
    rows = height // layers
    return call(
        functools.partial(join_kernel, rows, half, lane),
        f"join_{half}_{lane}",
        (c_lines, own, ext_part, int_part),
        [IN_SMEM] + [IN_VMEM] * 3,
        [
            jax.ShapeDtypeStruct((rows, width), jnp.float32),
            jax.ShapeDtypeStruct((layers, HEAD + rows, width), jnp.int16),
        ],
        [pltpu.VMEM((height, width), jnp.float32)],
        moved=8 * height * width,
    )


def square_kernel(kept_ref, got_ref, *rest):
    earlier, (square_ref, sums_ref) = rest[:-2], rest[-2:]
    layers = got_ref.shape[0]
    value = kept_ref[...]
    for distance in range(1, layers):
        other = lax.rem(lax.axis_index("layer") + distance, layers)
        value += decode(got_ref[other, HEAD:, :], scales(got_ref[other, 0:HEAD, :])[0:1])
    square = value * value
    square_ref[...] = square
    sums = jnp.broadcast_to(jnp.sum(square, axis=0, keepdims=True), (8, square.shape[1]))
    sums_ref[...] = jnp.concatenate([ref[...] for ref in earlier] + [sums], axis=1)


def square(kept, got, earlier, chunk):
    rows, width = kept.shape
    return call(
        square_kernel,
        f"square_{chunk}",
        (kept, got, *earlier),
        [IN_VMEM] * (2 + len(earlier)),
        [
            jax.ShapeDtypeStruct((rows, width), jnp.float32),
            jax.ShapeDtypeStruct((8, width + sum(sums.shape[1] for sums in earlier)), jnp.float32),
        ],
        moved=8 * kept.size,
    )


def rescale_kernel(height, count, *refs):
    squares, sums_ref, out_ref = refs[:count], refs[count], refs[-1]
    total = functools.reduce(jnp.add, [sums_ref[i, 0:1, :] for i in range(sums_ref.shape[0])])
    divisor = total / height + 1e-6
    column = 0
    for ref in squares:
        columns = slice(column, column + ref.shape[1])
        column += ref.shape[1]
        out_ref[0, :, columns] = ref[...] / divisor[:, columns]


def rescale(squares, sums, height):
    rows = squares[0].shape[0]
    width = sums.shape[2]
    return call(
        functools.partial(rescale_kernel, float(height), len(squares)),
        "rescale",
        (*squares, sums),
        [IN_VMEM] * (len(squares) + 1),
        jax.ShapeDtypeStruct((1, rows, width), jnp.float32),
        moved=8 * rows * width,
    )


def shards(flow_t, graph, a_pattern, b_pattern, c_pattern):
    layers = lax.axis_size("layer")
    blks = lax.axis_size("blk")
    width = flow_t.shape[2]
    panel = width // 3
    a_lines = a_pattern.transpose(2, 0, 1)
    b_lines = b_pattern.transpose(2, 0, 1)
    c_lines = c_pattern.transpose(0, 2, 1)

    def other_chip(i):
        return (i + 1 if i % 2 else i - 1) % blks

    def same_chip(i):
        return i ^ 1

    halves = panel // BS
    chunks = panel // LANES
    fine = (LANES,) * (BS // LANES)
    per_half = len(fine)
    *ext_parts, ext_rows, graph, flow_rest = first_products(flow_t, graph, a_lines, b_lines, fine)
    ext = [swap(part, "blk", other_chip) for part in ext_parts]
    wanted = {"own": (BS,), "int": fine}
    own, *int_parts, int_rows = products(a_lines, b_lines, graph, ext_rows, flow_rest, 0, wanted, turns=True)
    owns = [own]
    int_ = [swap(part, "blk", same_chip) for part in int_parts]
    latest = [own]

    def ordered(value):
        return after(value, latest[-1])

    def more_products(half):
        parts = products(ordered(a_lines), b_lines, graph, ext_rows, int_rows, half, {"ext": fine, "int": fine})
        ext.extend(swap(part, "blk", other_chip) for part in parts[:per_half])
        int_.extend(swap(part, "blk", same_chip) for part in parts[per_half:])
        latest.append(parts[0])
        owns.extend(products(ordered(a_lines), b_lines, graph, ext_rows, int_rows, half, {"own": (BS,)}))
        latest.append(owns[-1])

    strips, squares, sums = [], [], []

    def add_up(chunk):
        half, lane = divmod(chunk, per_half)
        kept, send = join(owns[half], ext[chunk], int_[chunk], ordered(c_lines), half, lane * LANES, layers)
        latest.append(send)
        strips.append((kept, lax.all_to_all(send, "layer", 0, 0, tiled=True)))

    def finish(chunk):
        kept, got = strips[chunk]
        squared, summed = square(ordered(kept), got, sums if chunk == chunks - 1 else [], chunk)
        latest.append(summed)
        squares.append(squared)
        sums.append(summed)

    for chunk in range(chunks + 1):
        if chunk < chunks:
            add_up(chunk)
        if chunk >= 1:
            finish(chunk - 1)
        if chunk % per_half == 0 and chunk // per_half + 1 < halves:
            more_products(chunk // per_half + 1)

    all_sums = lax.all_to_all(jnp.broadcast_to(sums[-1], (layers, *sums[-1].shape)), "layer", 0, 0, tiled=True)
    return rescale(squares, all_sums, width)


def solution(mesh):
    placed = (
        P("blk", "layer", None),
        P("blk", "layer", None),
        P("blk", None, None),
        P("blk", None, None),
        P("blk", None, None),
    )
    return jax.shard_map(
        shards, mesh=mesh, in_specs=placed, out_specs=P("blk", "layer", None), check_vma=False
    )
```

```python
import functools

import jax
import jax.numpy as jnp
from jax import lax
from jax.experimental import pallas as pl
from jax.experimental.pallas import tpu as pltpu
from jax.sharding import PartitionSpec as P

BS = 256
LANES = 128
HEAD = 16
STEPS = 256.0
TOP = 65534.0
LN2 = 0.6931471805599453
PRODUCT_LIMIT = 24000000
SMALL_LIMIT = 8 * 1024 * 1024
IN_SMEM = pl.BlockSpec(memory_space=pltpu.SMEM)
IN_VMEM = pl.BlockSpec(memory_space=pltpu.VMEM)
IN_HBM = pl.BlockSpec(memory_space=pltpu.HBM)


def swap(block, axis, partner):
    return lax.ppermute(block, axis, [(partner(i), i) for i in range(lax.axis_size(axis))])


def after(value, *others):
    return lax.optimization_barrier((value, *others))[0]


def call(kernel, name, operands, in_specs, out_shape, scratch_shapes=(), limit=SMALL_LIMIT):
    return pl.pallas_call(
        kernel,
        out_shape=out_shape,
        in_specs=in_specs,
        out_specs=jax.tree.map(lambda _: IN_VMEM, out_shape),
        scratch_shapes=list(scratch_shapes),
        compiler_params=pltpu.CompilerParams(vmem_limit_bytes=limit),
        cost_estimate=pl.CostEstimate(flops=1, bytes_accessed=1, transcendentals=0),
        name=name,
    )(*operands)


def powers(values):
    largest = jnp.maximum(jnp.max(values, axis=0, keepdims=True), 1e-3)
    return jnp.floor(jnp.log(largest) * (STEPS / LN2)) + 2.0


def code(values, power):
    scaled = values * (TOP * jnp.exp(power * (-LN2 / STEPS)))
    return ((scaled + 0.5).astype(jnp.int32) - 32767).astype(jnp.int16)


def scales(head):
    return jnp.exp(head.astype(jnp.int32).astype(jnp.float32) * (LN2 / STEPS)) * (1.0 / TOP)


def decode(codes, scale):
    return (codes.astype(jnp.int32) + 32767).astype(jnp.float32) * scale


def masked(values, pattern, column, first):
    depth, width = values.shape
    place = lax.broadcasted_iota(jnp.int32, (1, width), 1) // BS
    parts = []
    for u in range(depth // BS):
        factor = jnp.zeros((1, width), jnp.float32)
        for v in range(width // BS):
            factor = jnp.where(place == v, pattern[column + v, 0, first + u].astype(jnp.float32), factor)
        parts.append(values[u * BS : (u + 1) * BS] * factor.astype(values.dtype))
    return jnp.concatenate(parts, axis=0) if len(parts) > 1 else parts[0]


def dot(left_side, right_side):
    return lax.dot_general(
        left_side, right_side, (((1,), (0,)), ((), ())), preferred_element_type=jnp.float32
    )


def columns_of(ref, start, count):
    return ref.at[0, :, pl.ds(pl.multiple_of(start * BS, BS), count * BS)]


def rows_at(block, first=0):
    return pl.ds(pl.multiple_of(first + block * BS, HEAD), BS)


class Sides:
    def __init__(self, inner, panel):
        odd = lax.rem(lax.axis_index("blk"), 2)
        self.panel = panel
        self.first = lax.axis_index("layer") * (inner // BS)
        self.ext_side, self.int_side = odd * (2 * panel), (1 - odd) * (2 * panel)
        self.columns = {"ext": self.ext_side, "own": panel, "int": self.int_side}
        self.starts = {"ext": odd * panel, "own": 0, "int": (1 - odd) * panel}


class Coded:
    def __init__(self, refs):
        self.refs = refs
        self.heads = [jnp.zeros((HEAD, ref.shape[1]), jnp.float32) for ref in refs]

    def write(self, product, place):
        column = 0
        for c, ref in enumerate(self.refs):
            chunk = product[:, column : column + ref.shape[1]]
            column += ref.shape[1]
            power = powers(chunk)
            ref[rows_at(place, HEAD), :] = code(chunk, power)
            line = lax.broadcasted_iota(jnp.int32, self.heads[c].shape, 0)
            self.heads[c] = jnp.where(line == place, power, self.heads[c])

    def finish(self):
        for ref, head in zip(self.refs, self.heads):
            ref[0:HEAD, :] = head.astype(jnp.int32).astype(jnp.int16)


def multiply(at, parts, half, b_ref, graph_ref, ext_rows_ref, int_rows_ref, outs, ahead=None):
    coded = {part: Coded(outs[part]) for part in parts if part != "own"}
    right = []
    for part in parts:
        column = at.columns[part] + half
        right.append(masked(graph_ref[:, rows_at(column)], b_ref, column, at.first))
    right = jnp.concatenate(right, axis=1) if len(right) > 1 else right[0]
    sides = (
        (at.panel, at.starts["ext"], ext_rows_ref, ("ext", "own", "int")),
        (at.ext_side, at.starts["ext"], ext_rows_ref, ("ext", "own")),
        (at.int_side, at.int_side, int_rows_ref, ("own", "int")),
    )
    for side, start, source, names in sides:
        used = [part for part in parts if part in names]
        if not used:
            continue
        if ahead and source is int_rows_ref:
            ahead()
        low = parts.index(used[0]) * BS
        for i in range(at.panel):
            block = side + i
            product = dot(source[rows_at(block - start), :], right[:, low : low + len(used) * BS])
            for j, part in enumerate(used):
                piece = product[:, j * BS : (j + 1) * BS]
                if part == "own":
                    outs[part][0][rows_at(block), :] = piece
                else:
                    coded[part].write(piece, block - at.starts[part])
    for part in coded:
        coded[part].finish()


def take(refs, wanted):
    parts = [part for part in ("ext", "own", "int") if part in wanted]
    return parts, {part: [refs.pop(0) for _ in wanted[part]] for part in parts}


def product_shapes(wanted, width):
    shapes = []
    for part in ("ext", "own", "int"):
        for w in wanted.get(part, ()):
            if part == "own":
                shapes.append(jax.ShapeDtypeStruct((width, w), jnp.float32))
            else:
                shapes.append(jax.ShapeDtypeStruct((HEAD + 2 * (width // 3), w), jnp.int16))
    return shapes


def first_kernel(depth, wanted, a_hbm, b_hbm, flow_hbm, graph_hbm, *rest):
    refs = list(rest)
    parts, outs = take(refs, wanted)
    ext_rows_ref, int_rows_ref, graph_ref, ext_buf, int_buf, a_ref, b_ref, sems = refs
    inner, panel = int_buf.shape[0], int_buf.shape[1] // BS
    at = Sides(inner, panel)
    steps = inner // depth
    small = [pltpu.make_async_copy(a_hbm, a_ref, sems.at[0]), pltpu.make_async_copy(b_hbm, b_ref, sems.at[1])]
    side = pl.ds(pl.multiple_of(at.ext_side * BS, BS), panel * BS)
    others = pl.ds(pl.multiple_of((panel * BS) - at.ext_side // 2 * BS, BS), 2 * panel * BS)
    graphs = [
        pltpu.make_async_copy(graph_hbm.at[0, :, side], graph_ref.at[:, side], sems.at[2]),
        pltpu.make_async_copy(graph_hbm.at[0, :, others], graph_ref.at[:, others], sems.at[3]),
    ]

    def row_copies(start, buf, sem):
        source = columns_of(flow_hbm, start, buf.shape[1] // BS)
        for t in range(steps):
            rows = slice(t * depth, (t + 1) * depth)
            yield pltpu.make_async_copy(source.at[rows], buf.at[rows], sems.at[sem + t])

    ext_copies = list(row_copies(at.starts["ext"], ext_buf, 4))
    int_copies = list(row_copies(at.int_side, int_buf, 4 + steps))
    for copy in small + ext_copies[:1] + graphs[:1] + ext_copies[1:] + int_copies + graphs[1:]:
        copy.start()
    for copy in small:
        copy.wait()

    def turn(copies, buf, start, turned_ref):
        for t, copy in enumerate(copies):
            copy.wait()
            rows = slice(t * depth, (t + 1) * depth)
            turned_ref[:, rows] = masked(buf[rows, :], a_ref, start, at.first + t * (depth // BS)).T

    turn(ext_copies, ext_buf, at.starts["ext"], ext_rows_ref)
    for copy in graphs:
        copy.wait()
    turn_int = functools.partial(turn, int_copies, int_buf, at.int_side, int_rows_ref)
    multiply(at, parts, 0, b_ref, graph_ref, ext_rows_ref, int_rows_ref, outs, turn_int)


def first_products(flow_t, graph, a_lines, b_lines, wanted):
    inner, width = flow_t.shape[1:]
    panel = width // 3
    depth = min(512, inner)
    operands = [pltpu.with_memory_space_constraint(x, pltpu.HBM) for x in (a_lines, b_lines, flow_t, graph)]
    return call(
        functools.partial(first_kernel, depth, wanted),
        "first_products",
        operands,
        [IN_HBM] * 4,
        product_shapes(wanted, width)
        + [
            pltpu.VMEM((2 * panel, inner), flow_t.dtype),
            pltpu.VMEM((panel, inner), flow_t.dtype),
            pltpu.VMEM((inner, width), graph.dtype),
        ],
        [
            pltpu.VMEM((inner, 2 * panel), flow_t.dtype),
            pltpu.VMEM((inner, panel), flow_t.dtype),
            pltpu.SMEM(a_lines.shape, a_lines.dtype),
            pltpu.SMEM(b_lines.shape, b_lines.dtype),
            pltpu.SemaphoreType.DMA((4 + 2 * (inner // depth),)),
        ],
        limit=PRODUCT_LIMIT,
    )


def product_kernel(half, wanted, b_ref, graph_ref, ext_rows_ref, int_rows_ref, *rest):
    parts, outs = take(list(rest), wanted)
    inner, panel = graph_ref.shape[0], graph_ref.shape[1] // BS // 3
    multiply(Sides(inner, panel), parts, half, b_ref, graph_ref, ext_rows_ref, int_rows_ref, outs)


def products(b_lines, graph, ext_rows, int_rows, half, wanted):
    return call(
        functools.partial(product_kernel, half, wanted),
        "_".join(wanted) + f"_products_{half}",
        (b_lines, graph, ext_rows, int_rows),
        [IN_SMEM] + [IN_VMEM] * 3,
        product_shapes(wanted, graph.shape[1]),
        limit=PRODUCT_LIMIT,
    )


def split_strips(total, rows, position, keep_ref, send_ref):
    bit = lax.rem(lax.axis_index("layer") // position, 2)
    pairs = keep_ref.shape[0]
    for j in range(pairs):
        keep_ref[j] = total[pl.ds((2 * j + bit) * rows, rows), :]
    away = [total[pl.ds((2 * j + 1 - bit) * rows, rows), :] for j in range(pairs)]
    power = functools.reduce(jnp.maximum, [powers(strip) for strip in away])
    for j, strip in enumerate(away):
        send_ref[HEAD + j * rows : HEAD + (j + 1) * rows, :] = code(strip, power)
    send_ref[0:HEAD, :] = jnp.broadcast_to(power, (HEAD, power.shape[1])).astype(jnp.int32).astype(jnp.int16)


def join_kernel(rows, half, lane, c_ref, own_ref, ext_ref, int_ref, keep_ref, send_ref, total):
    odd = lax.rem(lax.axis_index("blk"), 2)
    blocks = own_ref.shape[0] // BS
    panel = blocks // 3
    lanes = slice(lane, lane + ext_ref.shape[1])

    def add(below_ref, above_ref):
        below_scale = scales(below_ref[0:HEAD, :])
        above_scale = scales(above_ref[0:HEAD, :])
        for v in range(blocks):
            kept = c_ref[0, half, v].astype(jnp.float32)
            block = own_ref[v * BS : (v + 1) * BS, lanes] * kept
            if v < 2 * panel:
                codes = below_ref[HEAD + v * BS : HEAD + (v + 1) * BS, :]
                block += decode(codes, below_scale[v : v + 1] * kept)
            if v >= panel:
                i = v - panel
                codes = above_ref[HEAD + i * BS : HEAD + (i + 1) * BS, :]
                block += decode(codes, above_scale[i : i + 1] * kept)
            total[v * BS : (v + 1) * BS, :] = block

    @pl.when(odd == 1)
    def _():
        add(int_ref, ext_ref)

    @pl.when(odd == 0)
    def _():
        add(ext_ref, int_ref)

    split_strips(total, rows, 1, keep_ref, send_ref)


def strips_shapes(pairs, rows, width):
    return [
        jax.ShapeDtypeStruct((pairs, rows, width), jnp.float32),
        jax.ShapeDtypeStruct((HEAD + pairs * rows, width), jnp.int16),
    ]


def join(own, ext_part, int_part, c_lines, half, lane, layers):
    height = own.shape[0]
    width = ext_part.shape[1]
    rows = height // layers
    return call(
        functools.partial(join_kernel, rows, half, lane),
        f"join_{half}_{lane}",
        (c_lines, own, ext_part, int_part),
        [IN_SMEM] + [IN_VMEM] * 3,
        strips_shapes(layers // 2, rows, width),
        [pltpu.VMEM((height, width), jnp.float32)],
    )


def halve_kernel(rows, position, kept_ref, got_ref, keep_ref, send_ref, total):
    scale = scales(got_ref[0:HEAD, :])[0:1]
    for j in range(kept_ref.shape[0]):
        codes = got_ref[HEAD + j * rows : HEAD + (j + 1) * rows, :]
        total[j * rows : (j + 1) * rows, :] = kept_ref[j] + decode(codes, scale)
    split_strips(total, rows, position, keep_ref, send_ref)


def halve(kept, got, position, chunk):
    strips, rows, width = kept.shape
    return call(
        functools.partial(halve_kernel, rows, position),
        f"halve_{position}_{chunk}",
        (kept, got),
        [IN_VMEM] * 2,
        strips_shapes(strips // 2, rows, width),
        [pltpu.VMEM((strips * rows, width), jnp.float32)],
    )


def square_kernel(kept_ref, got_ref, *rest):
    earlier, (square_ref, sums_ref) = rest[:-2], rest[-2:]
    value = kept_ref[0] + decode(got_ref[HEAD:, :], scales(got_ref[0:HEAD, :])[0:1])
    square = value * value
    square_ref[...] = square
    sums = jnp.broadcast_to(jnp.sum(square, axis=0, keepdims=True), (8, square.shape[1]))
    sums_ref[...] = jnp.concatenate([ref[...] for ref in earlier] + [sums], axis=1)


def square(kept, got, earlier, chunk):
    _, rows, width = kept.shape
    return call(
        square_kernel,
        f"square_{chunk}",
        (kept, got, *earlier),
        [IN_VMEM] * (2 + len(earlier)),
        [
            jax.ShapeDtypeStruct((rows, width), jnp.float32),
            jax.ShapeDtypeStruct((8, width + sum(sums.shape[1] for sums in earlier)), jnp.float32),
        ],
    )


def rescale_kernel(height, count, *refs):
    squares, sums, out_ref = refs[:count], refs[count:-1], refs[-1]
    total = functools.reduce(jnp.add, [ref[0:1, :] for ref in sums])
    divisor = total / height + 1e-6
    column = 0
    for ref in squares:
        columns = slice(column, column + ref.shape[1])
        column += ref.shape[1]
        out_ref[0, :, columns] = ref[...] / divisor[:, columns]


def rescale(squares, sums, height):
    rows = squares[0].shape[0]
    width = sums[0].shape[1]
    return call(
        functools.partial(rescale_kernel, float(height), len(squares)),
        "rescale",
        (*squares, *sums),
        [IN_VMEM] * (len(squares) + len(sums)),
        jax.ShapeDtypeStruct((1, rows, width), jnp.float32),
    )


def shards(flow_t, graph, a_pattern, b_pattern, c_pattern):
    layers = lax.axis_size("layer")
    blks = lax.axis_size("blk")
    width = flow_t.shape[2]
    panel = width // 3
    a_lines = a_pattern.transpose(2, 0, 1)
    b_lines = b_pattern.transpose(2, 0, 1)
    c_lines = c_pattern.transpose(0, 2, 1)

    def other_chip(i):
        return (i + 1 if i % 2 else i - 1) % blks

    def same_chip(i):
        return i ^ 1

    halves = panel // BS
    chunks = panel // LANES
    fine = (LANES,) * (BS // LANES)
    per_half = len(fine)
    ext, int_, owns, latest = [], [], [], []

    def ordered(value):
        return after(value, latest[-1])

    def send_sides(parts):
        ext.extend(swap(part, "blk", other_chip) for part in parts[:per_half])
        int_.extend(swap(part, "blk", same_chip) for part in parts[per_half:])

    both = {"ext": fine, "int": fine}
    *parts, ext_rows, int_rows, graph = first_products(flow_t, graph, a_lines, b_lines, both)
    send_sides(parts)
    latest.append(parts[0])

    def side_products(half):
        parts = products(ordered(b_lines), graph, ext_rows, int_rows, half, both)
        send_sides(parts)
        latest.append(parts[0])

    def own_products(half):
        owns.extend(products(ordered(b_lines), graph, ext_rows, int_rows, half, {"own": (BS,)}))
        latest.append(owns[-1])

    strips, squares, sums = [], [], []

    def add_up(chunk):
        half, lane = divmod(chunk, per_half)
        kept, send = join(owns[half], ext[chunk], int_[chunk], ordered(c_lines), half, lane * LANES, layers)
        latest.append(send)
        strips.append((kept, swap(send, "layer", lambda i: i ^ 1)))

    def scatter(chunk):
        kept, got = strips[chunk]
        position = 1
        while kept.shape[0] > 1:
            position *= 2
            kept, send = halve(ordered(kept), got, position, chunk)
            latest.append(send)
            got = swap(send, "layer", lambda i: i ^ position)
        strips[chunk] = kept, got

    def finish(chunk):
        kept, got = strips[chunk]
        squared, summed = square(ordered(kept), got, sums if chunk == chunks - 1 else [], chunk)
        latest.append(summed)
        squares.append(squared)
        sums.append(summed)

    own_products(0)
    for half in range(1, halves):
        side_products(half)
    for chunk in range(chunks + 2):
        if chunk < chunks:
            add_up(chunk)
        if (chunk + 1) % per_half == 0 and len(owns) < halves:
            own_products(len(owns))
        if 1 <= chunk <= chunks:
            scatter(chunk - 1)
        if chunk >= 2:
            finish(chunk - 2)

    mine = sums[-1]
    others = [swap(mine, "layer", lambda i: i ^ other) for other in range(1, layers)]
    return rescale(squares, [mine, *others], width)


def solution(mesh):
    placed = (
        P("blk", "layer", None),
        P("blk", "layer", None),
        P("blk", None, None),
        P("blk", None, None),
        P("blk", None, None),
    )
    return jax.shard_map(
        shards, mesh=mesh, in_specs=placed, out_specs=P("blk", "layer", None), check_vma=False
    )
```

```python
import functools

import jax
import jax.numpy as jnp
from jax import lax
from jax.experimental import pallas as pl
from jax.experimental.pallas import tpu as pltpu
from jax.sharding import PartitionSpec as P

BS = 256
LANES = 128
HEAD = 16
STEPS = 256.0
TOP = 65534.0
LN2 = 0.6931471805599453
PRODUCT_LIMIT = 24000000
SMALL_LIMIT = 8 * 1024 * 1024
IN_SMEM = pl.BlockSpec(memory_space=pltpu.SMEM)
IN_VMEM = pl.BlockSpec(memory_space=pltpu.VMEM)
IN_HBM = pl.BlockSpec(memory_space=pltpu.HBM)


def swap(block, axis, partner):
    return lax.ppermute(block, axis, [(partner(i), i) for i in range(lax.axis_size(axis))])


def after(value, *others):
    return lax.optimization_barrier((value, *others))[0]


def call(kernel, name, operands, in_specs, out_shape, scratch_shapes=(), limit=SMALL_LIMIT):
    return pl.pallas_call(
        kernel,
        out_shape=out_shape,
        in_specs=in_specs,
        out_specs=jax.tree.map(lambda _: IN_VMEM, out_shape),
        scratch_shapes=list(scratch_shapes),
        compiler_params=pltpu.CompilerParams(vmem_limit_bytes=limit),
        cost_estimate=pl.CostEstimate(flops=1, bytes_accessed=1, transcendentals=0),
        name=name,
    )(*operands)


def powers(values):
    largest = jnp.maximum(jnp.max(values, axis=0, keepdims=True), 1e-3)
    return jnp.floor(jnp.log(largest) * (STEPS / LN2)) + 2.0


def code(values, power):
    scaled = values * (TOP * jnp.exp(power * (-LN2 / STEPS)))
    return ((scaled + 0.5).astype(jnp.int32) - 32767).astype(jnp.int16)


def scales(head):
    return jnp.exp(head.astype(jnp.int32).astype(jnp.float32) * (LN2 / STEPS)) * (1.0 / TOP)


def decode(codes, scale):
    return (codes.astype(jnp.int32) + 32767).astype(jnp.float32) * scale


def masked(values, pattern, column, first):
    depth, width = values.shape
    place = lax.broadcasted_iota(jnp.int32, (1, width), 1) // BS
    parts = []
    for u in range(depth // BS):
        factor = jnp.zeros((1, width), jnp.float32)
        for v in range(width // BS):
            factor = jnp.where(place == v, pattern[column + v, 0, first + u].astype(jnp.float32), factor)
        parts.append(values[u * BS : (u + 1) * BS] * factor.astype(values.dtype))
    return jnp.concatenate(parts, axis=0) if len(parts) > 1 else parts[0]


def dot(left_side, right_side):
    return lax.dot_general(
        left_side, right_side, (((1,), (0,)), ((), ())), preferred_element_type=jnp.float32
    )


def columns_of(ref, start, count):
    return ref.at[0, :, pl.ds(pl.multiple_of(start * BS, BS), count * BS)]


def rows_at(block, first=0):
    return pl.ds(pl.multiple_of(first + block * BS, HEAD), BS)


class Sides:
    def __init__(self, inner, panel):
        odd = lax.rem(lax.axis_index("blk"), 2)
        self.panel = panel
        self.first = lax.axis_index("layer") * (inner // BS)
        self.ext_side, self.int_side = odd * (2 * panel), (1 - odd) * (2 * panel)
        self.columns = {"ext": self.ext_side, "own": panel, "int": self.int_side}
        self.starts = {"ext": odd * panel, "own": 0, "int": (1 - odd) * panel}


class Coded:
    def __init__(self, refs):
        self.refs = refs
        self.heads = [jnp.zeros((HEAD, ref.shape[1]), jnp.float32) for ref in refs]

    def write(self, product, place):
        column = 0
        for c, ref in enumerate(self.refs):
            chunk = product[:, column : column + ref.shape[1]]
            column += ref.shape[1]
            power = powers(chunk)
            ref[rows_at(place, HEAD), :] = code(chunk, power)
            line = lax.broadcasted_iota(jnp.int32, self.heads[c].shape, 0)
            self.heads[c] = jnp.where(line == place, power, self.heads[c])

    def finish(self):
        for ref, head in zip(self.refs, self.heads):
            ref[0:HEAD, :] = head.astype(jnp.int32).astype(jnp.int16)


def first_kernel(depth, a_hbm, b_hbm, flow_hbm, graph_hbm, *rest):
    out_ref, rows_ref, graph_ref, flow_ref, flow_buf, total, a_ref, b_ref, sems = rest
    inner, panel = flow_ref.shape[0], flow_ref.shape[1] // BS
    at = Sides(inner, panel)
    steps = inner // depth
    small = [pltpu.make_async_copy(a_hbm, a_ref, sems.at[0]), pltpu.make_async_copy(b_hbm, b_ref, sems.at[1])]
    side = pl.ds(pl.multiple_of(at.ext_side * BS, BS), panel * BS)
    others = pl.ds(pl.multiple_of((panel * BS) - at.ext_side // 2 * BS, BS), 2 * panel * BS)
    early = pltpu.make_async_copy(graph_hbm.at[0, :, side], graph_ref.at[:, side], sems.at[2])
    late = [
        pltpu.make_async_copy(columns_of(flow_hbm, at.int_side, panel), flow_ref, sems.at[3]),
        pltpu.make_async_copy(graph_hbm.at[0, :, others], graph_ref.at[:, others], sems.at[4]),
    ]
    source = columns_of(flow_hbm, at.starts["ext"], 2 * panel)
    flows = []
    for t in range(steps):
        rows = slice(t * depth, (t + 1) * depth)
        flows.append(pltpu.make_async_copy(source.at[rows], flow_buf.at[rows], sems.at[5 + t]))
    for copy in small + [early] + flows + late:
        copy.start()
    for copy in small:
        copy.wait()
    for t in range(steps):
        rows = slice(t * depth, (t + 1) * depth)
        first = at.first + t * (depth // BS)
        flows[t].wait()
        turned = masked(flow_buf[rows, :], a_ref, at.starts["ext"], first).T
        rows_ref[:, rows] = turned
        if t == 0:
            early.wait()
        right = masked(graph_ref[rows, rows_at(at.ext_side)], b_ref, at.ext_side, first)
        product = dot(turned, right[:, : out_ref.shape[1]])
        if t < steps - 1:
            total[...] = product if t == 0 else total[...] + product
    coded = Coded([out_ref])
    for i in range(2 * panel):
        rows = slice(i * BS, (i + 1) * BS)
        coded.write(product[rows] if steps == 1 else total[rows, :] + product[rows], i)
    coded.finish()
    for copy in late:
        copy.wait()


def first_products(flow_t, graph, a_lines, b_lines):
    inner, width = flow_t.shape[1:]
    panel = width // 3
    depth = min(512, inner)
    operands = [pltpu.with_memory_space_constraint(x, pltpu.HBM) for x in (a_lines, b_lines, flow_t, graph)]
    return call(
        functools.partial(first_kernel, depth),
        "first_products",
        operands,
        [IN_HBM] * 4,
        [
            jax.ShapeDtypeStruct((HEAD + 2 * panel, LANES), jnp.int16),
            pltpu.VMEM((2 * panel, inner), flow_t.dtype),
            pltpu.VMEM((inner, width), graph.dtype),
            pltpu.VMEM((inner, panel), flow_t.dtype),
        ],
        [
            pltpu.VMEM((inner, 2 * panel), flow_t.dtype),
            pltpu.VMEM((2 * panel, LANES), jnp.float32),
            pltpu.SMEM(a_lines.shape, a_lines.dtype),
            pltpu.SMEM(b_lines.shape, b_lines.dtype),
            pltpu.SemaphoreType.DMA((5 + inner // depth,)),
        ],
        limit=PRODUCT_LIMIT,
    )


def right_side(at, parts, half, b_ref, graph_ref):
    right = []
    for part in parts:
        column = at.columns[part] + half
        right.append(masked(graph_ref[:, rows_at(column)], b_ref, column, at.first))
    return jnp.concatenate(right, axis=1) if len(right) > 1 else right[0]


def ext_kernel(b_ref, graph_ref, ext_rows_ref, *out_refs):
    inner, panel = graph_ref.shape[0], graph_ref.shape[1] // BS // 3
    at = Sides(inner, panel)
    side = pl.ds(pl.multiple_of(at.ext_side * BS, BS), panel * BS)
    right = masked(graph_ref[:, side], b_ref, at.ext_side, at.first)[:, LANES:]
    coded = Coded(out_refs)
    for i in range(2 * panel):
        coded.write(dot(ext_rows_ref[i * BS : (i + 1) * BS, :], right), i)
    coded.finish()


def ext_products(b_lines, graph, ext_rows, widths):
    rows = HEAD + 2 * (graph.shape[1] // 3)
    return call(
        ext_kernel,
        "ext_products",
        (b_lines, graph, ext_rows),
        [IN_SMEM] + [IN_VMEM] * 2,
        [jax.ShapeDtypeStruct((rows, w), jnp.int16) for w in widths],
        limit=PRODUCT_LIMIT,
    )


def own_kernel(half, turns, a_ref, b_ref, graph_ref, ext_rows_ref, side_ref, own_ref, *rest):
    refs = list(rest)
    inner, panel = graph_ref.shape[0], graph_ref.shape[1] // BS // 3
    at = Sides(inner, panel)
    int_rows_ref = refs.pop() if turns else side_ref
    coded = Coded(refs)
    if turns:
        int_rows_ref[...] = masked(side_ref[...], a_ref, at.int_side, at.first).T
    right = right_side(at, ("own", "int"), half, b_ref, graph_ref)
    for i in range(panel):
        block = panel + i
        product = dot(ext_rows_ref[rows_at(block - at.starts["ext"]), :], right)
        own_ref[rows_at(block), :] = product[:, :BS]
        coded.write(product[:, BS:], i)
    for i in range(panel):
        block = at.ext_side + i
        own_ref[rows_at(block), :] = dot(ext_rows_ref[rows_at(block - at.starts["ext"]), :], right[:, :BS])
    for i in range(panel):
        product = dot(int_rows_ref[i * BS : (i + 1) * BS, :], right)
        own_ref[rows_at(at.int_side + i), :] = product[:, :BS]
        coded.write(product[:, BS:], panel + i)
    coded.finish()


def own_products(a_lines, b_lines, graph, ext_rows, side_rows, half, widths, turns=False):
    inner, width = graph.shape
    panel = width // 3
    outs = [jax.ShapeDtypeStruct((width, BS), jnp.float32)]
    outs += [jax.ShapeDtypeStruct((HEAD + 2 * panel, w), jnp.int16) for w in widths]
    if turns:
        outs.append(pltpu.VMEM((panel, inner), graph.dtype))
    return call(
        functools.partial(own_kernel, half, turns),
        f"own_products_{half}",
        (a_lines, b_lines, graph, ext_rows, side_rows),
        [IN_SMEM, IN_SMEM] + [IN_VMEM] * 3,
        outs,
        limit=PRODUCT_LIMIT,
    )


def split_strips(total, rows, position, keep_ref, send_ref):
    bit = lax.rem(lax.axis_index("layer") // position, 2)
    pairs = keep_ref.shape[0]
    for j in range(pairs):
        keep_ref[j] = total[pl.ds((2 * j + bit) * rows, rows), :]
    away = [total[pl.ds((2 * j + 1 - bit) * rows, rows), :] for j in range(pairs)]
    power = functools.reduce(jnp.maximum, [powers(strip) for strip in away])
    for j, strip in enumerate(away):
        send_ref[HEAD + j * rows : HEAD + (j + 1) * rows, :] = code(strip, power)
    send_ref[0:HEAD, :] = jnp.broadcast_to(power, (HEAD, power.shape[1])).astype(jnp.int32).astype(jnp.int16)


def join_kernel(rows, half, lane, ext_lane, c_ref, own_ref, ext_ref, int_ref, keep_ref, send_ref, total):
    odd = lax.rem(lax.axis_index("blk"), 2)
    panel = own_ref.shape[0] // BS // 3
    width = send_ref.shape[1]
    lanes = slice(lane, lane + width)
    refs = (ext_ref.at[:, ext_lane : ext_lane + width], int_ref)
    ext, int_ = ([(r, i) for i in range(2 * panel)] for r in range(2))
    odd_parts = [[part] for part in int_] + [[] for _ in range(panel)]
    even_parts = [[] for _ in range(panel)] + [[part] for part in int_[panel:] + int_[:panel]]
    for i, part in enumerate(ext):
        odd_parts[panel + i].append(part)
        even_parts[i].append(part)

    def add(parts):
        scale = [scales(ref[0:HEAD, :]) for ref in refs]
        for v in range(3 * panel):
            kept = c_ref[0, half, v].astype(jnp.float32)
            block = own_ref[v * BS : (v + 1) * BS, lanes] * kept
            for r, i in parts[v]:
                codes = refs[r][HEAD + i * BS : HEAD + (i + 1) * BS, :]
                block += decode(codes, scale[r][i : i + 1] * kept)
            total[v * BS : (v + 1) * BS, :] = block

    @pl.when(odd == 1)
    def _():
        add(odd_parts)

    @pl.when(odd == 0)
    def _():
        add(even_parts)

    split_strips(total, rows, 1, keep_ref, send_ref)


def strips_shapes(pairs, rows, width):
    return [
        jax.ShapeDtypeStruct((pairs, rows, width), jnp.float32),
        jax.ShapeDtypeStruct((HEAD + pairs * rows, width), jnp.int16),
    ]


def join(own, ext_part, ext_lane, int_part, c_lines, half, lane, layers):
    height = own.shape[0]
    width = int_part.shape[1]
    rows = height // layers
    return call(
        functools.partial(join_kernel, rows, half, lane, ext_lane),
        f"join_{half}_{lane}",
        (c_lines, own, ext_part, int_part),
        [IN_SMEM] + [IN_VMEM] * 3,
        strips_shapes(layers // 2, rows, width),
        [pltpu.VMEM((height, width), jnp.float32)],
    )


def halve_kernel(rows, position, kept_ref, got_ref, keep_ref, send_ref, total):
    scale = scales(got_ref[0:HEAD, :])[0:1]
    for j in range(kept_ref.shape[0]):
        codes = got_ref[HEAD + j * rows : HEAD + (j + 1) * rows, :]
        total[j * rows : (j + 1) * rows, :] = kept_ref[j] + decode(codes, scale)
    split_strips(total, rows, position, keep_ref, send_ref)


def halve(kept, got, position, chunk):
    strips, rows, width = kept.shape
    return call(
        functools.partial(halve_kernel, rows, position),
        f"halve_{position}_{chunk}",
        (kept, got),
        [IN_VMEM] * 2,
        strips_shapes(strips // 2, rows, width),
        [pltpu.VMEM((strips * rows, width), jnp.float32)],
    )


def square_kernel(kept_ref, got_ref, *rest):
    earlier, (square_ref, sums_ref) = rest[:-2], rest[-2:]
    value = kept_ref[0] + decode(got_ref[HEAD:, :], scales(got_ref[0:HEAD, :])[0:1])
    square = value * value
    square_ref[...] = square
    sums = jnp.broadcast_to(jnp.sum(square, axis=0, keepdims=True), (8, square.shape[1]))
    sums_ref[...] = jnp.concatenate([ref[...] for ref in earlier] + [sums], axis=1)


def square(kept, got, earlier, chunk):
    _, rows, width = kept.shape
    return call(
        square_kernel,
        f"square_{chunk}",
        (kept, got, *earlier),
        [IN_VMEM] * (2 + len(earlier)),
        [
            jax.ShapeDtypeStruct((rows, width), jnp.float32),
            jax.ShapeDtypeStruct((8, width + sum(sums.shape[1] for sums in earlier)), jnp.float32),
        ],
    )


def rescale_kernel(height, count, *refs):
    squares, sums, out_ref = refs[:count], refs[count:-1], refs[-1]
    total = functools.reduce(jnp.add, [ref[0:1, :] for ref in sums])
    divisor = total / height + 1e-6
    column = 0
    for ref in squares:
        columns = slice(column, column + ref.shape[1])
        column += ref.shape[1]
        out_ref[0, :, columns] = ref[...] / divisor[:, columns]


def rescale(squares, sums, height):
    rows = squares[0].shape[0]
    width = sums[0].shape[1]
    return call(
        functools.partial(rescale_kernel, float(height), len(squares)),
        "rescale",
        (*squares, *sums),
        [IN_VMEM] * (len(squares) + len(sums)),
        jax.ShapeDtypeStruct((1, rows, width), jnp.float32),
    )


def shards(flow_t, graph, a_pattern, b_pattern, c_pattern):
    layers = lax.axis_size("layer")
    blks = lax.axis_size("blk")
    width = flow_t.shape[2]
    panel = width // 3
    a_lines = a_pattern.transpose(2, 0, 1)
    b_lines = b_pattern.transpose(2, 0, 1)
    c_lines = c_pattern.transpose(0, 2, 1)

    def other_chip(i):
        return (i + 1 if i % 2 else i - 1) % blks

    def same_chip(i):
        return i ^ 1

    halves = panel // BS
    chunks = panel // LANES
    fine = (LANES,) * (BS // LANES)
    per_half = len(fine)
    ext, ints, owns, latest = [], [], [], []

    def ordered(value):
        return after(value, latest[-1])

    def send_ext(parts):
        for part in parts:
            got = swap(part, "blk", other_chip)
            ext.extend((got, lane) for lane in range(0, part.shape[1], LANES))
        latest.append(parts[0])

    first_part, ext_rows, graph, side_rows = first_products(flow_t, graph, a_lines, b_lines)
    send_ext([first_part])

    def own_half(half, side_rows, turns):
        own, *parts = own_products(a_lines, ordered(b_lines), graph, ext_rows, side_rows, half, fine, turns)
        if turns:
            side_rows = parts.pop()
        ints.extend(swap(part, "blk", same_chip) for part in parts)
        owns.append(own)
        latest.append(own)
        return side_rows

    side_rows = own_half(0, side_rows, True)
    send_ext(ext_products(ordered(b_lines), graph, ext_rows, (panel - 2 * LANES, LANES)))
    strips, squares, sums = [], [], []

    def add_up(chunk):
        half, lane = divmod(chunk, per_half)
        kept, send = join(owns[half], *ext[chunk], ints[chunk], ordered(c_lines), half, lane * LANES, layers)
        latest.append(send)
        strips.append((kept, swap(send, "layer", lambda i: i ^ 1)))

    def scatter(chunk):
        kept, got = strips[chunk]
        position = 1
        while kept.shape[0] > 1:
            position *= 2
            kept, send = halve(ordered(kept), got, position, chunk)
            latest.append(send)
            got = swap(send, "layer", lambda i: i ^ position)
        strips[chunk] = kept, got

    def finish(chunk):
        kept, got = strips[chunk]
        squared, summed = square(ordered(kept), got, sums if chunk == chunks - 1 else [], chunk)
        latest.append(summed)
        squares.append(squared)
        sums.append(summed)

    add_up(0)
    for half in range(1, halves):
        own_half(half, side_rows, False)
    scatter(0)
    for chunk in range(1, chunks):
        if chunk == chunks - 1:
            finish(0)
        add_up(chunk)
    for chunk in range(1, chunks):
        scatter(chunk)
    for chunk in range(1, chunks):
        finish(chunk)

    mine = sums[-1]
    others = [swap(mine, "layer", lambda i: i ^ other) for other in range(1, layers)]
    return rescale(squares, [mine, *others], width)


def solution(mesh):
    placed = (
        P("blk", "layer", None),
        P("blk", "layer", None),
        P("blk", None, None),
        P("blk", None, None),
        P("blk", None, None),
    )
    return jax.shard_map(
        shards, mesh=mesh, in_specs=placed, out_specs=P("blk", "layer", None), check_vma=False
    )
```

```python
import functools

import jax
import jax.numpy as jnp
from jax import lax
from jax.experimental import pallas as pl
from jax.experimental.pallas import tpu as pltpu
from jax.sharding import PartitionSpec as P

BS = 256
LANES = 128
HEAD = 16
STEPS = 256.0
TOP = 65534.0
LN2 = 0.6931471805599453
PRODUCT_LIMIT = 24000000
SMALL_LIMIT = 8 * 1024 * 1024
IN_SMEM = pl.BlockSpec(memory_space=pltpu.SMEM)
IN_VMEM = pl.BlockSpec(memory_space=pltpu.VMEM)
IN_HBM = pl.BlockSpec(memory_space=pltpu.HBM)


def swap(block, axis, partner):
    return lax.ppermute(block, axis, [(partner(i), i) for i in range(lax.axis_size(axis))])


def after(value, *others):
    return lax.optimization_barrier((value, *others))[0]


def call(kernel, name, operands, in_specs, out_shape, scratch_shapes=(), limit=SMALL_LIMIT):
    return pl.pallas_call(
        kernel,
        out_shape=out_shape,
        in_specs=in_specs,
        out_specs=jax.tree.map(lambda _: IN_VMEM, out_shape),
        scratch_shapes=list(scratch_shapes),
        compiler_params=pltpu.CompilerParams(vmem_limit_bytes=limit),
        cost_estimate=pl.CostEstimate(flops=1, bytes_accessed=1, transcendentals=0),
        name=name,
    )(*operands)


def powers(values):
    largest = jnp.maximum(jnp.max(values, axis=0, keepdims=True), 1e-3)
    return jnp.floor(jnp.log(largest) * (STEPS / LN2)) + 2.0


def code(values, power):
    scaled = values * (TOP * jnp.exp(power * (-LN2 / STEPS)))
    return ((scaled + 0.5).astype(jnp.int32) - 32767).astype(jnp.int16)


def scales(head):
    return jnp.exp(head.astype(jnp.int32).astype(jnp.float32) * (LN2 / STEPS)) * (1.0 / TOP)


def decode(codes, scale):
    return (codes.astype(jnp.int32) + 32767).astype(jnp.float32) * scale


def masked(values, pattern, column, first):
    depth, width = values.shape
    place = lax.broadcasted_iota(jnp.int32, (1, width), 1) // BS
    parts = []
    for u in range(depth // BS):
        factor = jnp.zeros((1, width), jnp.float32)
        for v in range(width // BS):
            factor = jnp.where(place == v, pattern[column + v, 0, first + u].astype(jnp.float32), factor)
        parts.append(values[u * BS : (u + 1) * BS] * factor.astype(values.dtype))
    return jnp.concatenate(parts, axis=0) if len(parts) > 1 else parts[0]


def dot(left_side, right_side):
    return lax.dot_general(
        left_side, right_side, (((1,), (0,)), ((), ())), preferred_element_type=jnp.float32
    )


def columns_of(ref, start, count):
    return ref.at[0, :, pl.ds(pl.multiple_of(start * BS, BS), count * BS)]


def blocks_at(block, count=1):
    return pl.ds(pl.multiple_of(block * BS, BS), count * BS)


class Sides:
    def __init__(self, inner, panel):
        odd = lax.rem(lax.axis_index("blk"), 2)
        self.panel = panel
        self.first = lax.axis_index("layer") * (inner // BS)
        self.ext_side, self.int_side = odd * (2 * panel), (1 - odd) * (2 * panel)
        self.ext_rows = odd * panel
        self.rest = (1 - odd) * panel
        self.own, self.int = odd * panel, (1 - odd) * panel


class Coded:
    def __init__(self, refs):
        self.refs = refs
        self.heads = [jnp.zeros((HEAD, ref.shape[1]), jnp.float32) for ref in refs]

    def write_all(self, product, place):
        for i in range(product.shape[0] // BS):
            self.write(product[i * BS : (i + 1) * BS], place + i)

    def write(self, product, place):
        column = 0
        for c, ref in enumerate(self.refs):
            chunk = product[:, column : column + ref.shape[1]]
            column += ref.shape[1]
            power = powers(chunk)
            ref[HEAD + place * BS : HEAD + (place + 1) * BS, :] = code(chunk, power)
            line = lax.broadcasted_iota(jnp.int32, self.heads[c].shape, 0)
            self.heads[c] = jnp.where(line == place, power, self.heads[c])

    def finish(self):
        for ref, head in zip(self.refs, self.heads):
            ref[0:HEAD, :] = head.astype(jnp.int32).astype(jnp.int16)


def first_kernel(depth, a_hbm, b_hbm, flow_hbm, graph_hbm, *rest):
    out_refs, (rows_ref, graph_ref, flow_buf, total, a_ref, b_ref, sems) = rest[:-7], rest[-7:]
    inner, panel = graph_ref.shape[0], graph_ref.shape[1] // BS
    at = Sides(inner, panel)
    steps = inner // depth
    small = [pltpu.make_async_copy(a_hbm, a_ref, sems.at[0]), pltpu.make_async_copy(b_hbm, b_ref, sems.at[1])]
    graph_copy = pltpu.make_async_copy(columns_of(graph_hbm, at.ext_side, panel), graph_ref, sems.at[2])
    source = columns_of(flow_hbm, at.ext_rows, 2 * panel)
    flows = []
    for t in range(steps):
        rows = slice(t * depth, (t + 1) * depth)
        flows.append(pltpu.make_async_copy(source.at[rows], flow_buf.at[rows], sems.at[3 + t]))
    for copy in small + flows[:1] + [graph_copy] + flows[1:]:
        copy.start()
    for copy in small:
        copy.wait()
    for t in range(steps):
        rows = slice(t * depth, (t + 1) * depth)
        first = at.first + t * (depth // BS)
        flows[t].wait()
        turned = masked(flow_buf[rows, :], a_ref, at.ext_rows, first).T
        rows_ref[:, rows] = turned
        if t == 0:
            graph_copy.wait()
        product = dot(turned, masked(graph_ref[rows, :BS], b_ref, at.ext_side, first))
        if t < steps - 1:
            total[...] = product if t == 0 else total[...] + product
    coded = Coded(out_refs)
    for i in range(2 * panel):
        rows = slice(i * BS, (i + 1) * BS)
        coded.write(product[rows] if steps == 1 else total[rows, :] + product[rows], i)
    coded.finish()


def in_hbm(*operands):
    return [pltpu.with_memory_space_constraint(x, pltpu.HBM) for x in operands]


def first_products(flow_t, graph, a_lines, b_lines, widths):
    inner, width = flow_t.shape[1:]
    panel = width // 3
    depth = min(512, inner)
    return call(
        functools.partial(first_kernel, depth),
        "first_products",
        in_hbm(a_lines, b_lines, flow_t, graph),
        [IN_HBM] * 4,
        [jax.ShapeDtypeStruct((HEAD + 2 * panel, w), jnp.int16) for w in widths]
        + [pltpu.VMEM((2 * panel, inner), flow_t.dtype), pltpu.VMEM((inner, panel), graph.dtype)],
        [
            pltpu.VMEM((inner, 2 * panel), flow_t.dtype),
            pltpu.VMEM((2 * panel, BS), jnp.float32),
            pltpu.SMEM(a_lines.shape, a_lines.dtype),
            pltpu.SMEM(b_lines.shape, b_lines.dtype),
            pltpu.SemaphoreType.DMA((3 + inner // depth,)),
        ],
        limit=PRODUCT_LIMIT,
    )


def own_half(at, half, b_ref, rest_ref, ext_rows_ref, int_rows_ref, own_ref, int_refs):
    panel = at.panel
    right = [
        masked(rest_ref[:, blocks_at(column + half)], b_ref, at.rest + column + half, at.first)
        for column in (at.own, at.int)
    ]
    both = jnp.concatenate(right, axis=1)
    coded = Coded(int_refs)
    mid = dot(ext_rows_ref[blocks_at(panel - at.ext_rows, panel), :], both)
    own_ref[panel * BS : 2 * panel * BS, :] = mid[:, :BS]
    coded.write_all(mid[:, BS:], 0)
    own_ref[blocks_at(at.ext_side, panel), :] = dot(
        ext_rows_ref[blocks_at(at.ext_side - at.ext_rows, panel), :], right[0]
    )
    side = dot(int_rows_ref[...], both)
    own_ref[blocks_at(at.int_side, panel), :] = side[:, :BS]
    coded.write_all(side[:, BS:], panel)
    coded.finish()


def second_kernel(ext_count, a_ref, b_ref, graph_ref, ext_rows_ref, flow_hbm, graph_hbm, *rest):
    out_refs, (int_rows_ref, rest_ref, flow_buf, sems) = rest[:-4], rest[-4:]
    ext_refs, (own_ref, *int_refs) = out_refs[:ext_count], out_refs[ext_count:]
    inner, panel = graph_ref.shape[0], graph_ref.shape[1] // BS
    at = Sides(inner, panel)
    copies = [
        pltpu.make_async_copy(columns_of(graph_hbm, at.rest, 2 * panel), rest_ref, sems.at[0]),
        pltpu.make_async_copy(columns_of(flow_hbm, at.int_side, panel), flow_buf, sems.at[1]),
    ]
    for copy in copies:
        copy.start()
    right = masked(graph_ref[:, BS:], b_ref, at.ext_side + 1, at.first)
    product = dot(ext_rows_ref[...], right)
    coded = Coded(ext_refs)
    coded.write_all(product, 0)
    coded.finish()
    for copy in copies:
        copy.wait()
    int_rows_ref[...] = masked(flow_buf[...], a_ref, at.int_side, at.first).T
    own_half(at, 0, b_ref, rest_ref, ext_rows_ref, int_rows_ref, own_ref, int_refs)


def second_products(a_lines, b_lines, graph_ext, ext_rows, flow_t, graph, ext_widths, int_widths):
    inner, width = flow_t.shape[1:]
    panel = width // 3
    coded = [jax.ShapeDtypeStruct((HEAD + 2 * panel, w), jnp.int16) for w in ext_widths + int_widths]
    own = jax.ShapeDtypeStruct((width, BS), jnp.float32)
    return call(
        functools.partial(second_kernel, len(ext_widths)),
        "second_products",
        (a_lines, b_lines, graph_ext, ext_rows, *in_hbm(flow_t, graph)),
        [IN_SMEM, IN_SMEM, IN_VMEM, IN_VMEM, IN_HBM, IN_HBM],
        coded[: len(ext_widths)]
        + [own]
        + coded[len(ext_widths) :]
        + [pltpu.VMEM((panel, inner), flow_t.dtype), pltpu.VMEM((inner, 2 * panel), graph.dtype)],
        [pltpu.VMEM((inner, panel), flow_t.dtype), pltpu.SemaphoreType.DMA((2,))],
        limit=PRODUCT_LIMIT,
    )


def own_kernel(half, b_ref, rest_ref, ext_rows_ref, int_rows_ref, own_ref, *int_refs):
    at = Sides(rest_ref.shape[0], rest_ref.shape[1] // BS // 2)
    own_half(at, half, b_ref, rest_ref, ext_rows_ref, int_rows_ref, own_ref, int_refs)


def own_products(b_lines, graph_rest, ext_rows, int_rows, half, widths):
    panel = graph_rest.shape[1] // 2
    return call(
        functools.partial(own_kernel, half),
        f"own_products_{half}",
        (b_lines, graph_rest, ext_rows, int_rows),
        [IN_SMEM] + [IN_VMEM] * 3,
        [jax.ShapeDtypeStruct((3 * panel, BS), jnp.float32)]
        + [jax.ShapeDtypeStruct((HEAD + 2 * panel, w), jnp.int16) for w in widths],
        limit=PRODUCT_LIMIT,
    )


def split_strips(total, rows, position, keep_ref, send_ref):
    bit = lax.rem(lax.axis_index("layer") // position, 2)
    pairs = keep_ref.shape[0]
    for j in range(pairs):
        keep_ref[j] = total[pl.ds((2 * j + bit) * rows, rows), :]
    away = [total[pl.ds((2 * j + 1 - bit) * rows, rows), :] for j in range(pairs)]
    power = functools.reduce(jnp.maximum, [powers(strip) for strip in away])
    for j, strip in enumerate(away):
        send_ref[HEAD + j * rows : HEAD + (j + 1) * rows, :] = code(strip, power)
    send_ref[0:HEAD, :] = jnp.broadcast_to(power, (HEAD, power.shape[1])).astype(jnp.int32).astype(jnp.int16)


def join_kernel(rows, half, lane, c_ref, own_ref, ext_ref, int_ref, keep_ref, send_ref, total):
    odd = lax.rem(lax.axis_index("blk"), 2)
    panel = own_ref.shape[0] // BS // 3
    lanes = slice(lane, lane + ext_ref.shape[1])
    refs = (ext_ref, int_ref)
    ext, int_ = ([(r, i) for i in range(2 * panel)] for r in range(2))
    odd_parts = [[part] for part in int_] + [[] for _ in range(panel)]
    even_parts = [[] for _ in range(panel)] + [[part] for part in int_[panel:] + int_[:panel]]
    for i, part in enumerate(ext):
        odd_parts[panel + i].append(part)
        even_parts[i].append(part)

    def add(parts):
        scale = [scales(ref[0:HEAD, :]) for ref in refs]
        for v in range(3 * panel):
            kept = c_ref[0, half, v].astype(jnp.float32)
            block = own_ref[v * BS : (v + 1) * BS, lanes] * kept
            for r, i in parts[v]:
                codes = refs[r][HEAD + i * BS : HEAD + (i + 1) * BS, :]
                block += decode(codes, scale[r][i : i + 1] * kept)
            total[v * BS : (v + 1) * BS, :] = block

    @pl.when(odd == 1)
    def _():
        add(odd_parts)

    @pl.when(odd == 0)
    def _():
        add(even_parts)

    split_strips(total, rows, 1, keep_ref, send_ref)


def strips_shapes(pairs, rows, width):
    return [
        jax.ShapeDtypeStruct((pairs, rows, width), jnp.float32),
        jax.ShapeDtypeStruct((HEAD + pairs * rows, width), jnp.int16),
    ]


def join(own, ext_part, int_part, c_lines, half, lane, layers):
    height = own.shape[0]
    width = int_part.shape[1]
    rows = height // layers
    return call(
        functools.partial(join_kernel, rows, half, lane),
        f"join_{half}_{lane}",
        (c_lines, own, ext_part, int_part),
        [IN_SMEM] + [IN_VMEM] * 3,
        strips_shapes(layers // 2, rows, width),
        [pltpu.VMEM((height, width), jnp.float32)],
    )


def halve_kernel(rows, position, kept_ref, got_ref, keep_ref, send_ref, total):
    scale = scales(got_ref[0:HEAD, :])[0:1]
    for j in range(kept_ref.shape[0]):
        codes = got_ref[HEAD + j * rows : HEAD + (j + 1) * rows, :]
        total[j * rows : (j + 1) * rows, :] = kept_ref[j] + decode(codes, scale)
    split_strips(total, rows, position, keep_ref, send_ref)


def halve(kept, got, position, chunk):
    strips, rows, width = kept.shape
    return call(
        functools.partial(halve_kernel, rows, position),
        f"halve_{position}_{chunk}",
        (kept, got),
        [IN_VMEM] * 2,
        strips_shapes(strips // 2, rows, width),
        [pltpu.VMEM((strips * rows, width), jnp.float32)],
    )


def square_kernel(kept_ref, got_ref, *rest):
    earlier, (square_ref, sums_ref) = rest[:-2], rest[-2:]
    value = kept_ref[0] + decode(got_ref[HEAD:, :], scales(got_ref[0:HEAD, :])[0:1])
    square = value * value
    square_ref[...] = square
    sums = jnp.broadcast_to(jnp.sum(square, axis=0, keepdims=True), (8, square.shape[1]))
    sums_ref[...] = jnp.concatenate([ref[...] for ref in earlier] + [sums], axis=1)


def square(kept, got, earlier, chunk):
    _, rows, width = kept.shape
    return call(
        square_kernel,
        f"square_{chunk}",
        (kept, got, *earlier),
        [IN_VMEM] * (2 + len(earlier)),
        [
            jax.ShapeDtypeStruct((rows, width), jnp.float32),
            jax.ShapeDtypeStruct((8, width + sum(sums.shape[1] for sums in earlier)), jnp.float32),
        ],
    )


def rescale_kernel(height, count, *refs):
    squares, sums, out_ref = refs[:count], refs[count:-1], refs[-1]
    total = functools.reduce(jnp.add, [ref[0:1, :] for ref in sums])
    divisor = total / height + 1e-6
    column = 0
    for ref in squares:
        columns = slice(column, column + ref.shape[1])
        column += ref.shape[1]
        out_ref[0, :, columns] = ref[...] / divisor[:, columns]


def rescale(squares, sums, height):
    rows = squares[0].shape[0]
    width = sums[0].shape[1]
    return call(
        functools.partial(rescale_kernel, float(height), len(squares)),
        "rescale",
        (*squares, *sums),
        [IN_VMEM] * (len(squares) + len(sums)),
        jax.ShapeDtypeStruct((1, rows, width), jnp.float32),
    )


def shards(flow_t, graph, a_pattern, b_pattern, c_pattern):
    layers = lax.axis_size("layer")
    blks = lax.axis_size("blk")
    width = flow_t.shape[2]
    panel = width // 3
    a_lines = a_pattern.transpose(2, 0, 1)
    b_lines = b_pattern.transpose(2, 0, 1)
    c_lines = c_pattern.transpose(0, 2, 1)

    def other_chip(i):
        return (i + 1 if i % 2 else i - 1) % blks

    def same_chip(i):
        return i ^ 1

    halves = panel // BS
    chunks = panel // LANES
    fine = (LANES,) * (BS // LANES)
    per_half = len(fine)
    ext, ints, owns, latest = [], [], [], []

    def ordered(value):
        return after(value, latest[-1])

    def send_ext(parts):
        for part in parts:
            ext.append(swap(part, "blk", other_chip))
        latest.append(parts[0])

    *parts, ext_rows, graph_ext = first_products(flow_t, graph, a_lines, b_lines, fine)
    send_ext(parts)
    ext_widths = fine * (halves - 1)
    *parts, int_rows, graph_rest = second_products(
        a_lines, b_lines, graph_ext, ext_rows, flow_t, graph, ext_widths, fine
    )
    send_ext(parts[: len(ext_widths)])

    def send_int(own, *parts):
        ints.extend(swap(part, "blk", same_chip) for part in parts)
        owns.append(own)
        latest.append(own)

    send_int(*parts[len(ext_widths) :])
    strips, squares, sums = [], [], []

    def add_up(chunk):
        half, lane = divmod(chunk, per_half)
        kept, send = join(owns[half], ext[chunk], ints[chunk], ordered(c_lines), half, lane * LANES, layers)
        latest.append(send)
        strips.append((kept, swap(send, "layer", lambda i: i ^ 1)))

    def scatter(chunk):
        kept, got = strips[chunk]
        position = 1
        while kept.shape[0] > 1:
            position *= 2
            kept, send = halve(ordered(kept), got, position, chunk)
            latest.append(send)
            got = swap(send, "layer", lambda i: i ^ position)
        strips[chunk] = kept, got

    def finish(chunk):
        kept, got = strips[chunk]
        squared, summed = square(ordered(kept), got, sums if chunk == chunks - 1 else [], chunk)
        latest.append(summed)
        squares.append(squared)
        sums.append(summed)

    add_up(0)
    for half in range(1, halves):
        send_int(*own_products(ordered(b_lines), graph_rest, ext_rows, int_rows, half, fine))
    add_up(1)
    scatter(0)
    for chunk in range(2, chunks):
        if chunk == chunks - 1:
            finish(0)
        add_up(chunk)
    for chunk in range(1, chunks):
        scatter(chunk)
    for chunk in range(1, chunks):
        finish(chunk)

    mine = sums[-1]
    others = [swap(mine, "layer", lambda i: i ^ other) for other in range(1, layers)]
    return rescale(squares, [mine, *others], width)


def solution(mesh):
    placed = (
        P("blk", "layer", None),
        P("blk", "layer", None),
        P("blk", None, None),
        P("blk", None, None),
        P("blk", None, None),
    )
    return jax.shard_map(
        shards, mesh=mesh, in_specs=placed, out_specs=P("blk", "layer", None), check_vma=False
    )
```

```python
import functools

import jax
import jax.numpy as jnp
from jax import lax
from jax.experimental import pallas as pl
from jax.experimental.pallas import tpu as pltpu
from jax.sharding import PartitionSpec as P

BS = 256
LANES = 128
HEAD = 16
STEPS = 256.0
TOP = 65534.0
LN2 = 0.6931471805599453
DIRECT = 0
PRODUCT_LIMIT = 24000000
SMALL_LIMIT = 8 * 1024 * 1024
IN_SMEM = pl.BlockSpec(memory_space=pltpu.SMEM)
IN_VMEM = pl.BlockSpec(memory_space=pltpu.VMEM)
IN_HBM = pl.BlockSpec(memory_space=pltpu.HBM)


def swap(block, axis, partner):
    return lax.ppermute(block, axis, [(partner(i), i) for i in range(lax.axis_size(axis))])


def after(value, *others):
    return lax.optimization_barrier((value, *others))[0]


def call(kernel, name, operands, in_specs, out_shape, scratch_shapes=(), limit=SMALL_LIMIT):
    return pl.pallas_call(
        kernel,
        out_shape=out_shape,
        in_specs=in_specs,
        out_specs=jax.tree.map(lambda _: IN_VMEM, out_shape),
        scratch_shapes=list(scratch_shapes),
        compiler_params=pltpu.CompilerParams(vmem_limit_bytes=limit),
        cost_estimate=pl.CostEstimate(flops=1, bytes_accessed=1, transcendentals=0),
        name=name,
    )(*operands)


def powers(values):
    largest = jnp.maximum(jnp.max(values, axis=0, keepdims=True), 1e-3)
    return jnp.floor(jnp.log(largest) * (STEPS / LN2)) + 2.0


def code(values, power):
    scaled = values * (TOP * jnp.exp(power * (-LN2 / STEPS)))
    return ((scaled + 0.5).astype(jnp.int32) - 32767).astype(jnp.int16)


def scales(head):
    return jnp.exp(head.astype(jnp.int32).astype(jnp.float32) * (LN2 / STEPS)) * (1.0 / TOP)


def decode(codes, scale):
    return (codes.astype(jnp.int32) + 32767).astype(jnp.float32) * scale


def masked(values, pattern, column, first):
    depth, width = values.shape
    place = lax.broadcasted_iota(jnp.int32, (1, width), 1) // BS
    parts = []
    for u in range(depth // BS):
        factor = jnp.zeros((1, width), jnp.float32)
        for v in range(width // BS):
            factor = jnp.where(place == v, pattern[column + v, 0, first + u].astype(jnp.float32), factor)
        parts.append(values[u * BS : (u + 1) * BS] * factor.astype(values.dtype))
    return jnp.concatenate(parts, axis=0) if len(parts) > 1 else parts[0]


def dot(left_side, right_side):
    return lax.dot_general(
        left_side, right_side, (((1,), (0,)), ((), ())), preferred_element_type=jnp.float32
    )


def columns_of(ref, start, count):
    return ref.at[0, :, pl.ds(pl.multiple_of(start * BS, BS), count * BS)]


def blocks_at(block, count=1):
    return pl.ds(pl.multiple_of(block * BS, BS), count * BS)


class Sides:
    def __init__(self, inner, panel):
        odd = lax.rem(lax.axis_index("blk"), 2)
        self.panel = panel
        self.first = lax.axis_index("layer") * (inner // BS)
        self.ext_side, self.int_side = odd * (2 * panel), (1 - odd) * (2 * panel)
        self.ext_rows = odd * panel
        self.columns = {"ext": self.ext_side, "own": panel, "int": self.int_side}


class Coded:
    def __init__(self, refs):
        self.refs = refs
        self.heads = [jnp.zeros((HEAD, ref.shape[1]), jnp.float32) for ref in refs]

    def write_all(self, product, place):
        for i in range(product.shape[0] // BS):
            self.write(product[i * BS : (i + 1) * BS], place + i)

    def write(self, product, place):
        column = 0
        for c, ref in enumerate(self.refs):
            chunk = product[:, column : column + ref.shape[1]]
            column += ref.shape[1]
            power = powers(chunk)
            ref[HEAD + place * BS : HEAD + (place + 1) * BS, :] = code(chunk, power)
            line = lax.broadcasted_iota(jnp.int32, self.heads[c].shape, 0)
            self.heads[c] = jnp.where(line == place, power, self.heads[c])

    def finish(self):
        for ref, head in zip(self.refs, self.heads):
            ref[0:HEAD, :] = head.astype(jnp.int32).astype(jnp.int16)


def first_kernel(a_hbm, b_hbm, flow_hbm, graph_hbm, *rest):
    out_refs, (rows_ref, graph_buf, flow_buf, total, a_ref, b_ref, sems) = rest[:-7], rest[-7:]
    inner, panel = flow_buf.shape[0], flow_buf.shape[1] // BS // 2
    at = Sides(inner, panel)
    steps = inner // BS
    small = [pltpu.make_async_copy(a_hbm, a_ref, sems.at[0]), pltpu.make_async_copy(b_hbm, b_ref, sems.at[1])]
    flows, graphs = [], []
    for t in range(steps):
        rows = slice(t * BS, (t + 1) * BS)
        flow = columns_of(flow_hbm, at.ext_rows, 2 * panel).at[rows]
        graph = columns_of(graph_hbm, at.ext_side, 1).at[rows]
        flows.append(pltpu.make_async_copy(flow, flow_buf.at[rows], sems.at[2 + 2 * t]))
        graphs.append(pltpu.make_async_copy(graph, graph_buf.at[rows], sems.at[3 + 2 * t]))
    for copy in small:
        copy.start()
    for t in range(steps):
        flows[t].start()
        graphs[t].start()
    for copy in small:
        copy.wait()
    per_dot = min(2, steps)
    for t in range(0, steps, per_dot):
        rows = slice(t * BS, (t + per_dot) * BS)
        for copy in flows[t : t + per_dot] + graphs[t : t + per_dot]:
            copy.wait()
        turned = masked(flow_buf[rows, :], a_ref, at.ext_rows, at.first + t).T
        rows_ref[:, rows] = turned
        product = dot(turned, masked(graph_buf[rows, :], b_ref, at.ext_side, at.first + t))
        if t + per_dot < steps:
            total[...] = product if t == 0 else total[...] + product
    if steps > per_dot:
        total[...] += product
    else:
        total[...] = product
    coded = Coded(out_refs)
    for place, first in ((0, panel), (panel, at.ext_side)):
        for i in range(panel):
            coded.write(total[blocks_at(first - at.ext_rows + i), :], place + i)
    coded.finish()


def first_products(flow_t, graph, a_lines, b_lines, widths):
    inner, width = flow_t.shape[1:]
    panel = width // 3
    return call(
        first_kernel,
        "first_products",
        [pltpu.with_memory_space_constraint(x, pltpu.HBM) for x in (a_lines, b_lines, flow_t, graph)],
        [IN_HBM] * 4,
        [jax.ShapeDtypeStruct((HEAD + 2 * panel, w), jnp.int16) for w in widths]
        + [pltpu.VMEM((2 * panel, inner), flow_t.dtype)],
        [
            pltpu.VMEM((inner, BS), graph.dtype),
            pltpu.VMEM((inner, 2 * panel), flow_t.dtype),
            pltpu.VMEM((2 * panel, BS), jnp.float32),
            pltpu.SMEM(a_lines.shape, a_lines.dtype),
            pltpu.SMEM(b_lines.shape, b_lines.dtype),
            pltpu.SemaphoreType.DMA((2 + 2 * (inner // BS),)),
        ],
        limit=PRODUCT_LIMIT,
    )


def product_kernel(half, wanted, turns, a_ref, b_ref, graph_ref, ext_rows_ref, side_ref, *rest):
    refs = list(rest)
    inner, panel = graph_ref.shape[1], graph_ref.shape[2] // BS // 3
    at = Sides(inner, panel)
    parts = [part for part in ("ext", "own", "int") if part in wanted]
    outs = {part: [refs.pop(0) for _ in wanted[part]] for part in parts}
    int_rows_ref = side_ref
    if turns:
        int_rows_ref = refs.pop(0)
        int_rows_ref[...] = masked(side_ref[0, :, blocks_at(at.int_side, panel)], a_ref, at.int_side, at.first).T
    coded = {part: Coded(outs[part]) for part in parts if part != "own"}
    right = []
    for part in parts:
        column = at.columns[part] + half
        right.append(masked(graph_ref[0, :, blocks_at(column)], b_ref, column, at.first))
    right = jnp.concatenate(right, axis=1) if len(right) > 1 else right[0]
    panels = (
        (panel, ext_rows_ref.at[blocks_at(panel - at.ext_rows, panel)], {"ext": 0, "own": 0, "int": 0}),
        (at.ext_side, ext_rows_ref.at[blocks_at(at.ext_side - at.ext_rows, panel)], {"ext": panel, "own": 0}),
        (at.int_side, int_rows_ref, {"own": 0, "int": panel}),
    )
    for first, source, takers in panels:
        used = [part for part in parts if part in takers]
        if not used:
            continue
        low = parts.index(used[0]) * BS
        for i in range(panel):
            product = dot(source[i * BS : (i + 1) * BS, :], right[:, low : low + len(used) * BS])
            for j, part in enumerate(used):
                piece = product[:, j * BS : (j + 1) * BS]
                if part == "own":
                    outs[part][0][blocks_at(first + i), :] = piece
                else:
                    coded[part].write(piece, takers[part] + i)
    for part in coded:
        coded[part].finish()


def products(a_lines, b_lines, graph, ext_rows, side, half, wanted, turns=False):
    inner, width = graph.shape[1:]
    panel = width // 3
    outs = []
    for part in ("ext", "own", "int"):
        for w in wanted.get(part, ()):
            if part == "own":
                outs.append(jax.ShapeDtypeStruct((width, w), jnp.float32))
            else:
                outs.append(jax.ShapeDtypeStruct((HEAD + 2 * panel, w), jnp.int16))
    if turns:
        outs.append(pltpu.VMEM((panel, inner), graph.dtype))
    return call(
        functools.partial(product_kernel, half, wanted, turns),
        "_".join(wanted) + f"_products_{half}",
        (a_lines, b_lines, graph, ext_rows, side),
        [IN_SMEM, IN_SMEM] + [IN_VMEM] * 3,
        outs,
        limit=PRODUCT_LIMIT,
    )


def send_strip(send_ref, strips, power):
    rows = strips[0].shape[0]
    for j, strip in enumerate(strips):
        send_ref[HEAD + j * rows : HEAD + (j + 1) * rows, :] = code(strip, power)
    send_ref[0:HEAD, :] = jnp.broadcast_to(power, (HEAD, power.shape[1])).astype(jnp.int32).astype(jnp.int16)


def split_strips(total, rows, position, keep_ref, send_refs):
    layer = lax.axis_index("layer")
    if len(send_refs) > 1:
        keep_ref[0] = total[pl.ds(layer * rows, rows), :]
        for other, send_ref in enumerate(send_refs, 1):
            strip = total[pl.ds((layer ^ other) * rows, rows), :]
            send_strip(send_ref, [strip], powers(strip))
        return
    bit = lax.rem(layer // position, 2)
    pairs = keep_ref.shape[0]
    for j in range(pairs):
        keep_ref[j] = total[pl.ds((2 * j + bit) * rows, rows), :]
    away = [total[pl.ds((2 * j + 1 - bit) * rows, rows), :] for j in range(pairs)]
    send_strip(send_refs[0], away, functools.reduce(jnp.maximum, [powers(strip) for strip in away]))


def join_kernel(rows, half, lane, c_ref, own_ref, ext_ref, int_ref, keep_ref, *rest):
    *send_refs, total = rest
    odd = lax.rem(lax.axis_index("blk"), 2)
    panel = own_ref.shape[0] // BS // 3
    lanes = slice(lane, lane + ext_ref.shape[1])
    refs = (ext_ref, int_ref)
    from_mid, from_side = ([[(r, start + i) for i in range(panel)] for r in range(2)] for start in (0, panel))
    middle = [list(both) for both in zip(from_side[0], from_side[1])]
    ext_only, int_only = ([[part] for part in from_mid[r]] for r in range(2))
    odd_parts = int_only + middle + ext_only
    even_parts = ext_only + middle + int_only

    def add(parts):
        scale = [scales(ref[0:HEAD, :]) for ref in refs]
        for v in range(3 * panel):
            kept = c_ref[0, half, v].astype(jnp.float32)
            block = own_ref[v * BS : (v + 1) * BS, lanes] * kept
            for r, i in parts[v]:
                codes = refs[r][HEAD + i * BS : HEAD + (i + 1) * BS, :]
                block += decode(codes, scale[r][i : i + 1] * kept)
            total[v * BS : (v + 1) * BS, :] = block

    @pl.when(odd == 1)
    def _():
        add(odd_parts)

    @pl.when(odd == 0)
    def _():
        add(even_parts)

    split_strips(total, rows, 1, keep_ref, send_refs)


def strips_shapes(pairs, rows, width, messages=1):
    return [
        jax.ShapeDtypeStruct((pairs, rows, width), jnp.float32),
        *[jax.ShapeDtypeStruct((HEAD + pairs * rows, width), jnp.int16)] * messages,
    ]


def join(own, ext_part, int_part, c_lines, half, lane, layers, direct):
    height = own.shape[0]
    width = int_part.shape[1]
    rows = height // layers
    return call(
        functools.partial(join_kernel, rows, half, lane),
        f"join_{half}_{lane}",
        (c_lines, own, ext_part, int_part),
        [IN_SMEM] + [IN_VMEM] * 3,
        strips_shapes(1, rows, width, layers - 1) if direct else strips_shapes(layers // 2, rows, width),
        [pltpu.VMEM((height, width), jnp.float32)],
    )


def halve_kernel(rows, position, kept_ref, got_ref, keep_ref, send_ref, total):
    scale = scales(got_ref[0:HEAD, :])[0:1]
    for j in range(kept_ref.shape[0]):
        codes = got_ref[HEAD + j * rows : HEAD + (j + 1) * rows, :]
        total[j * rows : (j + 1) * rows, :] = kept_ref[j] + decode(codes, scale)
    split_strips(total, rows, position, keep_ref, [send_ref])


def halve(kept, got, position, chunk):
    strips, rows, width = kept.shape
    return call(
        functools.partial(halve_kernel, rows, position),
        f"halve_{position}_{chunk}",
        (kept, got),
        [IN_VMEM] * 2,
        strips_shapes(strips // 2, rows, width),
        [pltpu.VMEM((strips * rows, width), jnp.float32)],
    )


def square_kernel(messages, kept_ref, *rest):
    got_refs, earlier, (square_ref, sums_ref) = rest[:messages], rest[messages:-2], rest[-2:]
    value = kept_ref[0]
    for ref in got_refs:
        value += decode(ref[HEAD:, :], scales(ref[0:HEAD, :])[0:1])
    square = value * value
    square_ref[...] = square
    sums = jnp.broadcast_to(jnp.sum(square, axis=0, keepdims=True), (8, square.shape[1]))
    sums_ref[...] = jnp.concatenate([ref[...] for ref in earlier] + [sums], axis=1)


def square(kept, got, earlier, chunk):
    _, rows, width = kept.shape
    return call(
        functools.partial(square_kernel, len(got)),
        f"square_{chunk}",
        (kept, *got, *earlier),
        [IN_VMEM] * (1 + len(got) + len(earlier)),
        [
            jax.ShapeDtypeStruct((rows, width), jnp.float32),
            jax.ShapeDtypeStruct((8, width + sum(sums.shape[1] for sums in earlier)), jnp.float32),
        ],
    )


def rescale_kernel(height, count, *refs):
    squares, sums, out_ref = refs[:count], refs[count:-1], refs[-1]
    total = functools.reduce(jnp.add, [ref[0:1, :] for ref in sums])
    divisor = total / height + 1e-6
    column = 0
    for ref in squares:
        columns = slice(column, column + ref.shape[1])
        column += ref.shape[1]
        out_ref[0, :, columns] = ref[...] / divisor[:, columns]


def rescale(squares, sums, height):
    rows = squares[0].shape[0]
    width = sums[0].shape[1]
    return call(
        functools.partial(rescale_kernel, float(height), len(squares)),
        "rescale",
        (*squares, *sums),
        [IN_VMEM] * (len(squares) + len(sums)),
        jax.ShapeDtypeStruct((1, rows, width), jnp.float32),
    )


def shards(flow_t, graph, a_pattern, b_pattern, c_pattern):
    layers = lax.axis_size("layer")
    blks = lax.axis_size("blk")
    width = flow_t.shape[2]
    panel = width // 3
    a_lines = a_pattern.transpose(2, 0, 1)
    b_lines = b_pattern.transpose(2, 0, 1)
    c_lines = c_pattern.transpose(0, 2, 1)

    def other_chip(i):
        return (i + 1 if i % 2 else i - 1) % blks

    def same_chip(i):
        return i ^ 1

    halves = panel // BS
    chunks = panel // LANES
    fine = (LANES,) * (BS // LANES)
    per_half = len(fine)
    ext, ints, owns, latest = [], [], [], []

    def ordered(value):
        return after(value, latest[-1])

    def send_ext(parts):
        ext.extend(swap(part, "blk", other_chip) for part in parts)
        latest.append(parts[0])

    def send_int(parts):
        ints.extend(swap(part, "blk", same_chip) for part in parts)
        latest.append(parts[0])

    *parts, ext_rows = first_products(flow_t, graph, a_lines, b_lines, fine)
    send_ext(parts)
    wanted = {"own": (BS,), "int": fine}
    own, *parts, int_rows = products(a_lines, ordered(b_lines), graph, ext_rows, flow_t, 0, wanted, turns=True)
    owns.append(own)
    send_int(parts)

    def more_products(half):
        wanted = {"ext": fine, "int": fine}
        parts = products(a_lines, ordered(b_lines), graph, ext_rows, int_rows, half, wanted)
        send_ext(parts[:per_half])
        send_int(parts[per_half:])
        owns.extend(products(a_lines, ordered(b_lines), graph, ext_rows, int_rows, half, {"own": (BS,)}))
        latest.append(owns[-1])

    strips, squares, sums = [], [], []

    def add_up(chunk):
        half, lane = divmod(chunk, per_half)
        direct = chunk >= chunks - DIRECT and layers <= 4
        kept, *sends = join(
            owns[half], ext[chunk], ints[chunk], ordered(c_lines), half, lane * LANES, layers, direct
        )
        latest.append(kept)
        strips.append((kept, [swap(send, "layer", lambda i: i ^ other) for other, send in enumerate(sends, 1)]))

    def scatter(chunk):
        kept, got = strips[chunk]
        position = 1
        while kept.shape[0] > 1:
            position *= 2
            kept, send = halve(ordered(kept), got[0], position, chunk)
            latest.append(kept)
            got = [swap(send, "layer", lambda i: i ^ position)]
        strips[chunk] = kept, got

    def finish(chunk):
        kept, got = strips[chunk]
        squared, summed = square(ordered(kept), got, sums if chunk == chunks - 1 else [], chunk)
        latest.append(summed)
        squares.append(squared)
        sums.append(summed)

    for chunk in range(chunks + 1):
        if chunk < chunks:
            add_up(chunk)
        if chunk >= 1:
            scatter(chunk - 1)
        if chunk == 2:
            finish(0)
        if chunk % per_half == 0 and chunk // per_half + 1 < halves:
            more_products(chunk // per_half + 1)
    for chunk in range(1, chunks):
        finish(chunk)

    mine = sums[-1]
    others = [swap(mine, "layer", lambda i: i ^ other) for other in range(1, layers)]
    return rescale(squares, [mine, *others], width)


def solution(mesh):
    placed = (
        P("blk", "layer", None),
        P("blk", "layer", None),
        P("blk", None, None),
        P("blk", None, None),
        P("blk", None, None),
    )
    return jax.shard_map(
        shards, mesh=mesh, in_specs=placed, out_specs=P("blk", "layer", None), check_vma=False
    )
```

```python
import functools

import jax
import jax.numpy as jnp
from jax import lax
from jax.experimental import pallas as pl
from jax.experimental.pallas import tpu as pltpu
from jax.sharding import PartitionSpec as P

BS = 256
LANES = 128
HEAD = 16
STEPS = 256.0
TOP = 65534.0
LN2 = 0.6931471805599453
DIRECT = 0
PRODUCT_LIMIT = 24000000
SMALL_LIMIT = 8 * 1024 * 1024
IN_VMEM = pl.BlockSpec(memory_space=pltpu.VMEM)
IN_HBM = pl.BlockSpec(memory_space=pltpu.HBM)


def swap(block, axis, partner):
    return lax.ppermute(block, axis, [(partner(i), i) for i in range(lax.axis_size(axis))])


def after(value, *others):
    return lax.optimization_barrier((value, *others))[0]


def call(kernel, name, operands, in_specs, out_shape, scratch_shapes=(), limit=SMALL_LIMIT):
    return pl.pallas_call(
        kernel,
        out_shape=out_shape,
        in_specs=in_specs,
        out_specs=jax.tree.map(lambda _: IN_VMEM, out_shape),
        scratch_shapes=list(scratch_shapes),
        compiler_params=pltpu.CompilerParams(vmem_limit_bytes=limit),
        cost_estimate=pl.CostEstimate(flops=1, bytes_accessed=1, transcendentals=0),
        name=name,
    )(*operands)


def powers(values):
    largest = jnp.maximum(jnp.max(values, axis=0, keepdims=True), 1e-3)
    return jnp.floor(jnp.log(largest) * (STEPS / LN2)) + 2.0


def code(values, power):
    scaled = values * (TOP * jnp.exp(power * (-LN2 / STEPS)))
    return ((scaled + 0.5).astype(jnp.int32) - 32767).astype(jnp.int16)


def scales(head):
    return jnp.exp(head.astype(jnp.int32).astype(jnp.float32) * (LN2 / STEPS)) * (1.0 / TOP)


def decode(codes, scale):
    return (codes.astype(jnp.int32) + 32767).astype(jnp.float32) * scale


def factor_rows(pattern, column, first, ref):
    place = lax.broadcasted_iota(jnp.int32, (1, ref.shape[1]), 1) // BS
    for u in range(ref.shape[0]):
        row = jnp.zeros((1, ref.shape[1]), jnp.float32)
        for v in range(ref.shape[1] // BS):
            row = jnp.where(place == v, pattern(column + v, first + u).astype(jnp.float32), row)
        ref[u : u + 1, :] = row


def masked(values, factors):
    parts = [
        values[u * BS : (u + 1) * BS] * factors[u : u + 1].astype(values.dtype) for u in range(values.shape[0] // BS)
    ]
    return jnp.concatenate(parts, axis=0) if len(parts) > 1 else parts[0]


def dot(left_side, right_side):
    return lax.dot_general(
        left_side, right_side, (((1,), (0,)), ((), ())), preferred_element_type=jnp.float32
    )


def columns_of(ref, start, count):
    return ref.at[0, :, pl.ds(pl.multiple_of(start * BS, BS), count * BS)]


def blocks_at(block, count=1):
    return pl.ds(pl.multiple_of(block * BS, BS), count * BS)


class Sides:
    def __init__(self, inner, panel):
        odd = lax.rem(lax.axis_index("blk"), 2)
        self.panel = panel
        self.first = lax.axis_index("layer") * (inner // BS)
        self.ext_side, self.int_side = odd * (2 * panel), (1 - odd) * (2 * panel)
        self.ext_rows = odd * panel
        self.columns = {"ext": self.ext_side, "own": panel, "int": self.int_side}


class Coded:
    def __init__(self, refs):
        self.refs = refs
        self.heads = [jnp.zeros((HEAD, ref.shape[1]), jnp.float32) for ref in refs]

    def write_all(self, product, place):
        for i in range(product.shape[0] // BS):
            self.write(product[i * BS : (i + 1) * BS], place + i)

    def write(self, product, place):
        column = 0
        for c, ref in enumerate(self.refs):
            chunk = product[:, column : column + ref.shape[1]]
            column += ref.shape[1]
            power = powers(chunk)
            ref[HEAD + place * BS : HEAD + (place + 1) * BS, :] = code(chunk, power)
            line = lax.broadcasted_iota(jnp.int32, self.heads[c].shape, 0)
            self.heads[c] = jnp.where(line == place, power, self.heads[c])

    def finish(self):
        for ref, head in zip(self.refs, self.heads):
            ref[0:HEAD, :] = head.astype(jnp.int32).astype(jnp.int16)


def first_kernel(a_hbm, b_hbm, c_hbm, flow_hbm, graph_hbm, *rest):
    out_refs, rest = rest[:-12], rest[-12:]
    rows_ref, a_rows_ref, b_rows_ref, c_rows_ref, graph_buf, flow_buf, total, ext_factors, a_ref, b_ref, c_ref, sems = rest
    inner, panel = flow_buf.shape[0], flow_buf.shape[1] // BS // 2
    at = Sides(inner, panel)
    steps = inner // BS
    small = [
        pltpu.make_async_copy(pattern, ref, sems.at[i])
        for i, (pattern, ref) in enumerate(((a_hbm, a_ref), (b_hbm, b_ref), (c_hbm, c_ref)))
    ]
    flows, graphs = [], []
    for t in range(steps):
        rows = slice(t * BS, (t + 1) * BS)
        flow = columns_of(flow_hbm, at.ext_rows, 2 * panel).at[rows]
        graph = columns_of(graph_hbm, at.ext_side, 1).at[rows]
        flows.append(pltpu.make_async_copy(flow, flow_buf.at[rows], sems.at[3 + 2 * t]))
        graphs.append(pltpu.make_async_copy(graph, graph_buf.at[rows], sems.at[4 + 2 * t]))
    for copy in small:
        copy.start()
    for t in range(steps):
        flows[t].start()
        graphs[t].start()
    for copy in small:
        copy.wait()
    factor_rows(lambda column, inner: a_ref[column, 0, inner], 0, at.first, a_rows_ref)
    factor_rows(lambda column, inner: b_ref[column, 0, inner], 0, at.first, b_rows_ref)
    factor_rows(lambda column, row: c_ref[0, column, row], 0, 0, c_rows_ref)
    ext_factors[...] = a_rows_ref[:, blocks_at(at.ext_rows, 2 * panel)]
    right_factors = b_rows_ref[:, blocks_at(at.ext_side)]
    per_dot = min(2, steps)
    for t in range(0, steps, per_dot):
        rows = slice(t * BS, (t + per_dot) * BS)
        for copy in flows[t : t + per_dot] + graphs[t : t + per_dot]:
            copy.wait()
        turned = masked(flow_buf[rows, :], ext_factors[t : t + per_dot]).T
        rows_ref[:, rows] = turned
        product = dot(turned, masked(graph_buf[rows, :], right_factors[t : t + per_dot]))
        if t + per_dot < steps:
            total[...] = product if t == 0 else total[...] + product
    if steps > per_dot:
        total[...] += product
    else:
        total[...] = product
    coded = Coded(out_refs)
    for place, first in ((0, panel), (panel, at.ext_side)):
        for i in range(panel):
            coded.write(total[blocks_at(first - at.ext_rows + i), :], place + i)
    coded.finish()


def first_products(flow_t, graph, a_lines, b_lines, c_lines, widths):
    inner, width = flow_t.shape[1:]
    panel = width // 3
    return call(
        first_kernel,
        "first_products",
        [pltpu.with_memory_space_constraint(x, pltpu.HBM) for x in (a_lines, b_lines, c_lines, flow_t, graph)],
        [IN_HBM] * 5,
        [jax.ShapeDtypeStruct((HEAD + 2 * panel, w), jnp.int16) for w in widths]
        + [
            pltpu.VMEM((2 * panel, inner), flow_t.dtype),
            pltpu.VMEM((inner // BS, width), jnp.float32),
            pltpu.VMEM((inner // BS, width), jnp.float32),
            pltpu.VMEM((width // BS, panel), jnp.float32),
        ],
        [
            pltpu.VMEM((inner, BS), graph.dtype),
            pltpu.VMEM((inner, 2 * panel), flow_t.dtype),
            pltpu.VMEM((2 * panel, BS), jnp.float32),
            pltpu.VMEM((inner // BS, 2 * panel), jnp.float32),
            pltpu.SMEM(a_lines.shape, a_lines.dtype),
            pltpu.SMEM(b_lines.shape, b_lines.dtype),
            pltpu.SMEM(c_lines.shape, c_lines.dtype),
            pltpu.SemaphoreType.DMA((3 + 2 * (inner // BS),)),
        ],
        limit=PRODUCT_LIMIT,
    )


def product_kernel(half, wanted, turns, a_rows_ref, b_rows_ref, graph_ref, ext_rows_ref, side_ref, *rest):
    refs = list(rest)
    inner, panel = graph_ref.shape[1], graph_ref.shape[2] // BS // 3
    at = Sides(inner, panel)
    parts = [part for part in ("ext", "own", "int") if part in wanted]
    outs = {part: [refs.pop(0) for _ in wanted[part]] for part in parts}
    int_rows_ref = side_ref
    if turns:
        int_rows_ref = refs.pop(0)
        place = blocks_at(at.int_side, panel)
        int_rows_ref[...] = masked(side_ref[0, :, place], a_rows_ref[:, place]).T
    coded = {part: Coded(outs[part]) for part in parts if part != "own"}
    right = []
    for part in parts:
        place = blocks_at(at.columns[part] + half)
        right.append(masked(graph_ref[0, :, place], b_rows_ref[:, place]))
    right = jnp.concatenate(right, axis=1) if len(right) > 1 else right[0]
    panels = (
        (panel, ext_rows_ref.at[blocks_at(panel - at.ext_rows, panel)], {"ext": 0, "own": 0, "int": 0}),
        (at.ext_side, ext_rows_ref.at[blocks_at(at.ext_side - at.ext_rows, panel)], {"ext": panel, "own": 0}),
        (at.int_side, int_rows_ref, {"own": 0, "int": panel}),
    )
    for first, source, takers in panels:
        used = [part for part in parts if part in takers]
        if not used:
            continue
        low = parts.index(used[0]) * BS
        for i in range(panel):
            product = dot(source[i * BS : (i + 1) * BS, :], right[:, low : low + len(used) * BS])
            for j, part in enumerate(used):
                piece = product[:, j * BS : (j + 1) * BS]
                if part == "own":
                    outs[part][0][blocks_at(first + i), :] = piece
                else:
                    coded[part].write(piece, takers[part] + i)
    for part in coded:
        coded[part].finish()


def products(a_rows, b_rows, graph, ext_rows, side, half, wanted, turns=False):
    inner, width = graph.shape[1:]
    panel = width // 3
    outs = []
    for part in ("ext", "own", "int"):
        for w in wanted.get(part, ()):
            if part == "own":
                outs.append(jax.ShapeDtypeStruct((width, w), jnp.float32))
            else:
                outs.append(jax.ShapeDtypeStruct((HEAD + 2 * panel, w), jnp.int16))
    if turns:
        outs.append(pltpu.VMEM((panel, inner), graph.dtype))
    return call(
        functools.partial(product_kernel, half, wanted, turns),
        "_".join(wanted) + f"_products_{half}",
        (a_rows, b_rows, graph, ext_rows, side),
        [IN_VMEM] * 5,
        outs,
        limit=PRODUCT_LIMIT,
    )


def send_strip(send_ref, strips, power):
    rows = strips[0].shape[0]
    for j, strip in enumerate(strips):
        send_ref[HEAD + j * rows : HEAD + (j + 1) * rows, :] = code(strip, power)
    send_ref[0:HEAD, :] = jnp.broadcast_to(power, (HEAD, power.shape[1])).astype(jnp.int32).astype(jnp.int16)


def split_strips(total, rows, position, keep_ref, send_refs):
    layer = lax.axis_index("layer")
    if len(send_refs) > 1:
        keep_ref[0] = total[pl.ds(layer * rows, rows), :]
        for other, send_ref in enumerate(send_refs, 1):
            strip = total[pl.ds((layer ^ other) * rows, rows), :]
            send_strip(send_ref, [strip], powers(strip))
        return
    bit = lax.rem(layer // position, 2)
    pairs = keep_ref.shape[0]
    for j in range(pairs):
        keep_ref[j] = total[pl.ds((2 * j + bit) * rows, rows), :]
    away = [total[pl.ds((2 * j + 1 - bit) * rows, rows), :] for j in range(pairs)]
    send_strip(send_refs[0], away, functools.reduce(jnp.maximum, [powers(strip) for strip in away]))


def join_kernel(rows, half, lane, c_ref, own_ref, ext_ref, int_ref, keep_ref, *rest):
    *send_refs, total = rest
    odd = lax.rem(lax.axis_index("blk"), 2)
    panel = own_ref.shape[0] // BS // 3
    lanes = slice(lane, lane + ext_ref.shape[1])
    refs = (ext_ref, int_ref)
    from_mid, from_side = ([[(r, start + i) for i in range(panel)] for r in range(2)] for start in (0, panel))
    middle = [list(both) for both in zip(from_side[0], from_side[1])]
    ext_only, int_only = ([[part] for part in from_mid[r]] for r in range(2))
    odd_parts = int_only + middle + ext_only
    even_parts = ext_only + middle + int_only

    def add(parts):
        scale = [scales(ref[0:HEAD, :]) for ref in refs]
        for v in range(3 * panel):
            kept = c_ref[v : v + 1, half * BS + lane : half * BS + lane + ext_ref.shape[1]]
            block = own_ref[v * BS : (v + 1) * BS, lanes] * kept
            for r, i in parts[v]:
                codes = refs[r][HEAD + i * BS : HEAD + (i + 1) * BS, :]
                block += decode(codes, scale[r][i : i + 1] * kept)
            total[v * BS : (v + 1) * BS, :] = block

    @pl.when(odd == 1)
    def _():
        add(odd_parts)

    @pl.when(odd == 0)
    def _():
        add(even_parts)

    split_strips(total, rows, 1, keep_ref, send_refs)


def strips_shapes(pairs, rows, width, messages=1):
    return [
        jax.ShapeDtypeStruct((pairs, rows, width), jnp.float32),
        *[jax.ShapeDtypeStruct((HEAD + pairs * rows, width), jnp.int16)] * messages,
    ]


def join(own, ext_part, int_part, c_rows, half, lane, layers, direct):
    height = own.shape[0]
    width = int_part.shape[1]
    rows = height // layers
    return call(
        functools.partial(join_kernel, rows, half, lane),
        f"join_{half}_{lane}",
        (c_rows, own, ext_part, int_part),
        [IN_VMEM] * 4,
        strips_shapes(1, rows, width, layers - 1) if direct else strips_shapes(layers // 2, rows, width),
        [pltpu.VMEM((height, width), jnp.float32)],
    )


def halve_kernel(rows, position, kept_ref, got_ref, keep_ref, send_ref, total):
    scale = scales(got_ref[0:HEAD, :])[0:1]
    for j in range(kept_ref.shape[0]):
        codes = got_ref[HEAD + j * rows : HEAD + (j + 1) * rows, :]
        total[j * rows : (j + 1) * rows, :] = kept_ref[j] + decode(codes, scale)
    split_strips(total, rows, position, keep_ref, [send_ref])


def halve(kept, got, position, chunk):
    strips, rows, width = kept.shape
    return call(
        functools.partial(halve_kernel, rows, position),
        f"halve_{position}_{chunk}",
        (kept, got),
        [IN_VMEM] * 2,
        strips_shapes(strips // 2, rows, width),
        [pltpu.VMEM((strips * rows, width), jnp.float32)],
    )


def square_kernel(messages, kept_ref, *rest):
    got_refs, earlier, (square_ref, sums_ref) = rest[:messages], rest[messages:-2], rest[-2:]
    value = kept_ref[0]
    for ref in got_refs:
        value += decode(ref[HEAD:, :], scales(ref[0:HEAD, :])[0:1])
    square = value * value
    square_ref[...] = square
    sums = jnp.broadcast_to(jnp.sum(square, axis=0, keepdims=True), (8, square.shape[1]))
    sums_ref[...] = jnp.concatenate([ref[...] for ref in earlier] + [sums], axis=1)


def square(kept, got, earlier, chunk):
    _, rows, width = kept.shape
    return call(
        functools.partial(square_kernel, len(got)),
        f"square_{chunk}",
        (kept, *got, *earlier),
        [IN_VMEM] * (1 + len(got) + len(earlier)),
        [
            jax.ShapeDtypeStruct((rows, width), jnp.float32),
            jax.ShapeDtypeStruct((8, width + sum(sums.shape[1] for sums in earlier)), jnp.float32),
        ],
    )


def rescale_kernel(height, count, *refs):
    squares, sums, out_ref = refs[:count], refs[count:-1], refs[-1]
    total = functools.reduce(jnp.add, [ref[0:1, :] for ref in sums])
    divisor = total / height + 1e-6
    column = 0
    for ref in squares:
        columns = slice(column, column + ref.shape[1])
        column += ref.shape[1]
        out_ref[0, :, columns] = ref[...] / divisor[:, columns]


def rescale(squares, sums, height):
    rows = squares[0].shape[0]
    width = sums[0].shape[1]
    return call(
        functools.partial(rescale_kernel, float(height), len(squares)),
        "rescale",
        (*squares, *sums),
        [IN_VMEM] * (len(squares) + len(sums)),
        jax.ShapeDtypeStruct((1, rows, width), jnp.float32),
    )


def shards(flow_t, graph, a_pattern, b_pattern, c_pattern):
    layers = lax.axis_size("layer")
    blks = lax.axis_size("blk")
    width = flow_t.shape[2]
    panel = width // 3
    a_lines = a_pattern.transpose(2, 0, 1)
    b_lines = b_pattern.transpose(2, 0, 1)
    c_lines = c_pattern.transpose(0, 2, 1)

    def other_chip(i):
        return (i + 1 if i % 2 else i - 1) % blks

    def same_chip(i):
        return i ^ 1

    halves = panel // BS
    chunks = panel // LANES
    fine = (LANES,) * (BS // LANES)
    per_half = len(fine)
    ext, ints, owns, latest = [], [], [], []

    def ordered(value):
        return after(value, latest[-1])

    def send_ext(parts):
        ext.extend(swap(part, "blk", other_chip) for part in parts)
        latest.append(parts[0])

    def send_int(parts):
        ints.extend(swap(part, "blk", same_chip) for part in parts)
        latest.append(parts[0])

    *parts, ext_rows, a_rows, b_rows, c_rows = first_products(flow_t, graph, a_lines, b_lines, c_lines, fine)
    send_ext(parts)
    wanted = {"own": (BS,), "int": fine}
    own, *parts, int_rows = products(a_rows, ordered(b_rows), graph, ext_rows, flow_t, 0, wanted, turns=True)
    owns.append(own)
    send_int(parts)

    def more_products(half):
        wanted = {"ext": fine, "int": fine}
        parts = products(a_rows, ordered(b_rows), graph, ext_rows, int_rows, half, wanted)
        send_ext(parts[:per_half])
        send_int(parts[per_half:])

    def more_own(half):
        owns.extend(products(a_rows, ordered(b_rows), graph, ext_rows, int_rows, half, {"own": (BS,)}))
        latest.append(owns[-1])

    strips, squares, sums = [], [], []

    def add_up(chunk):
        half, lane = divmod(chunk, per_half)
        direct = chunk >= chunks - DIRECT and layers <= 4
        kept, *sends = join(
            owns[half], ext[chunk], ints[chunk], ordered(c_rows), half, lane * LANES, layers, direct
        )
        latest.append(kept)
        strips.append((kept, [swap(send, "layer", lambda i: i ^ other) for other, send in enumerate(sends, 1)]))

    def scatter(chunk):
        kept, got = strips[chunk]
        position = 1
        while kept.shape[0] > 1:
            position *= 2
            kept, send = halve(ordered(kept), got[0], position, chunk)
            latest.append(kept)
            got = [swap(send, "layer", lambda i: i ^ position)]
        strips[chunk] = kept, got

    def finish(chunk):
        kept, got = strips[chunk]
        squared, summed = square(ordered(kept), got, sums if chunk == chunks - 1 else [], chunk)
        latest.append(summed)
        squares.append(squared)
        sums.append(summed)

    for chunk in range(chunks + 1):
        if chunk < chunks:
            add_up(chunk)
        if (chunk + 1) % per_half == 0 and len(owns) < halves:
            more_own(len(owns))
        if chunk >= 1:
            scatter(chunk - 1)
        if chunk == 2:
            finish(0)
        if chunk % per_half == 0 and chunk // per_half + 1 < halves:
            more_products(chunk // per_half + 1)
    for chunk in range(1, chunks):
        finish(chunk)

    mine = sums[-1]
    others = [swap(mine, "layer", lambda i: i ^ other) for other in range(1, layers)]
    return rescale(squares, [mine, *others], width)


def solution(mesh):
    placed = (
        P("blk", "layer", None),
        P("blk", "layer", None),
        P("blk", None, None),
        P("blk", None, None),
        P("blk", None, None),
    )
    return jax.shard_map(
        shards, mesh=mesh, in_specs=placed, out_specs=P("blk", "layer", None), check_vma=False
    )
```

```python
import functools

import jax
import jax.numpy as jnp
from jax import lax
from jax.experimental import pallas as pl
from jax.experimental.pallas import tpu as pltpu
from jax.sharding import PartitionSpec as P

BS = 256
LANES = 128
HEAD = 16
STEPS = 256.0
TOP = 65534.0
LN2 = 0.6931471805599453
DIRECT = 0
PRODUCT_LIMIT = 24000000
SMALL_LIMIT = 8 * 1024 * 1024
IN_VMEM = pl.BlockSpec(memory_space=pltpu.VMEM)
IN_HBM = pl.BlockSpec(memory_space=pltpu.HBM)


def swap(block, axis, partner):
    return lax.ppermute(block, axis, [(partner(i), i) for i in range(lax.axis_size(axis))])


def after(value, *others):
    return lax.optimization_barrier((value, *others))[0]


def call(kernel, name, operands, in_specs, out_shape, scratch_shapes=(), limit=SMALL_LIMIT):
    return pl.pallas_call(
        kernel,
        out_shape=out_shape,
        in_specs=in_specs,
        out_specs=jax.tree.map(lambda _: IN_VMEM, out_shape),
        scratch_shapes=list(scratch_shapes),
        compiler_params=pltpu.CompilerParams(vmem_limit_bytes=limit),
        cost_estimate=pl.CostEstimate(flops=1, bytes_accessed=1, transcendentals=0),
        name=name,
    )(*operands)


def powers(values):
    largest = jnp.maximum(jnp.max(values, axis=0, keepdims=True), 1e-3)
    return jnp.floor(jnp.log(largest) * (STEPS / LN2)) + 2.0


def code(values, power):
    scaled = values * (TOP * jnp.exp(power * (-LN2 / STEPS)))
    return ((scaled + 0.5).astype(jnp.int32) - 32767).astype(jnp.int16)


def scales(head):
    return jnp.exp(head.astype(jnp.int32).astype(jnp.float32) * (LN2 / STEPS)) * (1.0 / TOP)


def decode(codes, scale):
    return (codes.astype(jnp.int32) + 32767).astype(jnp.float32) * scale


def factor_rows(pattern, column, first, ref):
    place = lax.broadcasted_iota(jnp.int32, (1, ref.shape[1]), 1) // BS
    for u in range(ref.shape[0]):
        row = jnp.zeros((1, ref.shape[1]), jnp.float32)
        for v in range(ref.shape[1] // BS):
            row = jnp.where(place == v, pattern(column + v, first + u).astype(jnp.float32), row)
        ref[u : u + 1, :] = row


def masked(values, factors):
    parts = [
        values[u * BS : (u + 1) * BS] * factors[u : u + 1].astype(values.dtype) for u in range(values.shape[0] // BS)
    ]
    return jnp.concatenate(parts, axis=0) if len(parts) > 1 else parts[0]


def dot(left_side, right_side):
    return lax.dot_general(
        left_side, right_side, (((1,), (0,)), ((), ())), preferred_element_type=jnp.float32
    )


def columns_of(ref, start, count):
    return ref.at[0, :, pl.ds(pl.multiple_of(start * BS, BS), count * BS)]


def blocks_at(block, count=1):
    return pl.ds(pl.multiple_of(block * BS, BS), count * BS)


class Sides:
    def __init__(self, inner, panel):
        odd = lax.rem(lax.axis_index("blk"), 2)
        self.panel = panel
        self.first = lax.axis_index("layer") * (inner // BS)
        self.ext_side, self.int_side = odd * (2 * panel), (1 - odd) * (2 * panel)
        self.ext_rows = odd * panel
        self.columns = {"ext": self.ext_side, "own": panel, "int": self.int_side}


class Coded:
    def __init__(self, refs):
        self.refs = refs
        self.heads = [jnp.zeros((HEAD, ref.shape[1]), jnp.float32) for ref in refs]

    def write_all(self, product, place):
        for i in range(product.shape[0] // BS):
            self.write(product[i * BS : (i + 1) * BS], place + i)

    def write(self, product, place):
        column = 0
        for c, ref in enumerate(self.refs):
            chunk = product[:, column : column + ref.shape[1]]
            column += ref.shape[1]
            power = powers(chunk)
            ref[HEAD + place * BS : HEAD + (place + 1) * BS, :] = code(chunk, power)
            line = lax.broadcasted_iota(jnp.int32, self.heads[c].shape, 0)
            self.heads[c] = jnp.where(line == place, power, self.heads[c])

    def finish(self):
        for ref, head in zip(self.refs, self.heads):
            ref[0:HEAD, :] = head.astype(jnp.int32).astype(jnp.int16)


def first_kernel(a_hbm, b_hbm, c_hbm, flow_hbm, graph_hbm, *rest):
    out_refs, rest = rest[:-12], rest[-12:]
    rows_ref, a_rows_ref, b_rows_ref, c_rows_ref, graph_buf, flow_buf, total, ext_factors, a_ref, b_ref, c_ref, sems = rest
    inner, panel = flow_buf.shape[0], flow_buf.shape[1] // BS // 2
    at = Sides(inner, panel)
    steps = inner // BS
    small = [
        pltpu.make_async_copy(pattern, ref, sems.at[i])
        for i, (pattern, ref) in enumerate(((a_hbm, a_ref), (b_hbm, b_ref), (c_hbm, c_ref)))
    ]
    flows, graphs = [], []
    for t in range(steps):
        rows = slice(t * BS, (t + 1) * BS)
        flow = columns_of(flow_hbm, at.ext_rows, 2 * panel).at[rows]
        graph = columns_of(graph_hbm, at.ext_side, 1).at[rows]
        flows.append(pltpu.make_async_copy(flow, flow_buf.at[rows], sems.at[3 + 2 * t]))
        graphs.append(pltpu.make_async_copy(graph, graph_buf.at[rows], sems.at[4 + 2 * t]))
    for copy in small:
        copy.start()
    for t in range(steps):
        flows[t].start()
        graphs[t].start()
    for copy in small:
        copy.wait()
    factor_rows(lambda column, inner: a_ref[column, 0, inner], 0, at.first, a_rows_ref)
    factor_rows(lambda column, inner: b_ref[column, 0, inner], 0, at.first, b_rows_ref)
    factor_rows(lambda column, row: c_ref[0, column, row], 0, 0, c_rows_ref)
    ext_factors[...] = a_rows_ref[:, blocks_at(at.ext_rows, 2 * panel)]
    right_factors = b_rows_ref[:, blocks_at(at.ext_side)]
    per_dot = min(2, steps)
    for t in range(0, steps, per_dot):
        rows = slice(t * BS, (t + per_dot) * BS)
        for copy in flows[t : t + per_dot] + graphs[t : t + per_dot]:
            copy.wait()
        turned = masked(flow_buf[rows, :], ext_factors[t : t + per_dot]).T
        rows_ref[:, rows] = turned
        product = dot(turned, masked(graph_buf[rows, :], right_factors[t : t + per_dot]))
        if t + per_dot < steps:
            total[...] = product if t == 0 else total[...] + product
    if steps > per_dot:
        total[...] += product
    else:
        total[...] = product
    coded = Coded(out_refs)
    for place, first in ((0, panel), (panel, at.ext_side)):
        for i in range(panel):
            coded.write(total[blocks_at(first - at.ext_rows + i), :], place + i)
    coded.finish()


def first_products(flow_t, graph, a_lines, b_lines, c_lines, widths):
    inner, width = flow_t.shape[1:]
    panel = width // 3
    return call(
        first_kernel,
        "first_products",
        [pltpu.with_memory_space_constraint(x, pltpu.HBM) for x in (a_lines, b_lines, c_lines, flow_t, graph)],
        [IN_HBM] * 5,
        [jax.ShapeDtypeStruct((HEAD + 2 * panel, w), jnp.int16) for w in widths]
        + [
            pltpu.VMEM((2 * panel, inner), flow_t.dtype),
            pltpu.VMEM((inner // BS, width), jnp.float32),
            pltpu.VMEM((inner // BS, width), jnp.float32),
            pltpu.VMEM((width // BS, panel), jnp.float32),
        ],
        [
            pltpu.VMEM((inner, BS), graph.dtype),
            pltpu.VMEM((inner, 2 * panel), flow_t.dtype),
            pltpu.VMEM((2 * panel, BS), jnp.float32),
            pltpu.VMEM((inner // BS, 2 * panel), jnp.float32),
            pltpu.SMEM(a_lines.shape, a_lines.dtype),
            pltpu.SMEM(b_lines.shape, b_lines.dtype),
            pltpu.SMEM(c_lines.shape, c_lines.dtype),
            pltpu.SemaphoreType.DMA((3 + 2 * (inner // BS),)),
        ],
        limit=PRODUCT_LIMIT,
    )


def product_kernel(half, wanted, turns, a_rows_ref, b_rows_ref, graph_ref, ext_rows_ref, side_ref, *rest):
    refs = list(rest)
    inner, panel = graph_ref.shape[1], graph_ref.shape[2] // BS // 3
    at = Sides(inner, panel)
    parts = [part for part in ("ext", "own", "int") if part in wanted]
    outs = {part: [refs.pop(0) for _ in wanted[part]] for part in parts}
    int_rows_ref = side_ref
    if turns:
        int_rows_ref = refs.pop(0)
        place = blocks_at(at.int_side, panel)
        int_rows_ref[...] = masked(side_ref[0, :, place], a_rows_ref[:, place]).T
    coded = {part: Coded(outs[part]) for part in parts if part != "own"}
    right = []
    for part in parts:
        place = blocks_at(at.columns[part] + half)
        right.append(masked(graph_ref[0, :, place], b_rows_ref[:, place]))
    right = jnp.concatenate(right, axis=1) if len(right) > 1 else right[0]
    panels = (
        (panel, ext_rows_ref.at[blocks_at(panel - at.ext_rows, panel)], {"ext": 0, "own": 0, "int": 0}),
        (at.ext_side, ext_rows_ref.at[blocks_at(at.ext_side - at.ext_rows, panel)], {"ext": panel, "own": 0}),
        (at.int_side, int_rows_ref, {"own": 0, "int": panel}),
    )
    for first, source, takers in panels:
        used = [part for part in parts if part in takers]
        if not used:
            continue
        low = parts.index(used[0]) * BS
        for i in range(panel):
            product = dot(source[i * BS : (i + 1) * BS, :], right[:, low : low + len(used) * BS])
            for j, part in enumerate(used):
                piece = product[:, j * BS : (j + 1) * BS]
                if part == "own":
                    outs[part][0][blocks_at(first + i), :] = piece
                else:
                    coded[part].write(piece, takers[part] + i)
    for part in coded:
        coded[part].finish()


def products(a_rows, b_rows, graph, ext_rows, side, half, wanted, turns=False):
    inner, width = graph.shape[1:]
    panel = width // 3
    outs = []
    for part in ("ext", "own", "int"):
        for w in wanted.get(part, ()):
            if part == "own":
                outs.append(jax.ShapeDtypeStruct((width, w), jnp.float32))
            else:
                outs.append(jax.ShapeDtypeStruct((HEAD + 2 * panel, w), jnp.int16))
    if turns:
        outs.append(pltpu.VMEM((panel, inner), graph.dtype))
    return call(
        functools.partial(product_kernel, half, wanted, turns),
        "_".join(wanted) + f"_products_{half}",
        (a_rows, b_rows, graph, ext_rows, side),
        [IN_VMEM] * 5,
        outs,
        limit=PRODUCT_LIMIT,
    )


def send_strip(send_ref, strips, power):
    rows = strips[0].shape[0]
    for j, strip in enumerate(strips):
        send_ref[HEAD + j * rows : HEAD + (j + 1) * rows, :] = code(strip, power)
    send_ref[0:HEAD, :] = jnp.broadcast_to(power, (HEAD, power.shape[1])).astype(jnp.int32).astype(jnp.int16)


def split_strips(total, rows, position, keep_ref, send_refs):
    layer = lax.axis_index("layer")
    if len(send_refs) > 1:
        keep_ref[0] = total[pl.ds(layer * rows, rows), :]
        for other, send_ref in enumerate(send_refs, 1):
            strip = total[pl.ds((layer ^ other) * rows, rows), :]
            send_strip(send_ref, [strip], powers(strip))
        return
    bit = lax.rem(layer // position, 2)
    pairs = keep_ref.shape[0]
    for j in range(pairs):
        keep_ref[j] = total[pl.ds((2 * j + bit) * rows, rows), :]
    away = [total[pl.ds((2 * j + 1 - bit) * rows, rows), :] for j in range(pairs)]
    send_strip(send_refs[0], away, functools.reduce(jnp.maximum, [powers(strip) for strip in away]))


def join_kernel(rows, half, lane, c_ref, own_ref, ext_ref, int_ref, keep_ref, *rest):
    *send_refs, total = rest
    odd = lax.rem(lax.axis_index("blk"), 2)
    panel = own_ref.shape[0] // BS // 3
    lanes = slice(lane, lane + ext_ref.shape[1])
    refs = (ext_ref, int_ref)
    from_mid, from_side = ([[(r, start + i) for i in range(panel)] for r in range(2)] for start in (0, panel))
    middle = [list(both) for both in zip(from_side[0], from_side[1])]
    ext_only, int_only = ([[part] for part in from_mid[r]] for r in range(2))
    odd_parts = int_only + middle + ext_only
    even_parts = ext_only + middle + int_only

    def add(parts):
        scale = [scales(ref[0:HEAD, :]) for ref in refs]
        for v in range(3 * panel):
            kept = c_ref[v : v + 1, half * BS + lane : half * BS + lane + ext_ref.shape[1]]
            block = own_ref[v * BS : (v + 1) * BS, lanes] * kept
            for r, i in parts[v]:
                codes = refs[r][HEAD + i * BS : HEAD + (i + 1) * BS, :]
                block += decode(codes, scale[r][i : i + 1] * kept)
            total[v * BS : (v + 1) * BS, :] = block

    @pl.when(odd == 1)
    def _():
        add(odd_parts)

    @pl.when(odd == 0)
    def _():
        add(even_parts)

    split_strips(total, rows, 1, keep_ref, send_refs)


def strips_shapes(pairs, rows, width, messages=1):
    return [
        jax.ShapeDtypeStruct((pairs, rows, width), jnp.float32),
        *[jax.ShapeDtypeStruct((HEAD + pairs * rows, width), jnp.int16)] * messages,
    ]


def join(own, ext_part, int_part, c_rows, half, lane, layers, direct):
    height = own.shape[0]
    width = int_part.shape[1]
    rows = height // layers
    return call(
        functools.partial(join_kernel, rows, half, lane),
        f"join_{half}_{lane}",
        (c_rows, own, ext_part, int_part),
        [IN_VMEM] * 4,
        strips_shapes(1, rows, width, layers - 1) if direct else strips_shapes(layers // 2, rows, width),
        [pltpu.VMEM((height, width), jnp.float32)],
    )


def halve_kernel(rows, position, kept_ref, got_ref, keep_ref, send_ref, total):
    scale = scales(got_ref[0:HEAD, :])[0:1]
    for j in range(kept_ref.shape[0]):
        codes = got_ref[HEAD + j * rows : HEAD + (j + 1) * rows, :]
        total[j * rows : (j + 1) * rows, :] = kept_ref[j] + decode(codes, scale)
    split_strips(total, rows, position, keep_ref, [send_ref])


def halve(kept, got, position, chunk):
    strips, rows, width = kept.shape
    return call(
        functools.partial(halve_kernel, rows, position),
        f"halve_{position}_{chunk}",
        (kept, got),
        [IN_VMEM] * 2,
        strips_shapes(strips // 2, rows, width),
        [pltpu.VMEM((strips * rows, width), jnp.float32)],
    )


def square_kernel(messages, kept_ref, *rest):
    got_refs, earlier, (square_ref, sums_ref) = rest[:messages], rest[messages:-2], rest[-2:]
    value = kept_ref[0]
    for ref in got_refs:
        value += decode(ref[HEAD:, :], scales(ref[0:HEAD, :])[0:1])
    square = value * value
    square_ref[...] = square
    sums = jnp.broadcast_to(jnp.sum(square, axis=0, keepdims=True), (8, square.shape[1]))
    sums_ref[...] = jnp.concatenate([ref[...] for ref in earlier] + [sums], axis=1)


def square(kept, got, earlier, chunk):
    _, rows, width = kept.shape
    return call(
        functools.partial(square_kernel, len(got)),
        f"square_{chunk}",
        (kept, *got, *earlier),
        [IN_VMEM] * (1 + len(got) + len(earlier)),
        [
            jax.ShapeDtypeStruct((rows, width), jnp.float32),
            jax.ShapeDtypeStruct((8, width + sum(sums.shape[1] for sums in earlier)), jnp.float32),
        ],
    )


def rescale_kernel(height, count, *refs):
    squares, sums, out_ref = refs[:count], refs[count:-1], refs[-1]
    total = functools.reduce(jnp.add, [ref[0:1, :] for ref in sums])
    divisor = total / height + 1e-6
    column = 0
    for ref in squares:
        columns = slice(column, column + ref.shape[1])
        column += ref.shape[1]
        out_ref[0, :, columns] = ref[...] / divisor[:, columns]


def rescale(squares, sums, height):
    rows = squares[0].shape[0]
    width = sums[0].shape[1]
    return call(
        functools.partial(rescale_kernel, float(height), len(squares)),
        "rescale",
        (*squares, *sums),
        [IN_VMEM] * (len(squares) + len(sums)),
        jax.ShapeDtypeStruct((1, rows, width), jnp.float32),
    )


def shards(flow_t, graph, a_pattern, b_pattern, c_pattern):
    layers = lax.axis_size("layer")
    blks = lax.axis_size("blk")
    width = flow_t.shape[2]
    panel = width // 3
    a_lines = a_pattern.transpose(2, 0, 1)
    b_lines = b_pattern.transpose(2, 0, 1)
    c_lines = c_pattern.transpose(0, 2, 1)

    def other_chip(i):
        return (i + 1 if i % 2 else i - 1) % blks

    def same_chip(i):
        return i ^ 1

    halves = panel // BS
    chunks = panel // LANES
    fine = (LANES,) * (BS // LANES)
    per_half = len(fine)
    ext, ints, owns, latest = [], [], [], []

    def ordered(value):
        return after(value, latest[-1])

    def send_ext(parts):
        ext.extend(swap(part, "blk", other_chip) for part in parts)

    def send_int(parts):
        ints.extend(swap(part, "blk", same_chip) for part in parts)

    *parts, ext_rows, a_rows, b_rows, c_rows = first_products(flow_t, graph, a_lines, b_lines, c_lines, fine)
    send_ext(parts)
    latest.append(parts[0])
    wanted = {"own": (BS,), "int": fine}
    own, *parts, int_rows = products(a_rows, ordered(b_rows), graph, ext_rows, flow_t, 0, wanted, turns=True)
    owns.append(own)
    send_int(parts)
    latest.append(own)

    def more_products(half):
        wanted = {"ext": fine, "int": fine}
        parts = products(a_rows, ordered(b_rows), graph, ext_rows, int_rows, half, wanted)
        send_ext(parts[:1])
        send_int(parts[per_half : per_half + 1])
        latest.append(parts[0])
        return parts[1:per_half], parts[per_half + 1 :]

    def more_own(half):
        owns.extend(products(a_rows, ordered(b_rows), graph, ext_rows, int_rows, half, {"own": (BS,)}))
        latest.append(owns[-1])

    strips, squares, sums = [], [], []

    def add_up(chunk):
        half, lane = divmod(chunk, per_half)
        direct = chunk >= chunks - DIRECT and layers <= 4
        kept, *sends = join(
            owns[half], ext[chunk], ints[chunk], ordered(c_rows), half, lane * LANES, layers, direct
        )
        latest.append(kept)
        strips.append((kept, [swap(send, "layer", lambda i: i ^ other) for other, send in enumerate(sends, 1)]))

    def scatter(chunk):
        kept, got = strips[chunk]
        position = 1
        while kept.shape[0] > 1:
            position *= 2
            kept, send = halve(ordered(kept), got[0], position, chunk)
            latest.append(kept)
            got = [swap(send, "layer", lambda i: i ^ position)]
        strips[chunk] = kept, got

    def finish(chunk):
        kept, got = strips[chunk]
        squared, summed = square(ordered(kept), got, sums if chunk == chunks - 1 else [], chunk)
        latest.append(summed)
        squares.append(squared)
        sums.append(summed)

    for half in range(halves):
        first = half * per_half
        add_up(first)
        if half > 0:
            scatter(first - 1)
        if half + 1 < halves:
            ext_parts, int_parts = more_products(half + 1)
        for chunk in range(first + 1, first + per_half):
            if chunk == chunks - 1:
                finish(0)
            add_up(chunk)
            scatter(chunk - 1)
        if half + 1 < halves:
            before = latest[-1]
            send_ext(after(part, before) for part in ext_parts)
            send_int(after(part, before) for part in int_parts)
            more_own(half + 1)
    scatter(chunks - 1)
    for chunk in range(1, chunks):
        finish(chunk)

    mine = sums[-1]
    others = [swap(mine, "layer", lambda i: i ^ other) for other in range(1, layers)]
    return rescale(squares, [mine, *others], width)


def solution(mesh):
    placed = (
        P("blk", "layer", None),
        P("blk", "layer", None),
        P("blk", None, None),
        P("blk", None, None),
        P("blk", None, None),
    )
    return jax.shard_map(
        shards, mesh=mesh, in_specs=placed, out_specs=P("blk", "layer", None), check_vma=False
    )
```

```python
import functools

import jax
import jax.numpy as jnp
from jax import lax
from jax.experimental import pallas as pl
from jax.experimental.pallas import tpu as pltpu
from jax.sharding import PartitionSpec as P

BS = 256
LANES = 128
HEAD = 16
STEPS = 256.0
TOP = 65534.0
LN2 = 0.6931471805599453
PRODUCT_LIMIT = 24000000
SMALL_LIMIT = 8 * 1024 * 1024
IN_VMEM = pl.BlockSpec(memory_space=pltpu.VMEM)
IN_HBM = pl.BlockSpec(memory_space=pltpu.HBM)


def swap(block, axis, partner):
    return lax.ppermute(block, axis, [(partner(i), i) for i in range(lax.axis_size(axis))])


def after(value, *others):
    return lax.optimization_barrier((value, *others))[0]


def call(kernel, name, operands, in_specs, out_shape, scratch_shapes=(), limit=SMALL_LIMIT):
    return pl.pallas_call(
        kernel,
        out_shape=out_shape,
        in_specs=in_specs,
        out_specs=jax.tree.map(lambda _: IN_VMEM, out_shape),
        scratch_shapes=list(scratch_shapes),
        compiler_params=pltpu.CompilerParams(vmem_limit_bytes=limit),
        cost_estimate=pl.CostEstimate(flops=1, bytes_accessed=1, transcendentals=0),
        name=name,
    )(*operands)


def powers(values):
    largest = jnp.maximum(jnp.max(values, axis=0, keepdims=True), 1e-3)
    return jnp.floor(jnp.log(largest) * (STEPS / LN2)) + 2.0


def code(values, power):
    scaled = values * (TOP * jnp.exp(power * (-LN2 / STEPS)))
    return ((scaled + 0.5).astype(jnp.int32) - 32767).astype(jnp.int16)


def scales(head):
    return jnp.exp(head.astype(jnp.int32).astype(jnp.float32) * (LN2 / STEPS)) * (1.0 / TOP)


def decode(codes, scale):
    return (codes.astype(jnp.int32) + 32767).astype(jnp.float32) * scale


def factor_rows(pattern, column, first, ref):
    place = lax.broadcasted_iota(jnp.int32, (1, ref.shape[1]), 1) // BS
    for u in range(ref.shape[0]):
        row = jnp.zeros((1, ref.shape[1]), jnp.float32)
        for v in range(ref.shape[1] // BS):
            row = jnp.where(place == v, pattern(column + v, first + u).astype(jnp.float32), row)
        ref[u : u + 1, :] = row


def masked(values, factors):
    parts = [
        values[u * BS : (u + 1) * BS] * factors[u : u + 1].astype(values.dtype) for u in range(values.shape[0] // BS)
    ]
    return jnp.concatenate(parts, axis=0) if len(parts) > 1 else parts[0]


def dot(left_side, right_side):
    return lax.dot_general(
        left_side, right_side, (((1,), (0,)), ((), ())), preferred_element_type=jnp.float32
    )


def columns_of(ref, start, count):
    return ref.at[0, :, pl.ds(pl.multiple_of(start * BS, BS), count * BS)]


def blocks_at(block, count=1):
    return pl.ds(pl.multiple_of(block * BS, BS), count * BS)


class Sides:
    def __init__(self, inner, panel):
        odd = lax.rem(lax.axis_index("blk"), 2)
        self.panel = panel
        self.first = lax.axis_index("layer") * (inner // BS)
        self.ext_side, self.int_side = odd * (2 * panel), (1 - odd) * (2 * panel)
        self.ext_rows = odd * panel
        self.columns = {"ext": self.ext_side, "own": panel, "int": self.int_side}


class Coded:
    def __init__(self, refs):
        self.refs = refs
        self.heads = [jnp.zeros((HEAD, ref.shape[1]), jnp.float32) for ref in refs]

    def write_all(self, product, place):
        for i in range(product.shape[0] // BS):
            self.write(product[i * BS : (i + 1) * BS], place + i)

    def write(self, product, place):
        column = 0
        for c, ref in enumerate(self.refs):
            chunk = product[:, column : column + ref.shape[1]]
            column += ref.shape[1]
            power = powers(chunk)
            ref[HEAD + place * BS : HEAD + (place + 1) * BS, :] = code(chunk, power)
            line = lax.broadcasted_iota(jnp.int32, self.heads[c].shape, 0)
            self.heads[c] = jnp.where(line == place, power, self.heads[c])

    def finish(self):
        for ref, head in zip(self.refs, self.heads):
            ref[0:HEAD, :] = head.astype(jnp.int32).astype(jnp.int16)


def first_kernel(a_hbm, b_hbm, c_hbm, flow_hbm, graph_hbm, *rest):
    out_refs, rest = rest[:-12], rest[-12:]
    rows_ref, a_rows_ref, b_rows_ref, c_rows_ref, graph_buf, flow_buf, total, ext_factors, a_ref, b_ref, c_ref, sems = rest
    inner, panel = flow_buf.shape[0], flow_buf.shape[1] // BS // 2
    at = Sides(inner, panel)
    steps = inner // BS
    small = [
        pltpu.make_async_copy(pattern, ref, sems.at[i])
        for i, (pattern, ref) in enumerate(((a_hbm, a_ref), (b_hbm, b_ref), (c_hbm, c_ref)))
    ]
    flows, graphs = [], []
    for t in range(steps):
        rows = slice(t * BS, (t + 1) * BS)
        flow = columns_of(flow_hbm, at.ext_rows, 2 * panel).at[rows]
        graph = columns_of(graph_hbm, at.ext_side, 1).at[rows]
        flows.append(pltpu.make_async_copy(flow, flow_buf.at[rows], sems.at[3 + 2 * t]))
        graphs.append(pltpu.make_async_copy(graph, graph_buf.at[rows], sems.at[4 + 2 * t]))
    for copy in small:
        copy.start()
    for t in range(steps):
        flows[t].start()
        graphs[t].start()
    for copy in small:
        copy.wait()
    factor_rows(lambda column, inner: a_ref[column, 0, inner], 0, at.first, a_rows_ref)
    factor_rows(lambda column, inner: b_ref[column, 0, inner], 0, at.first, b_rows_ref)
    factor_rows(lambda column, row: c_ref[0, column, row], 0, 0, c_rows_ref)
    ext_factors[...] = a_rows_ref[:, blocks_at(at.ext_rows, 2 * panel)]
    right_factors = b_rows_ref[:, blocks_at(at.ext_side)]
    per_dot = min(2, steps)
    for t in range(0, steps, per_dot):
        rows = slice(t * BS, (t + per_dot) * BS)
        for copy in flows[t : t + per_dot] + graphs[t : t + per_dot]:
            copy.wait()
        turned = masked(flow_buf[rows, :], ext_factors[t : t + per_dot]).T
        rows_ref[:, rows] = turned
        product = dot(turned, masked(graph_buf[rows, :], right_factors[t : t + per_dot]))
        if t + per_dot < steps:
            total[...] = product if t == 0 else total[...] + product
    if steps > per_dot:
        total[...] += product
    else:
        total[...] = product
    coded = Coded(out_refs)
    for place, first in ((0, panel), (panel, at.ext_side)):
        for i in range(panel):
            coded.write(total[blocks_at(first - at.ext_rows + i), :], place + i)
    coded.finish()


def first_products(flow_t, graph, a_lines, b_lines, c_lines):
    inner, width = flow_t.shape[1:]
    panel = width // 3
    return call(
        first_kernel,
        "first_products",
        [pltpu.with_memory_space_constraint(x, pltpu.HBM) for x in (a_lines, b_lines, c_lines, flow_t, graph)],
        [IN_HBM] * 5,
        [
            jax.ShapeDtypeStruct((HEAD + 2 * panel, BS), jnp.int16),
            pltpu.VMEM((2 * panel, inner), flow_t.dtype),
            pltpu.VMEM((inner // BS, width), jnp.float32),
            pltpu.VMEM((inner // BS, width), jnp.float32),
            pltpu.VMEM((width // BS, panel), jnp.float32),
        ],
        [
            pltpu.VMEM((inner, BS), graph.dtype),
            pltpu.VMEM((inner, 2 * panel), flow_t.dtype),
            pltpu.VMEM((2 * panel, BS), jnp.float32),
            pltpu.VMEM((inner // BS, 2 * panel), jnp.float32),
            pltpu.SMEM(a_lines.shape, a_lines.dtype),
            pltpu.SMEM(b_lines.shape, b_lines.dtype),
            pltpu.SMEM(c_lines.shape, c_lines.dtype),
            pltpu.SemaphoreType.DMA((3 + 2 * (inner // BS),)),
        ],
        limit=PRODUCT_LIMIT,
    )


def product_kernel(half, wanted, turns, a_rows_ref, b_rows_ref, graph_ref, ext_rows_ref, side_ref, *rest):
    refs = list(rest)
    inner, panel = graph_ref.shape[1], graph_ref.shape[2] // BS // 3
    at = Sides(inner, panel)
    parts = [part for part in ("ext", "own", "int") if part in wanted]
    outs = {part: [refs.pop(0) for _ in wanted[part]] for part in parts}
    int_rows_ref = side_ref
    if turns:
        int_rows_ref = refs.pop(0)
        place = blocks_at(at.int_side, panel)
        int_rows_ref[...] = masked(side_ref[0, :, place], a_rows_ref[:, place]).T
    coded = {part: Coded(outs[part]) for part in parts if part != "own"}
    right = []
    for part in parts:
        place = blocks_at(at.columns[part] + half)
        right.append(masked(graph_ref[0, :, place], b_rows_ref[:, place]))
    right = jnp.concatenate(right, axis=1) if len(right) > 1 else right[0]
    panels = (
        (panel, ext_rows_ref.at[blocks_at(panel - at.ext_rows, panel)], {"ext": 0, "own": 0, "int": 0}),
        (at.ext_side, ext_rows_ref.at[blocks_at(at.ext_side - at.ext_rows, panel)], {"ext": panel, "own": 0}),
        (at.int_side, int_rows_ref, {"own": 0, "int": panel}),
    )
    for first, source, takers in panels:
        used = [part for part in parts if part in takers]
        if not used:
            continue
        low = parts.index(used[0]) * BS
        for i in range(panel):
            product = dot(source[i * BS : (i + 1) * BS, :], right[:, low : low + len(used) * BS])
            for j, part in enumerate(used):
                piece = product[:, j * BS : (j + 1) * BS]
                if part == "own":
                    outs[part][0][blocks_at(first + i), :] = piece
                else:
                    coded[part].write(piece, takers[part] + i)
    for part in coded:
        coded[part].finish()


def products(a_rows, b_rows, graph, ext_rows, side, half, wanted, turns=False):
    inner, width = graph.shape[1:]
    panel = width // 3
    outs = []
    for part in ("ext", "own", "int"):
        for w in wanted.get(part, ()):
            if part == "own":
                outs.append(jax.ShapeDtypeStruct((width, w), jnp.float32))
            else:
                outs.append(jax.ShapeDtypeStruct((HEAD + 2 * panel, w), jnp.int16))
    if turns:
        outs.append(pltpu.VMEM((panel, inner), graph.dtype))
    return call(
        functools.partial(product_kernel, half, wanted, turns),
        "_".join(wanted) + f"_products_{half}",
        (a_rows, b_rows, graph, ext_rows, side),
        [IN_VMEM] * 5,
        outs,
        limit=PRODUCT_LIMIT,
    )


def send_strip(send_ref, strips, power):
    rows = strips[0].shape[0]
    for j, strip in enumerate(strips):
        send_ref[HEAD + j * rows : HEAD + (j + 1) * rows, :] = code(strip, power)
    send_ref[0:HEAD, :] = jnp.broadcast_to(power, (HEAD, power.shape[1])).astype(jnp.int32).astype(jnp.int16)


def split_strips(total, rows, position, keep_ref, send_ref):
    bit = lax.rem(lax.axis_index("layer") // position, 2)
    pairs = keep_ref.shape[0]
    for j in range(pairs):
        keep_ref[j] = total[pl.ds((2 * j + bit) * rows, rows), :]
    away = [total[pl.ds((2 * j + 1 - bit) * rows, rows), :] for j in range(pairs)]
    power = functools.reduce(jnp.maximum, [powers(strip) for strip in away])
    for j, strip in enumerate(away):
        send_ref[HEAD + j * rows : HEAD + (j + 1) * rows, :] = code(strip, power)
    send_ref[0:HEAD, :] = jnp.broadcast_to(power, (HEAD, power.shape[1])).astype(jnp.int32).astype(jnp.int16)


def join_kernel(rows, half, lanes, c_ref, own_ref, ext_ref, int_ref, keep_ref, send_ref, total):
    odd = lax.rem(lax.axis_index("blk"), 2)
    panel = own_ref.shape[0] // BS // 3
    refs = (ext_ref.at[:, lanes], int_ref.at[:, lanes])
    c_lanes = slice(half * BS + lanes.start, half * BS + lanes.stop)
    from_mid, from_side = ([[(r, start + i) for i in range(panel)] for r in range(2)] for start in (0, panel))
    middle = [list(both) for both in zip(from_side[0], from_side[1])]
    ext_only, int_only = ([[part] for part in from_mid[r]] for r in range(2))
    odd_parts = int_only + middle + ext_only
    even_parts = ext_only + middle + int_only

    def add(parts):
        scale = [scales(ref[0:HEAD, :]) for ref in refs]
        for v in range(3 * panel):
            kept = c_ref[v : v + 1, c_lanes]
            block = own_ref[v * BS : (v + 1) * BS, lanes] * kept
            for r, i in parts[v]:
                codes = refs[r][HEAD + i * BS : HEAD + (i + 1) * BS, :]
                block += decode(codes, scale[r][i : i + 1] * kept)
            total[v * BS : (v + 1) * BS, :] = block

    @pl.when(odd == 1)
    def _():
        add(odd_parts)

    @pl.when(odd == 0)
    def _():
        add(even_parts)

    split_strips(total, rows, 1, keep_ref, send_ref)


def strips_shapes(pairs, rows, width):
    return [
        jax.ShapeDtypeStruct((pairs, rows, width), jnp.float32),
        jax.ShapeDtypeStruct((HEAD + pairs * rows, width), jnp.int16),
    ]


def join(own, ext_part, lane, int_part, c_rows, half, width, layers):
    height = own.shape[0]
    rows = height // layers
    return call(
        functools.partial(join_kernel, rows, half, slice(lane, lane + width)),
        f"join_{half}_{lane}",
        (c_rows, own, ext_part, int_part),
        [IN_VMEM] * 4,
        strips_shapes(layers // 2, rows, width),
        [pltpu.VMEM((height, width), jnp.float32)],
    )


def halve_kernel(rows, position, kept_ref, got_ref, keep_ref, send_ref, total):
    scale = scales(got_ref[0:HEAD, :])[0:1]
    for j in range(kept_ref.shape[0]):
        codes = got_ref[HEAD + j * rows : HEAD + (j + 1) * rows, :]
        total[j * rows : (j + 1) * rows, :] = kept_ref[j] + decode(codes, scale)
    split_strips(total, rows, position, keep_ref, send_ref)


def halve(kept, got, position, chunk):
    strips, rows, width = kept.shape
    return call(
        functools.partial(halve_kernel, rows, position),
        f"halve_{position}_{chunk}",
        (kept, got),
        [IN_VMEM] * 2,
        strips_shapes(strips // 2, rows, width),
        [pltpu.VMEM((strips * rows, width), jnp.float32)],
    )


def square_kernel(kept_ref, got_ref, *rest):
    earlier, (square_ref, sums_ref) = rest[:-2], rest[-2:]
    value = kept_ref[0] + decode(got_ref[HEAD:, :], scales(got_ref[0:HEAD, :])[0:1])
    square = value * value
    square_ref[...] = square
    sums = jnp.broadcast_to(jnp.sum(square, axis=0, keepdims=True), (8, square.shape[1]))
    sums_ref[...] = jnp.concatenate([ref[...] for ref in earlier] + [sums], axis=1)


def square(kept, got, earlier, chunk):
    _, rows, width = kept.shape
    return call(
        square_kernel,
        f"square_{chunk}",
        (kept, got, *earlier),
        [IN_VMEM] * (2 + len(earlier)),
        [
            jax.ShapeDtypeStruct((rows, width), jnp.float32),
            jax.ShapeDtypeStruct((8, width + sum(sums.shape[1] for sums in earlier)), jnp.float32),
        ],
    )


def rescale_kernel(height, count, *refs):
    squares, sums, out_ref = refs[:count], refs[count:-1], refs[-1]
    total = functools.reduce(jnp.add, [ref[0:1, :] for ref in sums])
    divisor = total / height + 1e-6
    column = 0
    for ref in squares:
        columns = slice(column, column + ref.shape[1])
        column += ref.shape[1]
        out_ref[0, :, columns] = ref[...] / divisor[:, columns]


def rescale(squares, sums, height):
    rows = squares[0].shape[0]
    width = sums[0].shape[1]
    return call(
        functools.partial(rescale_kernel, float(height), len(squares)),
        "rescale",
        (*squares, *sums),
        [IN_VMEM] * (len(squares) + len(sums)),
        jax.ShapeDtypeStruct((1, rows, width), jnp.float32),
    )


def shards(flow_t, graph, a_pattern, b_pattern, c_pattern):
    layers = lax.axis_size("layer")
    blks = lax.axis_size("blk")
    width = flow_t.shape[2]
    panel = width // 3
    a_lines = a_pattern.transpose(2, 0, 1)
    b_lines = b_pattern.transpose(2, 0, 1)
    c_lines = c_pattern.transpose(0, 2, 1)

    def other_chip(i):
        return (i + 1 if i % 2 else i - 1) % blks

    def same_chip(i):
        return i ^ 1

    halves = panel // BS
    fine = (LANES,) * (BS // LANES)
    widths = [(BS,)] * (halves - 1) + [fine]
    ext, ints, owns, latest = [], [], [], []

    def ordered(value):
        return after(value, latest[-1])

    def send(part, partner, got):
        whole = swap(part, "blk", partner)
        half_widths = widths[len(got)]
        got.append([(whole, sum(half_widths[:i])) for i in range(len(half_widths))])

    part, ext_rows, a_rows, b_rows, c_rows = first_products(flow_t, graph, a_lines, b_lines, c_lines)
    send(part, other_chip, ext)
    latest.append(part)
    wanted = {"own": (BS,), "int": (BS,)}
    own, part, int_rows = products(a_rows, ordered(b_rows), graph, ext_rows, flow_t, 0, wanted, turns=True)
    owns.append(own)
    send(part, same_chip, ints)
    latest.append(own)

    def side_products(half):
        wanted = {"ext": (BS,), "int": (BS,)}
        ext_part, int_part = products(a_rows, ordered(b_rows), graph, ext_rows, int_rows, half, wanted)
        send(ext_part, other_chip, ext)
        send(int_part, same_chip, ints)
        latest.append(ext_part)

    def own_products(half):
        owns.extend(products(a_rows, ordered(b_rows), graph, ext_rows, int_rows, half, {"own": (BS,)}))
        latest.append(owns[-1])

    strips, squares, sums = [], [], []
    places = [(half, i) for half, each in enumerate(widths) for i in range(len(each))]
    chunks = len(places)

    def add_up(chunk):
        half, i = places[chunk]
        width = widths[half][i]
        kept, send = join(owns[half], *ext[half][i], ints[half][i][0], ordered(c_rows), half, width, layers)
        latest.append(kept)
        strips.append((kept, swap(send, "layer", lambda i: i ^ 1)))

    def scatter(chunk):
        kept, got = strips[chunk]
        position = 1
        while kept.shape[0] > 1:
            position *= 2
            kept, send = halve(ordered(kept), got, position, chunk)
            latest.append(kept)
            got = swap(send, "layer", lambda i: i ^ position)
        strips[chunk] = kept, got

    def finish(chunk):
        kept, got = strips[chunk]
        squared, summed = square(ordered(kept), got, sums if chunk == chunks - 1 else [], chunk)
        latest.append(summed)
        squares.append(squared)
        sums.append(summed)

    for half in range(1, halves):
        side_products(half)
        add_up(half - 1)
        own_products(half)
    scatter(0)
    for chunk in range(halves - 1, chunks):
        add_up(chunk)
    scatter(1)
    finish(0)
    for chunk in range(2, chunks):
        scatter(chunk)
    for chunk in range(1, chunks):
        finish(chunk)

    mine = sums[-1]
    others = [swap(mine, "layer", lambda i: i ^ other) for other in range(1, layers)]
    return rescale(squares, [mine, *others], width)


def solution(mesh):
    placed = (
        P("blk", "layer", None),
        P("blk", "layer", None),
        P("blk", None, None),
        P("blk", None, None),
        P("blk", None, None),
    )
    return jax.shard_map(
        shards, mesh=mesh, in_specs=placed, out_specs=P("blk", "layer", None), check_vma=False
    )
```

```python
import functools

import jax
import jax.numpy as jnp
from jax import lax
from jax.experimental import pallas as pl
from jax.experimental.pallas import tpu as pltpu
from jax.sharding import PartitionSpec as P

BS = 256
LANES = 128
HEAD = 16
STEPS = 256.0
TOP = 65534.0
LN2 = 0.6931471805599453
DIRECT = 1
PRODUCT_LIMIT = 24000000
SMALL_LIMIT = 8 * 1024 * 1024
IN_VMEM = pl.BlockSpec(memory_space=pltpu.VMEM)
IN_HBM = pl.BlockSpec(memory_space=pltpu.HBM)


def swap(block, axis, partner):
    return lax.ppermute(block, axis, [(partner(i), i) for i in range(lax.axis_size(axis))])


def after(value, *others):
    return lax.optimization_barrier((value, *others))[0]


def call(kernel, name, operands, in_specs, out_shape, scratch_shapes=(), limit=SMALL_LIMIT):
    return pl.pallas_call(
        kernel,
        out_shape=out_shape,
        in_specs=in_specs,
        out_specs=jax.tree.map(lambda _: IN_VMEM, out_shape),
        scratch_shapes=list(scratch_shapes),
        compiler_params=pltpu.CompilerParams(vmem_limit_bytes=limit),
        cost_estimate=pl.CostEstimate(flops=1, bytes_accessed=1, transcendentals=0),
        name=name,
    )(*operands)


def powers(values):
    largest = jnp.maximum(jnp.max(values, axis=0, keepdims=True), 1e-3)
    return jnp.floor(jnp.log(largest) * (STEPS / LN2)) + 2.0


def code(values, power):
    scaled = values * (TOP * jnp.exp(power * (-LN2 / STEPS)))
    return ((scaled + 0.5).astype(jnp.int32) - 32767).astype(jnp.int16)


def scales(head):
    return jnp.exp(head.astype(jnp.int32).astype(jnp.float32) * (LN2 / STEPS)) * (1.0 / TOP)


def decode(codes, scale):
    return (codes.astype(jnp.int32) + 32767).astype(jnp.float32) * scale


def factor_rows(pattern, column, first, ref):
    place = lax.broadcasted_iota(jnp.int32, (1, ref.shape[1]), 1) // BS
    for u in range(ref.shape[0]):
        row = jnp.zeros((1, ref.shape[1]), jnp.float32)
        for v in range(ref.shape[1] // BS):
            row = jnp.where(place == v, pattern(column + v, first + u).astype(jnp.float32), row)
        ref[u : u + 1, :] = row


def masked(values, factors):
    parts = [
        values[u * BS : (u + 1) * BS] * factors[u : u + 1].astype(values.dtype) for u in range(values.shape[0] // BS)
    ]
    return jnp.concatenate(parts, axis=0) if len(parts) > 1 else parts[0]


def dot(left_side, right_side):
    return lax.dot_general(
        left_side, right_side, (((1,), (0,)), ((), ())), preferred_element_type=jnp.float32
    )


def columns_of(ref, start, count):
    return ref.at[0, :, pl.ds(pl.multiple_of(start * BS, BS), count * BS)]


def blocks_at(block, count=1):
    return pl.ds(pl.multiple_of(block * BS, BS), count * BS)


class Sides:
    def __init__(self, inner, panel):
        odd = lax.rem(lax.axis_index("blk"), 2)
        self.panel = panel
        self.first = lax.axis_index("layer") * (inner // BS)
        self.ext_side, self.int_side = odd * (2 * panel), (1 - odd) * (2 * panel)
        self.ext_rows = odd * panel
        self.columns = {"ext": self.ext_side, "own": panel, "int": self.int_side}


class Coded:
    def __init__(self, refs):
        self.refs = refs
        self.heads = [jnp.zeros((HEAD, ref.shape[1]), jnp.float32) for ref in refs]

    def write_all(self, product, place):
        for i in range(product.shape[0] // BS):
            self.write(product[i * BS : (i + 1) * BS], place + i)

    def write(self, product, place):
        column = 0
        for c, ref in enumerate(self.refs):
            chunk = product[:, column : column + ref.shape[1]]
            column += ref.shape[1]
            power = powers(chunk)
            ref[HEAD + place * BS : HEAD + (place + 1) * BS, :] = code(chunk, power)
            line = lax.broadcasted_iota(jnp.int32, self.heads[c].shape, 0)
            self.heads[c] = jnp.where(line == place, power, self.heads[c])

    def finish(self):
        for ref, head in zip(self.refs, self.heads):
            ref[0:HEAD, :] = head.astype(jnp.int32).astype(jnp.int16)


def first_kernel(a_hbm, b_hbm, c_hbm, flow_hbm, graph_hbm, *rest):
    out_refs, rest = rest[:-12], rest[-12:]
    rows_ref, a_rows_ref, b_rows_ref, c_rows_ref, graph_buf, flow_buf, total, ext_factors, a_ref, b_ref, c_ref, sems = rest
    inner, panel = flow_buf.shape[0], flow_buf.shape[1] // BS // 2
    at = Sides(inner, panel)
    steps = inner // BS
    small = [
        pltpu.make_async_copy(pattern, ref, sems.at[i])
        for i, (pattern, ref) in enumerate(((a_hbm, a_ref), (b_hbm, b_ref), (c_hbm, c_ref)))
    ]
    flows, graphs = [], []
    for t in range(steps):
        rows = slice(t * BS, (t + 1) * BS)
        flow = columns_of(flow_hbm, at.ext_rows, 2 * panel).at[rows]
        graph = columns_of(graph_hbm, at.ext_side, 1).at[rows]
        flows.append(pltpu.make_async_copy(flow, flow_buf.at[rows], sems.at[3 + 2 * t]))
        graphs.append(pltpu.make_async_copy(graph, graph_buf.at[rows], sems.at[4 + 2 * t]))
    for copy in small:
        copy.start()
    for t in range(steps):
        flows[t].start()
        graphs[t].start()
    for copy in small:
        copy.wait()
    factor_rows(lambda column, inner: a_ref[column, 0, inner], 0, at.first, a_rows_ref)
    factor_rows(lambda column, inner: b_ref[column, 0, inner], 0, at.first, b_rows_ref)
    factor_rows(lambda column, row: c_ref[0, column, row], 0, 0, c_rows_ref)
    ext_factors[...] = a_rows_ref[:, blocks_at(at.ext_rows, 2 * panel)]
    right_factors = b_rows_ref[:, blocks_at(at.ext_side)]
    per_dot = min(2, steps)
    for t in range(0, steps, per_dot):
        rows = slice(t * BS, (t + per_dot) * BS)
        for copy in flows[t : t + per_dot] + graphs[t : t + per_dot]:
            copy.wait()
        turned = masked(flow_buf[rows, :], ext_factors[t : t + per_dot]).T
        rows_ref[:, rows] = turned
        product = dot(turned, masked(graph_buf[rows, :], right_factors[t : t + per_dot]))
        if t + per_dot < steps:
            total[...] = product if t == 0 else total[...] + product
    if steps > per_dot:
        total[...] += product
    else:
        total[...] = product
    coded = Coded(out_refs)
    for place, first in ((0, panel), (panel, at.ext_side)):
        for i in range(panel):
            coded.write(total[blocks_at(first - at.ext_rows + i), :], place + i)
    coded.finish()


def first_products(flow_t, graph, a_lines, b_lines, c_lines, widths):
    inner, width = flow_t.shape[1:]
    panel = width // 3
    return call(
        first_kernel,
        "first_products",
        [pltpu.with_memory_space_constraint(x, pltpu.HBM) for x in (a_lines, b_lines, c_lines, flow_t, graph)],
        [IN_HBM] * 5,
        [jax.ShapeDtypeStruct((HEAD + 2 * panel, w), jnp.int16) for w in widths]
        + [
            pltpu.VMEM((2 * panel, inner), flow_t.dtype),
            pltpu.VMEM((inner // BS, width), jnp.float32),
            pltpu.VMEM((inner // BS, width), jnp.float32),
            pltpu.VMEM((width // BS, panel), jnp.float32),
        ],
        [
            pltpu.VMEM((inner, BS), graph.dtype),
            pltpu.VMEM((inner, 2 * panel), flow_t.dtype),
            pltpu.VMEM((2 * panel, BS), jnp.float32),
            pltpu.VMEM((inner // BS, 2 * panel), jnp.float32),
            pltpu.SMEM(a_lines.shape, a_lines.dtype),
            pltpu.SMEM(b_lines.shape, b_lines.dtype),
            pltpu.SMEM(c_lines.shape, c_lines.dtype),
            pltpu.SemaphoreType.DMA((3 + 2 * (inner // BS),)),
        ],
        limit=PRODUCT_LIMIT,
    )


def product_kernel(half, wanted, turns, a_rows_ref, b_rows_ref, graph_ref, ext_rows_ref, side_ref, *rest):
    refs = list(rest)
    inner, panel = graph_ref.shape[1], graph_ref.shape[2] // BS // 3
    at = Sides(inner, panel)
    parts = [part for part in ("ext", "own", "int") if part in wanted]
    outs = {part: [refs.pop(0) for _ in wanted[part]] for part in parts}
    int_rows_ref = side_ref
    if turns:
        int_rows_ref = refs.pop(0)
        place = blocks_at(at.int_side, panel)
        int_rows_ref[...] = masked(side_ref[0, :, place], a_rows_ref[:, place]).T
    coded = {part: Coded(outs[part]) for part in parts if part != "own"}
    right = []
    for part in parts:
        place = blocks_at(at.columns[part] + half)
        right.append(masked(graph_ref[0, :, place], b_rows_ref[:, place]))
    right = jnp.concatenate(right, axis=1) if len(right) > 1 else right[0]
    panels = (
        (panel, ext_rows_ref.at[blocks_at(panel - at.ext_rows, panel)], {"ext": 0, "own": 0, "int": 0}),
        (at.ext_side, ext_rows_ref.at[blocks_at(at.ext_side - at.ext_rows, panel)], {"ext": panel, "own": 0}),
        (at.int_side, int_rows_ref, {"own": 0, "int": panel}),
    )
    for first, source, takers in panels:
        used = [part for part in parts if part in takers]
        if not used:
            continue
        low = parts.index(used[0]) * BS
        for i in range(panel):
            product = dot(source[i * BS : (i + 1) * BS, :], right[:, low : low + len(used) * BS])
            for j, part in enumerate(used):
                piece = product[:, j * BS : (j + 1) * BS]
                if part == "own":
                    outs[part][0][blocks_at(first + i), :] = piece
                else:
                    coded[part].write(piece, takers[part] + i)
    for part in coded:
        coded[part].finish()


def products(a_rows, b_rows, graph, ext_rows, side, half, wanted, turns=False):
    inner, width = graph.shape[1:]
    panel = width // 3
    outs = []
    for part in ("ext", "own", "int"):
        for w in wanted.get(part, ()):
            if part == "own":
                outs.append(jax.ShapeDtypeStruct((width, w), jnp.float32))
            else:
                outs.append(jax.ShapeDtypeStruct((HEAD + 2 * panel, w), jnp.int16))
    if turns:
        outs.append(pltpu.VMEM((panel, inner), graph.dtype))
    return call(
        functools.partial(product_kernel, half, wanted, turns),
        "_".join(wanted) + f"_products_{half}",
        (a_rows, b_rows, graph, ext_rows, side),
        [IN_VMEM] * 5,
        outs,
        limit=PRODUCT_LIMIT,
    )


def send_strip(send_ref, strips, power):
    rows = strips[0].shape[0]
    for j, strip in enumerate(strips):
        send_ref[HEAD + j * rows : HEAD + (j + 1) * rows, :] = code(strip, power)
    send_ref[0:HEAD, :] = jnp.broadcast_to(power, (HEAD, power.shape[1])).astype(jnp.int32).astype(jnp.int16)


def split_strips(total, rows, position, keep_ref, send_refs):
    layer = lax.axis_index("layer")
    if len(send_refs) > 1:
        keep_ref[0] = total[pl.ds(layer * rows, rows), :]
        for other, send_ref in enumerate(send_refs, 1):
            strip = total[pl.ds((layer ^ other) * rows, rows), :]
            send_strip(send_ref, [strip], powers(strip))
        return
    bit = lax.rem(layer // position, 2)
    pairs = keep_ref.shape[0]
    for j in range(pairs):
        keep_ref[j] = total[pl.ds((2 * j + bit) * rows, rows), :]
    away = [total[pl.ds((2 * j + 1 - bit) * rows, rows), :] for j in range(pairs)]
    send_strip(send_refs[0], away, functools.reduce(jnp.maximum, [powers(strip) for strip in away]))


def join_kernel(rows, half, lane, c_ref, own_ref, ext_ref, int_ref, keep_ref, *rest):
    *send_refs, total = rest
    odd = lax.rem(lax.axis_index("blk"), 2)
    panel = own_ref.shape[0] // BS // 3
    lanes = slice(lane, lane + ext_ref.shape[1])
    refs = (ext_ref, int_ref)
    from_mid, from_side = ([[(r, start + i) for i in range(panel)] for r in range(2)] for start in (0, panel))
    middle = [list(both) for both in zip(from_side[0], from_side[1])]
    ext_only, int_only = ([[part] for part in from_mid[r]] for r in range(2))
    odd_parts = int_only + middle + ext_only
    even_parts = ext_only + middle + int_only

    def add(parts):
        scale = [scales(ref[0:HEAD, :]) for ref in refs]
        for v in range(3 * panel):
            kept = c_ref[v : v + 1, half * BS + lane : half * BS + lane + ext_ref.shape[1]]
            block = own_ref[v * BS : (v + 1) * BS, lanes] * kept
            for r, i in parts[v]:
                codes = refs[r][HEAD + i * BS : HEAD + (i + 1) * BS, :]
                block += decode(codes, scale[r][i : i + 1] * kept)
            total[v * BS : (v + 1) * BS, :] = block

    @pl.when(odd == 1)
    def _():
        add(odd_parts)

    @pl.when(odd == 0)
    def _():
        add(even_parts)

    split_strips(total, rows, 1, keep_ref, send_refs)


def strips_shapes(pairs, rows, width, messages=1):
    return [
        jax.ShapeDtypeStruct((pairs, rows, width), jnp.float32),
        *[jax.ShapeDtypeStruct((HEAD + pairs * rows, width), jnp.int16)] * messages,
    ]


def join(own, ext_part, int_part, c_rows, half, lane, layers, direct):
    height = own.shape[0]
    width = int_part.shape[1]
    rows = height // layers
    return call(
        functools.partial(join_kernel, rows, half, lane),
        f"join_{half}_{lane}",
        (c_rows, own, ext_part, int_part),
        [IN_VMEM] * 4,
        strips_shapes(1, rows, width, layers - 1) if direct else strips_shapes(layers // 2, rows, width),
        [pltpu.VMEM((height, width), jnp.float32)],
    )


def halve_kernel(rows, position, kept_ref, got_ref, keep_ref, send_ref, total):
    scale = scales(got_ref[0:HEAD, :])[0:1]
    for j in range(kept_ref.shape[0]):
        codes = got_ref[HEAD + j * rows : HEAD + (j + 1) * rows, :]
        total[j * rows : (j + 1) * rows, :] = kept_ref[j] + decode(codes, scale)
    split_strips(total, rows, position, keep_ref, [send_ref])


def halve(kept, got, position, chunk):
    strips, rows, width = kept.shape
    return call(
        functools.partial(halve_kernel, rows, position),
        f"halve_{position}_{chunk}",
        (kept, got),
        [IN_VMEM] * 2,
        strips_shapes(strips // 2, rows, width),
        [pltpu.VMEM((strips * rows, width), jnp.float32)],
    )


def square_kernel(messages, place, kept_ref, *rest):
    got_refs, others, (square_ref, sums_ref) = rest[:messages], rest[messages:-2], rest[-2:]
    value = kept_ref[0]
    for ref in got_refs:
        value += decode(ref[HEAD:, :], scales(ref[0:HEAD, :])[0:1])
    square = value * value
    square_ref[...] = square
    sums = jnp.broadcast_to(jnp.sum(square, axis=0, keepdims=True), (8, square.shape[1]))
    every = [ref[...] for ref in others]
    sums_ref[...] = jnp.concatenate(every[:place] + [sums] + every[place:], axis=1)


def square(kept, got, others, place, chunk):
    _, rows, width = kept.shape
    return call(
        functools.partial(square_kernel, len(got), place),
        f"square_{chunk}",
        (kept, *got, *others),
        [IN_VMEM] * (1 + len(got) + len(others)),
        [
            jax.ShapeDtypeStruct((rows, width), jnp.float32),
            jax.ShapeDtypeStruct((8, width + sum(sums.shape[1] for sums in others)), jnp.float32),
        ],
    )


def rescale_kernel(height, count, *refs):
    squares, sums, out_ref = refs[:count], refs[count:-1], refs[-1]
    total = functools.reduce(jnp.add, [ref[0:1, :] for ref in sums])
    divisor = total / height + 1e-6
    column = 0
    for ref in squares:
        columns = slice(column, column + ref.shape[1])
        column += ref.shape[1]
        out_ref[0, :, columns] = ref[...] / divisor[:, columns]


def rescale(squares, sums, height):
    rows = squares[0].shape[0]
    width = sums[0].shape[1]
    return call(
        functools.partial(rescale_kernel, float(height), len(squares)),
        "rescale",
        (*squares, *sums),
        [IN_VMEM] * (len(squares) + len(sums)),
        jax.ShapeDtypeStruct((1, rows, width), jnp.float32),
    )


def shards(flow_t, graph, a_pattern, b_pattern, c_pattern):
    layers = lax.axis_size("layer")
    blks = lax.axis_size("blk")
    width = flow_t.shape[2]
    panel = width // 3
    a_lines = a_pattern.transpose(2, 0, 1)
    b_lines = b_pattern.transpose(2, 0, 1)
    c_lines = c_pattern.transpose(0, 2, 1)

    def other_chip(i):
        return (i + 1 if i % 2 else i - 1) % blks

    def same_chip(i):
        return i ^ 1

    halves = panel // BS
    chunks = panel // LANES
    fine = (LANES,) * (BS // LANES)
    per_half = len(fine)
    ext, ints, owns, latest = [], [], [], []

    def ordered(value):
        return after(value, latest[-1])

    def send_ext(parts):
        ext.extend(swap(part, "blk", other_chip) for part in parts)
        latest.append(parts[0])

    def send_int(parts):
        ints.extend(swap(part, "blk", same_chip) for part in parts)
        latest.append(parts[0])

    *parts, ext_rows, a_rows, b_rows, c_rows = first_products(flow_t, graph, a_lines, b_lines, c_lines, fine)
    send_ext(parts)
    wanted = {"own": (BS,), "int": fine}
    own, *parts, int_rows = products(a_rows, ordered(b_rows), graph, ext_rows, flow_t, 0, wanted, turns=True)
    owns.append(own)
    send_int(parts)

    def more_products(half):
        wanted = {"ext": fine, "int": fine}
        parts = products(a_rows, ordered(b_rows), graph, ext_rows, int_rows, half, wanted)
        send_ext(parts[:per_half])
        send_int(parts[per_half:])

    def more_own(half):
        owns.extend(products(a_rows, ordered(b_rows), graph, ext_rows, int_rows, half, {"own": (BS,)}))
        latest.append(owns[-1])

    strips, squares, sums = [], {}, {}

    def add_up(chunk):
        half, lane = divmod(chunk, per_half)
        direct = chunk >= chunks - DIRECT and layers <= 4
        kept, *sends = join(
            owns[half], ext[chunk], ints[chunk], ordered(c_rows), half, lane * LANES, layers, direct
        )
        latest.append(kept)
        strips.append((kept, [swap(send, "layer", lambda i: i ^ other) for other, send in enumerate(sends, 1)]))

    def scatter(chunk):
        kept, got = strips[chunk]
        position = 1
        while kept.shape[0] > 1:
            position *= 2
            kept, send = halve(ordered(kept), got[0], position, chunk)
            latest.append(kept)
            got = [swap(send, "layer", lambda i: i ^ position)]
        strips[chunk] = kept, got

    def finish(chunk):
        kept, got = strips[chunk]
        others, place = ([], 0)
        if len(squares) == chunks - 1:
            others, place = [sums[i] for i in sorted(sums)], chunk
        squares[chunk], sums[chunk] = square(ordered(kept), got, others, place, chunk)
        latest.append(sums[chunk])

    for chunk in range(chunks):
        add_up(chunk)
        if (chunk + 1) % per_half == 0 and len(owns) < halves:
            more_own(len(owns))
        if 1 <= chunk < chunks - 1:
            scatter(chunk - 1)
        if chunk % per_half == 0 and chunk // per_half + 1 < halves:
            more_products(chunk // per_half + 1)
    finish(0)
    finish(1)
    for chunk in range(chunks - 2, chunks):
        scatter(chunk)
    finish(chunks - 1)
    finish(chunks - 2)

    squares = [squares[i] for i in sorted(squares)]
    mine = sums[chunks - 2]
    others = [swap(mine, "layer", lambda i: i ^ other) for other in range(1, layers)]
    return rescale(squares, [mine, *others], width)


def solution(mesh):
    placed = (
        P("blk", "layer", None),
        P("blk", "layer", None),
        P("blk", None, None),
        P("blk", None, None),
        P("blk", None, None),
    )
    return jax.shard_map(
        shards, mesh=mesh, in_specs=placed, out_specs=P("blk", "layer", None), check_vma=False
    )
```

```python
import functools

import jax
import jax.numpy as jnp
from jax import lax
from jax.experimental import pallas as pl
from jax.experimental.pallas import tpu as pltpu
from jax.sharding import PartitionSpec as P

BS = 256
LANES = 128
HEAD = 16
STEPS = 256.0
TOP = 65534.0
LN2 = 0.6931471805599453
DIRECT = 1
PRODUCT_LIMIT = 24000000
SMALL_LIMIT = 8 * 1024 * 1024
IN_VMEM = pl.BlockSpec(memory_space=pltpu.VMEM)
IN_HBM = pl.BlockSpec(memory_space=pltpu.HBM)


def swap(block, axis, partner):
    return lax.ppermute(block, axis, [(partner(i), i) for i in range(lax.axis_size(axis))])


def after(value, *others):
    return lax.optimization_barrier((value, *others))[0]


def call(kernel, name, operands, in_specs, out_shape, scratch_shapes=(), limit=SMALL_LIMIT):
    return pl.pallas_call(
        kernel,
        out_shape=out_shape,
        in_specs=in_specs,
        out_specs=jax.tree.map(lambda _: IN_VMEM, out_shape),
        scratch_shapes=list(scratch_shapes),
        compiler_params=pltpu.CompilerParams(vmem_limit_bytes=limit),
        cost_estimate=pl.CostEstimate(flops=1, bytes_accessed=1, transcendentals=0),
        name=name,
    )(*operands)


def powers(values):
    largest = jnp.maximum(jnp.max(values, axis=0, keepdims=True), 1e-3)
    return jnp.floor(jnp.log(largest) * (STEPS / LN2)) + 2.0


def code(values, power):
    scaled = values * (TOP * jnp.exp(power * (-LN2 / STEPS)))
    return ((scaled + 0.5).astype(jnp.int32) - 32767).astype(jnp.int16)


def scales(head):
    return jnp.exp(head.astype(jnp.int32).astype(jnp.float32) * (LN2 / STEPS)) * (1.0 / TOP)


def decode(codes, scale):
    return (codes.astype(jnp.int32) + 32767).astype(jnp.float32) * scale


def factor_rows(pattern, column, first, ref):
    place = lax.broadcasted_iota(jnp.int32, (1, ref.shape[1]), 1) // BS
    for u in range(ref.shape[0]):
        row = jnp.zeros((1, ref.shape[1]), jnp.float32)
        for v in range(ref.shape[1] // BS):
            row = jnp.where(place == v, pattern(column + v, first + u).astype(jnp.float32), row)
        ref[u : u + 1, :] = row


def masked(values, factors):
    parts = [
        values[u * BS : (u + 1) * BS] * factors[u : u + 1].astype(values.dtype) for u in range(values.shape[0] // BS)
    ]
    return jnp.concatenate(parts, axis=0) if len(parts) > 1 else parts[0]


def dot(left_side, right_side):
    return lax.dot_general(
        left_side, right_side, (((1,), (0,)), ((), ())), preferred_element_type=jnp.float32
    )


def columns_of(ref, start, count):
    return ref.at[0, :, pl.ds(pl.multiple_of(start * BS, BS), count * BS)]


def blocks_at(block, count=1):
    return pl.ds(pl.multiple_of(block * BS, BS), count * BS)


class Sides:
    def __init__(self, inner, panel):
        odd = lax.rem(lax.axis_index("blk"), 2)
        self.panel = panel
        self.first = lax.axis_index("layer") * (inner // BS)
        self.ext_side, self.int_side = odd * (2 * panel), (1 - odd) * (2 * panel)
        self.ext_rows = odd * panel
        self.columns = {"ext": self.ext_side, "own": panel, "int": self.int_side}


class Coded:
    def __init__(self, refs):
        self.refs = refs
        self.heads = [jnp.zeros((HEAD, ref.shape[1]), jnp.float32) for ref in refs]

    def write_all(self, product, place):
        for i in range(product.shape[0] // BS):
            self.write(product[i * BS : (i + 1) * BS], place + i)

    def write(self, product, place):
        column = 0
        for c, ref in enumerate(self.refs):
            chunk = product[:, column : column + ref.shape[1]]
            column += ref.shape[1]
            power = powers(chunk)
            ref[HEAD + place * BS : HEAD + (place + 1) * BS, :] = code(chunk, power)
            line = lax.broadcasted_iota(jnp.int32, self.heads[c].shape, 0)
            self.heads[c] = jnp.where(line == place, power, self.heads[c])

    def finish(self):
        for ref, head in zip(self.refs, self.heads):
            ref[0:HEAD, :] = head.astype(jnp.int32).astype(jnp.int16)


def first_kernel(a_hbm, b_hbm, c_hbm, flow_hbm, graph_hbm, *rest):
    out_refs, rest = rest[:-12], rest[-12:]
    rows_ref, a_rows_ref, b_rows_ref, c_rows_ref, graph_buf, flow_buf, total, ext_factors, a_ref, b_ref, c_ref, sems = rest
    inner, panel = flow_buf.shape[0], flow_buf.shape[1] // BS // 2
    at = Sides(inner, panel)
    steps = inner // BS
    small = [
        pltpu.make_async_copy(pattern, ref, sems.at[i])
        for i, (pattern, ref) in enumerate(((a_hbm, a_ref), (b_hbm, b_ref), (c_hbm, c_ref)))
    ]
    flows, graphs = [], []
    for t in range(steps):
        rows = slice(t * BS, (t + 1) * BS)
        flow = columns_of(flow_hbm, at.ext_rows, 2 * panel).at[rows]
        graph = columns_of(graph_hbm, at.ext_side, 1).at[rows]
        flows.append(pltpu.make_async_copy(flow, flow_buf.at[rows], sems.at[3 + 2 * t]))
        graphs.append(pltpu.make_async_copy(graph, graph_buf.at[rows], sems.at[4 + 2 * t]))
    for copy in small:
        copy.start()
    for t in range(steps):
        flows[t].start()
        graphs[t].start()
    for copy in small:
        copy.wait()
    factor_rows(lambda column, inner: a_ref[column, 0, inner], 0, at.first, a_rows_ref)
    factor_rows(lambda column, inner: b_ref[column, 0, inner], 0, at.first, b_rows_ref)
    factor_rows(lambda column, row: c_ref[0, column, row], 0, 0, c_rows_ref)
    ext_factors[...] = a_rows_ref[:, blocks_at(at.ext_rows, 2 * panel)]
    right_factors = b_rows_ref[:, blocks_at(at.ext_side)]
    per_dot = min(2, steps)
    for t in range(0, steps, per_dot):
        rows = slice(t * BS, (t + per_dot) * BS)
        for copy in flows[t : t + per_dot] + graphs[t : t + per_dot]:
            copy.wait()
        turned = masked(flow_buf[rows, :], ext_factors[t : t + per_dot]).T
        rows_ref[:, rows] = turned
        product = dot(turned, masked(graph_buf[rows, :], right_factors[t : t + per_dot]))
        if t + per_dot < steps:
            total[...] = product if t == 0 else total[...] + product
    if steps > per_dot:
        total[...] += product
    else:
        total[...] = product
    coded = Coded(out_refs)
    for place, first in ((0, panel), (panel, at.ext_side)):
        for i in range(panel):
            coded.write(total[blocks_at(first - at.ext_rows + i), :], place + i)
    coded.finish()


def first_products(flow_t, graph, a_lines, b_lines, c_lines, widths):
    inner, width = flow_t.shape[1:]
    panel = width // 3
    return call(
        first_kernel,
        "first_products",
        [pltpu.with_memory_space_constraint(x, pltpu.HBM) for x in (a_lines, b_lines, c_lines, flow_t, graph)],
        [IN_HBM] * 5,
        [jax.ShapeDtypeStruct((HEAD + 2 * panel, w), jnp.int16) for w in widths]
        + [
            pltpu.VMEM((2 * panel, inner), flow_t.dtype),
            pltpu.VMEM((inner // BS, width), jnp.float32),
            pltpu.VMEM((inner // BS, width), jnp.float32),
            pltpu.VMEM((width // BS, panel), jnp.float32),
        ],
        [
            pltpu.VMEM((inner, BS), graph.dtype),
            pltpu.VMEM((inner, 2 * panel), flow_t.dtype),
            pltpu.VMEM((2 * panel, BS), jnp.float32),
            pltpu.VMEM((inner // BS, 2 * panel), jnp.float32),
            pltpu.SMEM(a_lines.shape, a_lines.dtype),
            pltpu.SMEM(b_lines.shape, b_lines.dtype),
            pltpu.SMEM(c_lines.shape, c_lines.dtype),
            pltpu.SemaphoreType.DMA((3 + 2 * (inner // BS),)),
        ],
        limit=PRODUCT_LIMIT,
    )


def product_kernel(half, wanted, turns, a_rows_ref, b_rows_ref, graph_ref, ext_rows_ref, side_ref, *rest):
    refs = list(rest)
    inner, panel = graph_ref.shape[1], graph_ref.shape[2] // BS // 3
    at = Sides(inner, panel)
    parts = [part for part in ("ext", "own", "int") if part in wanted]
    outs = {part: [refs.pop(0) for _ in wanted[part]] for part in parts}
    int_rows_ref = side_ref
    if turns:
        int_rows_ref = refs.pop(0)
        place = blocks_at(at.int_side, panel)
        int_rows_ref[...] = masked(side_ref[0, :, place], a_rows_ref[:, place]).T
    coded = {part: Coded(outs[part]) for part in parts if part != "own"}
    right = []
    for part in parts:
        place = blocks_at(at.columns[part] + half)
        right.append(masked(graph_ref[0, :, place], b_rows_ref[:, place]))
    right = jnp.concatenate(right, axis=1) if len(right) > 1 else right[0]
    panels = (
        (panel, ext_rows_ref.at[blocks_at(panel - at.ext_rows, panel)], {"ext": 0, "own": 0, "int": 0}),
        (at.ext_side, ext_rows_ref.at[blocks_at(at.ext_side - at.ext_rows, panel)], {"ext": panel, "own": 0}),
        (at.int_side, int_rows_ref, {"own": 0, "int": panel}),
    )
    for first, source, takers in panels:
        used = [part for part in parts if part in takers]
        if not used:
            continue
        low = parts.index(used[0]) * BS
        for i in range(panel):
            product = dot(source[i * BS : (i + 1) * BS, :], right[:, low : low + len(used) * BS])
            for j, part in enumerate(used):
                piece = product[:, j * BS : (j + 1) * BS]
                if part == "own":
                    outs[part][0][blocks_at(first + i), :] = piece
                else:
                    coded[part].write(piece, takers[part] + i)
    for part in coded:
        coded[part].finish()


def products(a_rows, b_rows, graph, ext_rows, side, half, wanted, turns=False):
    inner, width = graph.shape[1:]
    panel = width // 3
    outs = []
    for part in ("ext", "own", "int"):
        for w in wanted.get(part, ()):
            if part == "own":
                outs.append(jax.ShapeDtypeStruct((width, w), jnp.float32))
            else:
                outs.append(jax.ShapeDtypeStruct((HEAD + 2 * panel, w), jnp.int16))
    if turns:
        outs.append(pltpu.VMEM((panel, inner), graph.dtype))
    return call(
        functools.partial(product_kernel, half, wanted, turns),
        "_".join(wanted) + f"_products_{half}",
        (a_rows, b_rows, graph, ext_rows, side),
        [IN_VMEM] * 5,
        outs,
        limit=PRODUCT_LIMIT,
    )


def send_strip(send_ref, strips, power):
    rows = strips[0].shape[0]
    for j, strip in enumerate(strips):
        send_ref[HEAD + j * rows : HEAD + (j + 1) * rows, :] = code(strip, power)
    send_ref[0:HEAD, :] = jnp.broadcast_to(power, (HEAD, power.shape[1])).astype(jnp.int32).astype(jnp.int16)


def split_strips(total, rows, position, keep_ref, send_refs):
    layer = lax.axis_index("layer")
    if len(send_refs) > 1:
        keep_ref[0] = total[pl.ds(layer * rows, rows), :]
        for other, send_ref in enumerate(send_refs, 1):
            strip = total[pl.ds((layer ^ other) * rows, rows), :]
            send_strip(send_ref, [strip], powers(strip))
        return
    bit = lax.rem(layer // position, 2)
    pairs = keep_ref.shape[0]
    for j in range(pairs):
        keep_ref[j] = total[pl.ds((2 * j + bit) * rows, rows), :]
    away = [total[pl.ds((2 * j + 1 - bit) * rows, rows), :] for j in range(pairs)]
    send_strip(send_refs[0], away, functools.reduce(jnp.maximum, [powers(strip) for strip in away]))


def join_kernel(rows, half, lane, c_ref, own_ref, ext_ref, int_ref, keep_ref, *rest):
    *send_refs, total = rest
    odd = lax.rem(lax.axis_index("blk"), 2)
    panel = own_ref.shape[0] // BS // 3
    lanes = slice(lane, lane + ext_ref.shape[1])
    refs = (ext_ref, int_ref)
    from_mid, from_side = ([[(r, start + i) for i in range(panel)] for r in range(2)] for start in (0, panel))
    middle = [list(both) for both in zip(from_side[0], from_side[1])]
    ext_only, int_only = ([[part] for part in from_mid[r]] for r in range(2))
    odd_parts = int_only + middle + ext_only
    even_parts = ext_only + middle + int_only

    def add(parts):
        scale = [scales(ref[0:HEAD, :]) for ref in refs]
        for v in range(3 * panel):
            kept = c_ref[v : v + 1, half * BS + lane : half * BS + lane + ext_ref.shape[1]]
            block = own_ref[v * BS : (v + 1) * BS, lanes] * kept
            for r, i in parts[v]:
                codes = refs[r][HEAD + i * BS : HEAD + (i + 1) * BS, :]
                block += decode(codes, scale[r][i : i + 1] * kept)
            total[v * BS : (v + 1) * BS, :] = block

    @pl.when(odd == 1)
    def _():
        add(odd_parts)

    @pl.when(odd == 0)
    def _():
        add(even_parts)

    split_strips(total, rows, 1, keep_ref, send_refs)


def strips_shapes(pairs, rows, width, messages=1):
    return [
        jax.ShapeDtypeStruct((pairs, rows, width), jnp.float32),
        *[jax.ShapeDtypeStruct((HEAD + pairs * rows, width), jnp.int16)] * messages,
    ]


def join(own, ext_part, int_part, c_rows, half, lane, layers, direct):
    height = own.shape[0]
    width = int_part.shape[1]
    rows = height // layers
    return call(
        functools.partial(join_kernel, rows, half, lane),
        f"join_{half}_{lane}",
        (c_rows, own, ext_part, int_part),
        [IN_VMEM] * 4,
        strips_shapes(1, rows, width, layers - 1) if direct else strips_shapes(layers // 2, rows, width),
        [pltpu.VMEM((height, width), jnp.float32)],
    )


def halve_kernel(rows, position, kept_ref, got_ref, keep_ref, send_ref, total):
    scale = scales(got_ref[0:HEAD, :])[0:1]
    for j in range(kept_ref.shape[0]):
        codes = got_ref[HEAD + j * rows : HEAD + (j + 1) * rows, :]
        total[j * rows : (j + 1) * rows, :] = kept_ref[j] + decode(codes, scale)
    split_strips(total, rows, position, keep_ref, [send_ref])


def halve(kept, got, position, chunk):
    strips, rows, width = kept.shape
    return call(
        functools.partial(halve_kernel, rows, position),
        f"halve_{position}_{chunk}",
        (kept, got),
        [IN_VMEM] * 2,
        strips_shapes(strips // 2, rows, width),
        [pltpu.VMEM((strips * rows, width), jnp.float32)],
    )


def square_kernel(messages, place, kept_ref, *rest):
    got_refs, others, (square_ref, sums_ref) = rest[:messages], rest[messages:-2], rest[-2:]
    value = kept_ref[0]
    for ref in got_refs:
        value += decode(ref[HEAD:, :], scales(ref[0:HEAD, :])[0:1])
    square = value * value
    square_ref[...] = square
    sums = jnp.broadcast_to(jnp.sum(square, axis=0, keepdims=True), (8, square.shape[1]))
    every = [ref[...] for ref in others]
    sums_ref[...] = jnp.concatenate(every[:place] + [sums] + every[place:], axis=1)


def square(kept, got, others, place, chunk):
    _, rows, width = kept.shape
    return call(
        functools.partial(square_kernel, len(got), place),
        f"square_{chunk}",
        (kept, *got, *others),
        [IN_VMEM] * (1 + len(got) + len(others)),
        [
            jax.ShapeDtypeStruct((rows, width), jnp.float32),
            jax.ShapeDtypeStruct((8, width + sum(sums.shape[1] for sums in others)), jnp.float32),
        ],
    )


def rescale_kernel(height, count, *refs):
    squares, sums, out_ref = refs[:count], refs[count:-1], refs[-1]
    total = functools.reduce(jnp.add, [ref[0:1, :] for ref in sums])
    divisor = total / height + 1e-6
    column = 0
    for ref in squares:
        columns = slice(column, column + ref.shape[1])
        column += ref.shape[1]
        out_ref[0, :, columns] = ref[...] / divisor[:, columns]


def rescale(squares, sums, height):
    rows = squares[0].shape[0]
    width = sums[0].shape[1]
    return call(
        functools.partial(rescale_kernel, float(height), len(squares)),
        "rescale",
        (*squares, *sums),
        [IN_VMEM] * (len(squares) + len(sums)),
        jax.ShapeDtypeStruct((1, rows, width), jnp.float32),
    )


def shards(flow_t, graph, a_pattern, b_pattern, c_pattern):
    layers = lax.axis_size("layer")
    blks = lax.axis_size("blk")
    width = flow_t.shape[2]
    panel = width // 3
    a_lines = a_pattern.transpose(2, 0, 1)
    b_lines = b_pattern.transpose(2, 0, 1)
    c_lines = c_pattern.transpose(0, 2, 1)

    def other_chip(i):
        return (i + 1 if i % 2 else i - 1) % blks

    def same_chip(i):
        return i ^ 1

    halves = panel // BS
    chunks = panel // LANES
    fine = (LANES,) * (BS // LANES)
    per_half = len(fine)
    ext, ints, owns, latest = [], [], [], []

    def ordered(value):
        return after(value, latest[-1])

    def send_ext(parts):
        ext.extend(swap(part, "blk", other_chip) for part in parts)
        latest.append(parts[0])

    def send_int(parts):
        ints.extend(swap(part, "blk", same_chip) for part in parts)
        latest.append(parts[0])

    *parts, ext_rows, a_rows, b_rows, c_rows = first_products(flow_t, graph, a_lines, b_lines, c_lines, fine)
    send_ext(parts)
    wanted = {"own": (BS,), "int": fine}
    own, *parts, int_rows = products(a_rows, ordered(b_rows), graph, ext_rows, flow_t, 0, wanted, turns=True)
    owns.append(own)
    send_int(parts)

    def more_products(half):
        wanted = {"ext": fine, "int": fine}
        parts = products(a_rows, ordered(b_rows), graph, ext_rows, int_rows, half, wanted)
        send_ext(parts[:per_half])
        send_int(parts[per_half:])

    def more_own(half):
        owns.extend(products(a_rows, ordered(b_rows), graph, ext_rows, int_rows, half, {"own": (BS,)}))
        latest.append(owns[-1])

    strips, squares, sums = [], {}, {}

    def add_up(chunk):
        half, lane = divmod(chunk, per_half)
        direct = chunk >= chunks - DIRECT and layers <= 4
        kept, *sends = join(
            owns[half], ext[chunk], ints[chunk], ordered(c_rows), half, lane * LANES, layers, direct
        )
        latest.append(kept)
        strips.append((kept, [swap(send, "layer", lambda i: i ^ other) for other, send in enumerate(sends, 1)]))

    def scatter(chunk):
        kept, got = strips[chunk]
        position = 1
        while kept.shape[0] > 1:
            position *= 2
            kept, send = halve(ordered(kept), got[0], position, chunk)
            latest.append(kept)
            got = [swap(send, "layer", lambda i: i ^ position)]
        strips[chunk] = kept, got

    def finish(chunk):
        kept, got = strips[chunk]
        others, place = ([], 0)
        if len(squares) == chunks - 1:
            others, place = [sums[i] for i in sorted(sums)], chunk
        squares[chunk], sums[chunk] = square(ordered(kept), got, others, place, chunk)
        latest.append(sums[chunk])

    add_up(0)
    for half in range(1, halves):
        more_products(half)
    add_up(1)
    more_own(1)
    scatter(0)
    add_up(2)
    scatter(1)
    add_up(3)
    scatter(2)
    scatter(3)
    finish(1)
    finish(0)
    finish(3)
    finish(2)

    squares = [squares[i] for i in sorted(squares)]
    mine = sums[2]
    others = [swap(mine, "layer", lambda i: i ^ other) for other in range(1, layers)]
    return rescale(squares, [mine, *others], width)


def solution(mesh):
    placed = (
        P("blk", "layer", None),
        P("blk", "layer", None),
        P("blk", None, None),
        P("blk", None, None),
        P("blk", None, None),
    )
    return jax.shard_map(
        shards, mesh=mesh, in_specs=placed, out_specs=P("blk", "layer", None), check_vma=False
    )
```

```python
import functools

import jax
import jax.numpy as jnp
from jax import lax
from jax.experimental import pallas as pl
from jax.experimental.pallas import tpu as pltpu
from jax.sharding import PartitionSpec as P

BS = 256
LANES = 128
HEAD = 16
STEPS = 256.0
TOP = 65534.0
LN2 = 0.6931471805599453
DIRECT = 1
PRODUCT_LIMIT = 24000000
SMALL_LIMIT = 8 * 1024 * 1024
IN_VMEM = pl.BlockSpec(memory_space=pltpu.VMEM)
IN_HBM = pl.BlockSpec(memory_space=pltpu.HBM)


def swap(block, axis, partner):
    return lax.ppermute(block, axis, [(partner(i), i) for i in range(lax.axis_size(axis))])


def after(value, *others):
    return lax.optimization_barrier((value, *others))[0]


def call(kernel, name, operands, in_specs, out_shape, scratch_shapes=(), limit=SMALL_LIMIT):
    return pl.pallas_call(
        kernel,
        out_shape=out_shape,
        in_specs=in_specs,
        out_specs=jax.tree.map(lambda _: IN_VMEM, out_shape),
        scratch_shapes=list(scratch_shapes),
        compiler_params=pltpu.CompilerParams(vmem_limit_bytes=limit),
        cost_estimate=pl.CostEstimate(flops=1, bytes_accessed=1, transcendentals=0),
        name=name,
    )(*operands)


def powers(values):
    largest = jnp.maximum(jnp.max(values, axis=0, keepdims=True), 1e-3)
    return jnp.floor(jnp.log(largest) * (STEPS / LN2)) + 2.0


def code(values, power):
    scaled = values * (TOP * jnp.exp(power * (-LN2 / STEPS)))
    return ((scaled + 0.5).astype(jnp.int32) - 32767).astype(jnp.int16)


def scales(head):
    return jnp.exp(head.astype(jnp.int32).astype(jnp.float32) * (LN2 / STEPS)) * (1.0 / TOP)


def decode(codes, scale):
    return (codes.astype(jnp.int32) + 32767).astype(jnp.float32) * scale


def factor_rows(pattern, column, first, ref):
    place = lax.broadcasted_iota(jnp.int32, (1, ref.shape[1]), 1) // BS
    for u in range(ref.shape[0]):
        row = jnp.zeros((1, ref.shape[1]), jnp.float32)
        for v in range(ref.shape[1] // BS):
            row = jnp.where(place == v, pattern(column + v, first + u).astype(jnp.float32), row)
        ref[u : u + 1, :] = row


def masked(values, factors):
    parts = [
        values[u * BS : (u + 1) * BS] * factors[u : u + 1].astype(values.dtype) for u in range(values.shape[0] // BS)
    ]
    return jnp.concatenate(parts, axis=0) if len(parts) > 1 else parts[0]


def dot(left_side, right_side):
    return lax.dot_general(
        left_side, right_side, (((1,), (0,)), ((), ())), preferred_element_type=jnp.float32
    )


def columns_of(ref, start, count):
    return ref.at[0, :, pl.ds(pl.multiple_of(start * BS, BS), count * BS)]


def blocks_at(block, count=1):
    return pl.ds(pl.multiple_of(block * BS, BS), count * BS)


class Sides:
    def __init__(self, inner, panel):
        odd = lax.rem(lax.axis_index("blk"), 2)
        self.panel = panel
        self.first = lax.axis_index("layer") * (inner // BS)
        self.ext_side, self.int_side = odd * (2 * panel), (1 - odd) * (2 * panel)
        self.ext_rows = odd * panel
        self.columns = {"ext": self.ext_side, "own": panel, "int": self.int_side}


class Coded:
    def __init__(self, refs):
        self.refs = refs
        self.heads = [jnp.zeros((HEAD, ref.shape[1]), jnp.float32) for ref in refs]

    def write_all(self, product, place):
        for i in range(product.shape[0] // BS):
            self.write(product[i * BS : (i + 1) * BS], place + i)

    def write(self, product, place):
        column = 0
        for c, ref in enumerate(self.refs):
            chunk = product[:, column : column + ref.shape[1]]
            column += ref.shape[1]
            power = powers(chunk)
            ref[HEAD + place * BS : HEAD + (place + 1) * BS, :] = code(chunk, power)
            line = lax.broadcasted_iota(jnp.int32, self.heads[c].shape, 0)
            self.heads[c] = jnp.where(line == place, power, self.heads[c])

    def finish(self):
        for ref, head in zip(self.refs, self.heads):
            ref[0:HEAD, :] = head.astype(jnp.int32).astype(jnp.int16)


def first_kernel(a_hbm, b_hbm, c_hbm, flow_hbm, graph_hbm, *rest):
    out_refs, rest = rest[:-12], rest[-12:]
    rows_ref, a_rows_ref, b_rows_ref, c_rows_ref, graph_buf, flow_buf, total, ext_factors, a_ref, b_ref, c_ref, sems = rest
    inner, panel = flow_buf.shape[0], flow_buf.shape[1] // BS // 2
    at = Sides(inner, panel)
    steps = inner // BS
    small = [
        pltpu.make_async_copy(pattern, ref, sems.at[i])
        for i, (pattern, ref) in enumerate(((a_hbm, a_ref), (b_hbm, b_ref), (c_hbm, c_ref)))
    ]
    flows, graphs = [], []
    for t in range(steps):
        rows = slice(t * BS, (t + 1) * BS)
        flow = columns_of(flow_hbm, at.ext_rows, 2 * panel).at[rows]
        graph = columns_of(graph_hbm, at.ext_side, 1).at[rows]
        flows.append(pltpu.make_async_copy(flow, flow_buf.at[rows], sems.at[3 + 2 * t]))
        graphs.append(pltpu.make_async_copy(graph, graph_buf.at[rows], sems.at[4 + 2 * t]))
    for copy in small:
        copy.start()
    for t in range(steps):
        flows[t].start()
        graphs[t].start()
    for copy in small:
        copy.wait()
    factor_rows(lambda column, inner: a_ref[column, 0, inner], 0, at.first, a_rows_ref)
    factor_rows(lambda column, inner: b_ref[column, 0, inner], 0, at.first, b_rows_ref)
    factor_rows(lambda column, row: c_ref[0, column, row], 0, 0, c_rows_ref)
    ext_factors[...] = a_rows_ref[:, blocks_at(at.ext_rows, 2 * panel)]
    right_factors = b_rows_ref[:, blocks_at(at.ext_side)]
    per_dot = min(2, steps)
    for t in range(0, steps, per_dot):
        rows = slice(t * BS, (t + per_dot) * BS)
        for copy in flows[t : t + per_dot] + graphs[t : t + per_dot]:
            copy.wait()
        turned = masked(flow_buf[rows, :], ext_factors[t : t + per_dot]).T
        rows_ref[:, rows] = turned
        product = dot(turned, masked(graph_buf[rows, :], right_factors[t : t + per_dot]))
        if t + per_dot < steps:
            total[...] = product if t == 0 else total[...] + product
    if steps > per_dot:
        total[...] += product
    else:
        total[...] = product
    coded = Coded(out_refs)
    for place, first in ((0, panel), (panel, at.ext_side)):
        for i in range(panel):
            coded.write(total[blocks_at(first - at.ext_rows + i), :], place + i)
    coded.finish()


def first_products(flow_t, graph, a_lines, b_lines, c_lines, widths):
    inner, width = flow_t.shape[1:]
    panel = width // 3
    return call(
        first_kernel,
        "first_products",
        [pltpu.with_memory_space_constraint(x, pltpu.HBM) for x in (a_lines, b_lines, c_lines, flow_t, graph)],
        [IN_HBM] * 5,
        [jax.ShapeDtypeStruct((HEAD + 2 * panel, w), jnp.int16) for w in widths]
        + [
            pltpu.VMEM((2 * panel, inner), flow_t.dtype),
            pltpu.VMEM((inner // BS, width), jnp.float32),
            pltpu.VMEM((inner // BS, width), jnp.float32),
            pltpu.VMEM((width // BS, panel), jnp.float32),
        ],
        [
            pltpu.VMEM((inner, BS), graph.dtype),
            pltpu.VMEM((inner, 2 * panel), flow_t.dtype),
            pltpu.VMEM((2 * panel, BS), jnp.float32),
            pltpu.VMEM((inner // BS, 2 * panel), jnp.float32),
            pltpu.SMEM(a_lines.shape, a_lines.dtype),
            pltpu.SMEM(b_lines.shape, b_lines.dtype),
            pltpu.SMEM(c_lines.shape, c_lines.dtype),
            pltpu.SemaphoreType.DMA((3 + 2 * (inner // BS),)),
        ],
        limit=PRODUCT_LIMIT,
    )


def product_kernel(half, wanted, turns, a_rows_ref, b_rows_ref, graph_ref, ext_rows_ref, side_ref, *rest):
    refs = list(rest)
    inner, panel = graph_ref.shape[1], graph_ref.shape[2] // BS // 3
    at = Sides(inner, panel)
    parts = [part for part in ("ext", "own", "int") if part in wanted]
    outs = {part: [refs.pop(0) for _ in wanted[part]] for part in parts}
    int_rows_ref = side_ref
    if turns:
        int_rows_ref = refs.pop(0)
        place = blocks_at(at.int_side, panel)
        int_rows_ref[...] = masked(side_ref[0, :, place], a_rows_ref[:, place]).T
    coded = {part: Coded(outs[part]) for part in parts if part != "own"}
    right = []
    for part in parts:
        place = blocks_at(at.columns[part] + half)
        right.append(masked(graph_ref[0, :, place], b_rows_ref[:, place]))
    right = jnp.concatenate(right, axis=1) if len(right) > 1 else right[0]
    panels = (
        (panel, ext_rows_ref.at[blocks_at(panel - at.ext_rows, panel)], {"ext": 0, "own": 0, "int": 0}),
        (at.ext_side, ext_rows_ref.at[blocks_at(at.ext_side - at.ext_rows, panel)], {"ext": panel, "own": 0}),
        (at.int_side, int_rows_ref, {"own": 0, "int": panel}),
    )
    for first, source, takers in panels:
        used = [part for part in parts if part in takers]
        if not used:
            continue
        low = parts.index(used[0]) * BS
        for i in range(panel):
            product = dot(source[i * BS : (i + 1) * BS, :], right[:, low : low + len(used) * BS])
            for j, part in enumerate(used):
                piece = product[:, j * BS : (j + 1) * BS]
                if part == "own":
                    outs[part][0][blocks_at(first + i), :] = piece
                else:
                    coded[part].write(piece, takers[part] + i)
    for part in coded:
        coded[part].finish()


def products(a_rows, b_rows, graph, ext_rows, side, half, wanted, turns=False):
    inner, width = graph.shape[1:]
    panel = width // 3
    outs = []
    for part in ("ext", "own", "int"):
        for w in wanted.get(part, ()):
            if part == "own":
                outs.append(jax.ShapeDtypeStruct((width, w), jnp.float32))
            else:
                outs.append(jax.ShapeDtypeStruct((HEAD + 2 * panel, w), jnp.int16))
    if turns:
        outs.append(pltpu.VMEM((panel, inner), graph.dtype))
    return call(
        functools.partial(product_kernel, half, wanted, turns),
        "_".join(wanted) + f"_products_{half}",
        (a_rows, b_rows, graph, ext_rows, side),
        [IN_VMEM] * 5,
        outs,
        limit=PRODUCT_LIMIT,
    )


def send_strip(send_ref, strips, power):
    rows = strips[0].shape[0]
    for j, strip in enumerate(strips):
        send_ref[HEAD + j * rows : HEAD + (j + 1) * rows, :] = code(strip, power)
    send_ref[0:HEAD, :] = jnp.broadcast_to(power, (HEAD, power.shape[1])).astype(jnp.int32).astype(jnp.int16)


def split_strips(total, rows, position, keep_ref, send_refs):
    layer = lax.axis_index("layer")
    if len(send_refs) > 1:
        keep_ref[0] = total[pl.ds(layer * rows, rows), :]
        for other, send_ref in enumerate(send_refs, 1):
            strip = total[pl.ds((layer ^ other) * rows, rows), :]
            send_strip(send_ref, [strip], powers(strip))
        return
    bit = lax.rem(layer // position, 2)
    pairs = keep_ref.shape[0]
    for j in range(pairs):
        keep_ref[j] = total[pl.ds((2 * j + bit) * rows, rows), :]
    away = [total[pl.ds((2 * j + 1 - bit) * rows, rows), :] for j in range(pairs)]
    send_strip(send_refs[0], away, functools.reduce(jnp.maximum, [powers(strip) for strip in away]))


def join_kernel(rows, half, lane, c_ref, own_ref, ext_ref, int_ref, keep_ref, *rest):
    *send_refs, total = rest
    odd = lax.rem(lax.axis_index("blk"), 2)
    panel = own_ref.shape[0] // BS // 3
    lanes = slice(lane, lane + ext_ref.shape[1])
    refs = (ext_ref, int_ref)
    from_mid, from_side = ([[(r, start + i) for i in range(panel)] for r in range(2)] for start in (0, panel))
    middle = [list(both) for both in zip(from_side[0], from_side[1])]
    ext_only, int_only = ([[part] for part in from_mid[r]] for r in range(2))
    odd_parts = int_only + middle + ext_only
    even_parts = ext_only + middle + int_only

    def add(parts):
        scale = [scales(ref[0:HEAD, :]) for ref in refs]
        for v in range(3 * panel):
            kept = c_ref[v : v + 1, half * BS + lane : half * BS + lane + ext_ref.shape[1]]
            block = own_ref[v * BS : (v + 1) * BS, lanes] * kept
            for r, i in parts[v]:
                codes = refs[r][HEAD + i * BS : HEAD + (i + 1) * BS, :]
                block += decode(codes, scale[r][i : i + 1] * kept)
            total[v * BS : (v + 1) * BS, :] = block

    @pl.when(odd == 1)
    def _():
        add(odd_parts)

    @pl.when(odd == 0)
    def _():
        add(even_parts)

    split_strips(total, rows, 1, keep_ref, send_refs)


def strips_shapes(pairs, rows, width, messages=1):
    return [
        jax.ShapeDtypeStruct((pairs, rows, width), jnp.float32),
        *[jax.ShapeDtypeStruct((HEAD + pairs * rows, width), jnp.int16)] * messages,
    ]


def join(own, ext_part, int_part, c_rows, half, lane, layers, direct):
    height = own.shape[0]
    width = int_part.shape[1]
    rows = height // layers
    return call(
        functools.partial(join_kernel, rows, half, lane),
        f"join_{half}_{lane}",
        (c_rows, own, ext_part, int_part),
        [IN_VMEM] * 4,
        strips_shapes(1, rows, width, layers - 1) if direct else strips_shapes(layers // 2, rows, width),
        [pltpu.VMEM((height, width), jnp.float32)],
    )


def halve_kernel(rows, position, kept_ref, got_ref, keep_ref, send_ref, total):
    scale = scales(got_ref[0:HEAD, :])[0:1]
    for j in range(kept_ref.shape[0]):
        codes = got_ref[HEAD + j * rows : HEAD + (j + 1) * rows, :]
        total[j * rows : (j + 1) * rows, :] = kept_ref[j] + decode(codes, scale)
    split_strips(total, rows, position, keep_ref, [send_ref])


def halve(kept, got, position, chunk):
    strips, rows, width = kept.shape
    return call(
        functools.partial(halve_kernel, rows, position),
        f"halve_{position}_{chunk}",
        (kept, got),
        [IN_VMEM] * 2,
        strips_shapes(strips // 2, rows, width),
        [pltpu.VMEM((strips * rows, width), jnp.float32)],
    )


def square_kernel(messages, place, kept_ref, *rest):
    got_refs, others, (square_ref, sums_ref) = rest[:messages], rest[messages:-2], rest[-2:]
    value = kept_ref[0]
    for ref in got_refs:
        value += decode(ref[HEAD:, :], scales(ref[0:HEAD, :])[0:1])
    square = value * value
    square_ref[...] = square
    sums = jnp.broadcast_to(jnp.sum(square, axis=0, keepdims=True), (8, square.shape[1]))
    every = [ref[...] for ref in others]
    sums_ref[...] = jnp.concatenate(every[:place] + [sums] + every[place:], axis=1)


def square(kept, got, others, place, chunk):
    _, rows, width = kept.shape
    return call(
        functools.partial(square_kernel, len(got), place),
        f"square_{chunk}",
        (kept, *got, *others),
        [IN_VMEM] * (1 + len(got) + len(others)),
        [
            jax.ShapeDtypeStruct((rows, width), jnp.float32),
            jax.ShapeDtypeStruct((8, width + sum(sums.shape[1] for sums in others)), jnp.float32),
        ],
    )


def rescale_kernel(height, count, *refs):
    squares, sums, out_ref = refs[:count], refs[count:-1], refs[-1]
    total = functools.reduce(jnp.add, [ref[0:1, :] for ref in sums])
    divisor = total / height + 1e-6
    column = 0
    for ref in squares:
        columns = slice(column, column + ref.shape[1])
        column += ref.shape[1]
        out_ref[0, :, columns] = ref[...] / divisor[:, columns]


def rescale(squares, sums, height):
    rows = squares[0].shape[0]
    width = sums[0].shape[1]
    return call(
        functools.partial(rescale_kernel, float(height), len(squares)),
        "rescale",
        (*squares, *sums),
        [IN_VMEM] * (len(squares) + len(sums)),
        jax.ShapeDtypeStruct((1, rows, width), jnp.float32),
    )


def shards(flow_t, graph, a_pattern, b_pattern, c_pattern):
    layers = lax.axis_size("layer")
    blks = lax.axis_size("blk")
    width = flow_t.shape[2]
    panel = width // 3
    a_lines = a_pattern.transpose(2, 0, 1)
    b_lines = b_pattern.transpose(2, 0, 1)
    c_lines = c_pattern.transpose(0, 2, 1)

    def other_chip(i):
        return (i + 1 if i % 2 else i - 1) % blks

    def same_chip(i):
        return i ^ 1

    halves = panel // BS
    chunks = panel // LANES
    fine = (LANES,) * (BS // LANES)
    per_half = len(fine)
    ext, ints, owns, latest = [], [], [], []

    def ordered(value):
        return after(value, latest[-1])

    def send_ext(parts):
        ext.extend(swap(part, "blk", other_chip) for part in parts)
        latest.append(parts[0])

    def send_int(parts):
        ints.extend(swap(part, "blk", same_chip) for part in parts)
        latest.append(parts[0])

    *parts, ext_rows, a_rows, b_rows, c_rows = first_products(flow_t, graph, a_lines, b_lines, c_lines, fine)
    send_ext(parts)
    wanted = {"own": (BS,), "int": fine}
    own, *parts, int_rows = products(a_rows, ordered(b_rows), graph, ext_rows, flow_t, 0, wanted, turns=True)
    owns.append(own)
    send_int(parts)

    def more_products(half):
        wanted = {"ext": fine, "int": fine}
        parts = products(a_rows, ordered(b_rows), graph, ext_rows, int_rows, half, wanted)
        send_ext(parts[:per_half])
        send_int(parts[per_half:])

    def more_own(half):
        owns.extend(products(a_rows, ordered(b_rows), graph, ext_rows, int_rows, half, {"own": (BS,)}))
        latest.append(owns[-1])

    strips, squares, sums = [], {}, {}

    def add_up(chunk):
        half, lane = divmod(chunk, per_half)
        direct = chunk >= chunks - DIRECT and layers <= 4
        kept, *sends = join(
            owns[half], ext[chunk], ints[chunk], ordered(c_rows), half, lane * LANES, layers, direct
        )
        latest.append(kept)
        strips.append((kept, [swap(send, "layer", lambda i: i ^ other) for other, send in enumerate(sends, 1)]))

    def scatter(chunk):
        kept, got = strips[chunk]
        position = 1
        while kept.shape[0] > 1:
            position *= 2
            kept, send = halve(ordered(kept), got[0], position, chunk)
            latest.append(kept)
            got = [swap(send, "layer", lambda i: i ^ position)]
        strips[chunk] = kept, got

    def finish(chunk):
        kept, got = strips[chunk]
        others, place = ([], 0)
        if len(squares) == chunks - 1:
            others, place = [sums[i] for i in sorted(sums)], chunk
        squares[chunk], sums[chunk] = square(ordered(kept), got, others, place, chunk)
        latest.append(sums[chunk])

    add_up(0)
    more_products(1)
    scatter(0)
    add_up(1)
    more_own(1)
    finish(0)
    add_up(2)
    scatter(1)
    add_up(3)
    finish(1)
    scatter(2)
    scatter(3)
    finish(3)
    finish(2)

    squares = [squares[i] for i in sorted(squares)]
    mine = sums[2]
    others = [swap(mine, "layer", lambda i: i ^ other) for other in range(1, layers)]
    return rescale(squares, [mine, *others], width)


def solution(mesh):
    placed = (
        P("blk", "layer", None),
        P("blk", "layer", None),
        P("blk", None, None),
        P("blk", None, None),
        P("blk", None, None),
    )
    return jax.shard_map(
        shards, mesh=mesh, in_specs=placed, out_specs=P("blk", "layer", None), check_vma=False
    )
```

```python
import functools

import jax
import jax.numpy as jnp
from jax import lax
from jax.experimental import pallas as pl
from jax.experimental.pallas import tpu as pltpu
from jax.sharding import PartitionSpec as P

BS = 256
LANES = 128
HEAD = 16
STEPS = 256.0
TOP = 65534.0
LN2 = 0.6931471805599453
PRODUCT_LIMIT = 24000000
SMALL_LIMIT = 8 * 1024 * 1024
IN_VMEM = pl.BlockSpec(memory_space=pltpu.VMEM)
IN_HBM = pl.BlockSpec(memory_space=pltpu.HBM)


def swap(block, axis, partner):
    return lax.ppermute(block, axis, [(partner(i), i) for i in range(lax.axis_size(axis))])


def after(value, *others):
    return lax.optimization_barrier((value, *others))[0]


def call(kernel, name, operands, in_specs, out_shape, scratch_shapes=(), limit=SMALL_LIMIT):
    return pl.pallas_call(
        kernel,
        out_shape=out_shape,
        in_specs=in_specs,
        out_specs=jax.tree.map(lambda _: IN_VMEM, out_shape),
        scratch_shapes=list(scratch_shapes),
        compiler_params=pltpu.CompilerParams(vmem_limit_bytes=limit),
        cost_estimate=pl.CostEstimate(flops=1, bytes_accessed=1, transcendentals=0),
        name=name,
    )(*operands)


def powers(values):
    largest = jnp.maximum(jnp.max(values, axis=0, keepdims=True), 1e-3)
    return jnp.floor(jnp.log(largest) * (STEPS / LN2)) + 2.0


def code(values, power):
    scaled = values * (TOP * jnp.exp(power * (-LN2 / STEPS)))
    return ((scaled + 0.5).astype(jnp.int32) - 32767).astype(jnp.int16)


def scales(head):
    return jnp.exp(head.astype(jnp.int32).astype(jnp.float32) * (LN2 / STEPS)) * (1.0 / TOP)


def decode(codes, scale):
    return (codes.astype(jnp.int32) + 32767).astype(jnp.float32) * scale


def factor_rows(pattern, column, first, ref):
    place = lax.broadcasted_iota(jnp.int32, (1, ref.shape[1]), 1) // BS
    for u in range(ref.shape[0]):
        row = jnp.zeros((1, ref.shape[1]), jnp.float32)
        for v in range(ref.shape[1] // BS):
            row = jnp.where(place == v, pattern(column + v, first + u).astype(jnp.float32), row)
        ref[u : u + 1, :] = row


def masked(values, factors):
    parts = [
        values[u * BS : (u + 1) * BS] * factors[u : u + 1].astype(values.dtype) for u in range(values.shape[0] // BS)
    ]
    return jnp.concatenate(parts, axis=0) if len(parts) > 1 else parts[0]


def dot(left_side, right_side):
    return lax.dot_general(
        left_side, right_side, (((1,), (0,)), ((), ())), preferred_element_type=jnp.float32
    )


def columns_of(ref, start, count):
    return ref.at[0, :, pl.ds(pl.multiple_of(start * BS, BS), count * BS)]


def blocks_at(block, count=1):
    return pl.ds(pl.multiple_of(block * BS, BS), count * BS)


class Sides:
    def __init__(self, inner, panel):
        odd = lax.rem(lax.axis_index("blk"), 2)
        self.panel = panel
        self.first = lax.axis_index("layer") * (inner // BS)
        self.ext_side, self.int_side = odd * (2 * panel), (1 - odd) * (2 * panel)
        self.ext_rows = odd * panel
        self.columns = {"ext": self.ext_side, "own": panel, "int": self.int_side}


class Coded:
    def __init__(self, refs):
        self.refs = refs
        self.heads = [jnp.zeros((HEAD, ref.shape[1]), jnp.float32) for ref in refs]

    def write_all(self, product, place):
        for i in range(product.shape[0] // BS):
            self.write(product[i * BS : (i + 1) * BS], place + i)

    def write(self, product, place):
        column = 0
        for c, ref in enumerate(self.refs):
            chunk = product[:, column : column + ref.shape[1]]
            column += ref.shape[1]
            power = powers(chunk)
            ref[HEAD + place * BS : HEAD + (place + 1) * BS, :] = code(chunk, power)
            line = lax.broadcasted_iota(jnp.int32, self.heads[c].shape, 0)
            self.heads[c] = jnp.where(line == place, power, self.heads[c])

    def finish(self):
        for ref, head in zip(self.refs, self.heads):
            ref[0:HEAD, :] = head.astype(jnp.int32).astype(jnp.int16)


def first_kernel(a_hbm, b_hbm, c_hbm, flow_hbm, graph_hbm, *rest):
    out_refs, rest = rest[:-12], rest[-12:]
    rows_ref, a_rows_ref, b_rows_ref, c_rows_ref, graph_buf, flow_buf, total, ext_factors, a_ref, b_ref, c_ref, sems = rest
    inner, panel = flow_buf.shape[0], flow_buf.shape[1] // BS // 2
    at = Sides(inner, panel)
    steps = inner // BS
    small = [
        pltpu.make_async_copy(pattern, ref, sems.at[i])
        for i, (pattern, ref) in enumerate(((a_hbm, a_ref), (b_hbm, b_ref), (c_hbm, c_ref)))
    ]
    flows, graphs = [], []
    for t in range(steps):
        rows = slice(t * BS, (t + 1) * BS)
        flow = columns_of(flow_hbm, at.ext_rows, 2 * panel).at[rows]
        graph = columns_of(graph_hbm, at.ext_side, 1).at[rows]
        flows.append(pltpu.make_async_copy(flow, flow_buf.at[rows], sems.at[3 + 2 * t]))
        graphs.append(pltpu.make_async_copy(graph, graph_buf.at[rows], sems.at[4 + 2 * t]))
    for copy in small:
        copy.start()
    for t in range(steps):
        flows[t].start()
        graphs[t].start()
    for copy in small:
        copy.wait()
    factor_rows(lambda column, inner: a_ref[column, 0, inner], 0, at.first, a_rows_ref)
    factor_rows(lambda column, inner: b_ref[column, 0, inner], 0, at.first, b_rows_ref)
    factor_rows(lambda column, row: c_ref[0, column, row], 0, 0, c_rows_ref)
    ext_factors[...] = a_rows_ref[:, blocks_at(at.ext_rows, 2 * panel)]
    right_factors = b_rows_ref[:, blocks_at(at.ext_side)]
    per_dot = min(2, steps)
    for t in range(0, steps, per_dot):
        rows = slice(t * BS, (t + per_dot) * BS)
        for copy in flows[t : t + per_dot] + graphs[t : t + per_dot]:
            copy.wait()
        turned = masked(flow_buf[rows, :], ext_factors[t : t + per_dot]).T
        rows_ref[:, rows] = turned
        product = dot(turned, masked(graph_buf[rows, :], right_factors[t : t + per_dot]))
        if t + per_dot < steps:
            total[...] = product if t == 0 else total[...] + product
    if steps > per_dot:
        total[...] += product
    else:
        total[...] = product
    coded = Coded(out_refs)
    for place, first in ((0, panel), (panel, at.ext_side)):
        for i in range(panel):
            coded.write(total[blocks_at(first - at.ext_rows + i), :], place + i)
    coded.finish()


def first_products(flow_t, graph, a_lines, b_lines, c_lines):
    inner, width = flow_t.shape[1:]
    panel = width // 3
    return call(
        first_kernel,
        "first_products",
        [pltpu.with_memory_space_constraint(x, pltpu.HBM) for x in (a_lines, b_lines, c_lines, flow_t, graph)],
        [IN_HBM] * 5,
        [
            jax.ShapeDtypeStruct((HEAD + 2 * panel, BS), jnp.int16),
            pltpu.VMEM((2 * panel, inner), flow_t.dtype),
            pltpu.VMEM((inner // BS, width), jnp.float32),
            pltpu.VMEM((inner // BS, width), jnp.float32),
            pltpu.VMEM((width // BS, panel), jnp.float32),
        ],
        [
            pltpu.VMEM((inner, BS), graph.dtype),
            pltpu.VMEM((inner, 2 * panel), flow_t.dtype),
            pltpu.VMEM((2 * panel, BS), jnp.float32),
            pltpu.VMEM((inner // BS, 2 * panel), jnp.float32),
            pltpu.SMEM(a_lines.shape, a_lines.dtype),
            pltpu.SMEM(b_lines.shape, b_lines.dtype),
            pltpu.SMEM(c_lines.shape, c_lines.dtype),
            pltpu.SemaphoreType.DMA((3 + 2 * (inner // BS),)),
        ],
        limit=PRODUCT_LIMIT,
    )


def product_kernel(half, wanted, turns, a_rows_ref, b_rows_ref, graph_ref, ext_rows_ref, side_ref, *rest):
    refs = list(rest)
    inner, panel = graph_ref.shape[1], graph_ref.shape[2] // BS // 3
    at = Sides(inner, panel)
    parts = [part for part in ("ext", "own", "int") if part in wanted]
    outs = {part: [refs.pop(0) for _ in wanted[part]] for part in parts}
    int_rows_ref = side_ref
    if turns:
        int_rows_ref = refs.pop(0)
        place = blocks_at(at.int_side, panel)
        int_rows_ref[...] = masked(side_ref[0, :, place], a_rows_ref[:, place]).T
    coded = {part: Coded(outs[part]) for part in parts if part != "own"}
    right = []
    for part in parts:
        place = blocks_at(at.columns[part] + half)
        right.append(masked(graph_ref[0, :, place], b_rows_ref[:, place]))
    right = jnp.concatenate(right, axis=1) if len(right) > 1 else right[0]
    panels = (
        (panel, ext_rows_ref.at[blocks_at(panel - at.ext_rows, panel)], {"ext": 0, "own": 0, "int": 0}),
        (at.ext_side, ext_rows_ref.at[blocks_at(at.ext_side - at.ext_rows, panel)], {"ext": panel, "own": 0}),
        (at.int_side, int_rows_ref, {"own": 0, "int": panel}),
    )
    for first, source, takers in panels:
        used = [part for part in parts if part in takers]
        if not used:
            continue
        low = parts.index(used[0]) * BS
        for i in range(panel):
            product = dot(source[i * BS : (i + 1) * BS, :], right[:, low : low + len(used) * BS])
            for j, part in enumerate(used):
                piece = product[:, j * BS : (j + 1) * BS]
                if part == "own":
                    outs[part][0][blocks_at(first + i), :] = piece
                else:
                    coded[part].write(piece, takers[part] + i)
    for part in coded:
        coded[part].finish()


def products(a_rows, b_rows, graph, ext_rows, side, half, wanted, turns=False):
    inner, width = graph.shape[1:]
    panel = width // 3
    outs = []
    for part in ("ext", "own", "int"):
        for w in wanted.get(part, ()):
            if part == "own":
                outs.append(jax.ShapeDtypeStruct((width, w), jnp.float32))
            else:
                outs.append(jax.ShapeDtypeStruct((HEAD + 2 * panel, w), jnp.int16))
    if turns:
        outs.append(pltpu.VMEM((panel, inner), graph.dtype))
    return call(
        functools.partial(product_kernel, half, wanted, turns),
        "_".join(wanted) + f"_products_{half}",
        (a_rows, b_rows, graph, ext_rows, side),
        [IN_VMEM] * 5,
        outs,
        limit=PRODUCT_LIMIT,
    )


def send_strip(send_ref, strips, power):
    rows = strips[0].shape[0]
    for j, strip in enumerate(strips):
        send_ref[HEAD + j * rows : HEAD + (j + 1) * rows, :] = code(strip, power)
    send_ref[0:HEAD, :] = jnp.broadcast_to(power, (HEAD, power.shape[1])).astype(jnp.int32).astype(jnp.int16)


def split_strips(total, rows, position, keep_ref, send_ref):
    bit = lax.rem(lax.axis_index("layer") // position, 2)
    pairs = keep_ref.shape[0]
    for j in range(pairs):
        keep_ref[j] = total[pl.ds((2 * j + bit) * rows, rows), :]
    away = [total[pl.ds((2 * j + 1 - bit) * rows, rows), :] for j in range(pairs)]
    power = functools.reduce(jnp.maximum, [powers(strip) for strip in away])
    for j, strip in enumerate(away):
        send_ref[HEAD + j * rows : HEAD + (j + 1) * rows, :] = code(strip, power)
    send_ref[0:HEAD, :] = jnp.broadcast_to(power, (HEAD, power.shape[1])).astype(jnp.int32).astype(jnp.int16)


def join_kernel(rows, half, lanes, c_ref, own_ref, ext_ref, int_ref, keep_ref, send_ref, total):
    odd = lax.rem(lax.axis_index("blk"), 2)
    panel = own_ref.shape[0] // BS // 3
    refs = (ext_ref.at[:, lanes], int_ref.at[:, lanes])
    c_lanes = slice(half * BS + lanes.start, half * BS + lanes.stop)
    from_mid, from_side = ([[(r, start + i) for i in range(panel)] for r in range(2)] for start in (0, panel))
    middle = [list(both) for both in zip(from_side[0], from_side[1])]
    ext_only, int_only = ([[part] for part in from_mid[r]] for r in range(2))
    odd_parts = int_only + middle + ext_only
    even_parts = ext_only + middle + int_only

    def add(parts):
        scale = [scales(ref[0:HEAD, :]) for ref in refs]
        for v in range(3 * panel):
            kept = c_ref[v : v + 1, c_lanes]
            block = own_ref[v * BS : (v + 1) * BS, lanes] * kept
            for r, i in parts[v]:
                codes = refs[r][HEAD + i * BS : HEAD + (i + 1) * BS, :]
                block += decode(codes, scale[r][i : i + 1] * kept)
            total[v * BS : (v + 1) * BS, :] = block

    @pl.when(odd == 1)
    def _():
        add(odd_parts)

    @pl.when(odd == 0)
    def _():
        add(even_parts)

    split_strips(total, rows, 1, keep_ref, send_ref)


def strips_shapes(pairs, rows, width):
    return [
        jax.ShapeDtypeStruct((pairs, rows, width), jnp.float32),
        jax.ShapeDtypeStruct((HEAD + pairs * rows, width), jnp.int16),
    ]


def join(own, ext_part, lane, int_part, c_rows, half, width, layers):
    height = own.shape[0]
    rows = height // layers
    return call(
        functools.partial(join_kernel, rows, half, slice(lane, lane + width)),
        f"join_{half}_{lane}",
        (c_rows, own, ext_part, int_part),
        [IN_VMEM] * 4,
        strips_shapes(layers // 2, rows, width),
        [pltpu.VMEM((height, width), jnp.float32)],
    )


def halve_kernel(rows, position, kept_ref, got_ref, keep_ref, send_ref, total):
    scale = scales(got_ref[0:HEAD, :])[0:1]
    for j in range(kept_ref.shape[0]):
        codes = got_ref[HEAD + j * rows : HEAD + (j + 1) * rows, :]
        total[j * rows : (j + 1) * rows, :] = kept_ref[j] + decode(codes, scale)
    split_strips(total, rows, position, keep_ref, send_ref)


def halve(kept, got, position, chunk):
    strips, rows, width = kept.shape
    return call(
        functools.partial(halve_kernel, rows, position),
        f"halve_{position}_{chunk}",
        (kept, got),
        [IN_VMEM] * 2,
        strips_shapes(strips // 2, rows, width),
        [pltpu.VMEM((strips * rows, width), jnp.float32)],
    )


def square_kernel(place, kept_ref, got_ref, *rest):
    others, (square_ref, sums_ref) = rest[:-2], rest[-2:]
    value = kept_ref[0] + decode(got_ref[HEAD:, :], scales(got_ref[0:HEAD, :])[0:1])
    square = value * value
    square_ref[...] = square
    sums = jnp.broadcast_to(jnp.sum(square, axis=0, keepdims=True), (8, square.shape[1]))
    every = [ref[...] for ref in others]
    sums_ref[...] = jnp.concatenate(every[:place] + [sums] + every[place:], axis=1)


def square(kept, got, others, place, chunk):
    _, rows, width = kept.shape
    return call(
        functools.partial(square_kernel, place),
        f"square_{chunk}",
        (kept, got, *others),
        [IN_VMEM] * (2 + len(others)),
        [
            jax.ShapeDtypeStruct((rows, width), jnp.float32),
            jax.ShapeDtypeStruct((8, width + sum(sums.shape[1] for sums in others)), jnp.float32),
        ],
    )


def rescale_kernel(height, count, *refs):
    squares, sums, out_ref = refs[:count], refs[count:-1], refs[-1]
    total = functools.reduce(jnp.add, [ref[0:1, :] for ref in sums])
    divisor = total / height + 1e-6
    column = 0
    for ref in squares:
        columns = slice(column, column + ref.shape[1])
        column += ref.shape[1]
        out_ref[0, :, columns] = ref[...] / divisor[:, columns]


def rescale(squares, sums, height):
    rows = squares[0].shape[0]
    width = sums[0].shape[1]
    return call(
        functools.partial(rescale_kernel, float(height), len(squares)),
        "rescale",
        (*squares, *sums),
        [IN_VMEM] * (len(squares) + len(sums)),
        jax.ShapeDtypeStruct((1, rows, width), jnp.float32),
    )


def shards(flow_t, graph, a_pattern, b_pattern, c_pattern):
    layers = lax.axis_size("layer")
    blks = lax.axis_size("blk")
    width = flow_t.shape[2]
    panel = width // 3
    a_lines = a_pattern.transpose(2, 0, 1)
    b_lines = b_pattern.transpose(2, 0, 1)
    c_lines = c_pattern.transpose(0, 2, 1)

    def other_chip(i):
        return (i + 1 if i % 2 else i - 1) % blks

    def same_chip(i):
        return i ^ 1

    halves = panel // BS
    fine = (LANES,) * (BS // LANES)
    widths = [fine] * halves
    ext, ints, owns, latest = [], [], [], []

    def ordered(value):
        return after(value, latest[-1])

    def send(part, partner, got):
        whole = swap(part, "blk", partner)
        half_widths = widths[len(got)]
        got.append([(whole, sum(half_widths[:i])) for i in range(len(half_widths))])

    part, ext_rows, a_rows, b_rows, c_rows = first_products(flow_t, graph, a_lines, b_lines, c_lines)
    send(part, other_chip, ext)
    latest.append(part)
    wanted = {"own": (BS,), "int": (BS,)}
    own, part, int_rows = products(a_rows, ordered(b_rows), graph, ext_rows, flow_t, 0, wanted, turns=True)
    owns.append(own)
    send(part, same_chip, ints)
    latest.append(own)

    def side_products(half):
        wanted = {"ext": (BS,), "int": (BS,)}
        ext_part, int_part = products(a_rows, ordered(b_rows), graph, ext_rows, int_rows, half, wanted)
        send(ext_part, other_chip, ext)
        send(int_part, same_chip, ints)
        latest.append(ext_part)

    def own_products(half):
        owns.extend(products(a_rows, ordered(b_rows), graph, ext_rows, int_rows, half, {"own": (BS,)}))
        latest.append(owns[-1])

    strips, squares, sums = [], {}, {}
    places = [(half, i) for half, each in enumerate(widths) for i in range(len(each))]
    chunks = len(places)

    def add_up(chunk):
        half, i = places[chunk]
        width = widths[half][i]
        kept, send = join(owns[half], *ext[half][i], ints[half][i][0], ordered(c_rows), half, width, layers)
        latest.append(kept)
        strips.append((kept, swap(send, "layer", lambda i: i ^ 1)))

    def scatter(chunk):
        kept, got = strips[chunk]
        position = 1
        while kept.shape[0] > 1:
            position *= 2
            kept, send = halve(ordered(kept), got, position, chunk)
            latest.append(kept)
            got = swap(send, "layer", lambda i: i ^ position)
        strips[chunk] = kept, got

    def finish(chunk):
        kept, got = strips[chunk]
        others, place = ([], 0)
        if len(squares) == chunks - 1:
            others, place = [sums[i] for i in sorted(sums)], chunk
        squares[chunk], sums[chunk] = square(ordered(kept), got, others, place, chunk)
        latest.append(sums[chunk])

    side_products(1)
    add_up(0)
    add_up(1)
    own_products(1)
    scatter(0)
    scatter(1)
    add_up(2)
    finish(0)
    add_up(3)
    finish(1)
    scatter(2)
    scatter(3)
    finish(2)
    finish(3)

    squares = [squares[i] for i in sorted(squares)]
    mine = sums[3]
    others = [swap(mine, "layer", lambda i: i ^ other) for other in range(1, layers)]
    return rescale(squares, [mine, *others], width)


def solution(mesh):
    placed = (
        P("blk", "layer", None),
        P("blk", "layer", None),
        P("blk", None, None),
        P("blk", None, None),
        P("blk", None, None),
    )
    return jax.shard_map(
        shards, mesh=mesh, in_specs=placed, out_specs=P("blk", "layer", None), check_vma=False
    )
```

```python
import functools

import jax
import jax.numpy as jnp
from jax import lax
from jax.experimental import pallas as pl
from jax.experimental.pallas import tpu as pltpu
from jax.sharding import PartitionSpec as P

BS = 256
LANES = 128
HEAD = 16
STEPS = 256.0
TOP = 65534.0
LN2 = 0.6931471805599453
DIRECT = 1
PRODUCT_LIMIT = 24000000
SMALL_LIMIT = 8 * 1024 * 1024
IN_VMEM = pl.BlockSpec(memory_space=pltpu.VMEM)
IN_HBM = pl.BlockSpec(memory_space=pltpu.HBM)


def swap(block, axis, partner):
    return lax.ppermute(block, axis, [(partner(i), i) for i in range(lax.axis_size(axis))])


def after(value, *others):
    return lax.optimization_barrier((value, *others))[0]


def call(kernel, name, operands, in_specs, out_shape, scratch_shapes=(), limit=SMALL_LIMIT):
    return pl.pallas_call(
        kernel,
        out_shape=out_shape,
        in_specs=in_specs,
        out_specs=jax.tree.map(lambda _: IN_VMEM, out_shape),
        scratch_shapes=list(scratch_shapes),
        compiler_params=pltpu.CompilerParams(vmem_limit_bytes=limit),
        cost_estimate=pl.CostEstimate(flops=1, bytes_accessed=1, transcendentals=0),
        name=name,
    )(*operands)


def powers(values):
    largest = jnp.maximum(jnp.max(values, axis=0, keepdims=True), 1e-3)
    return jnp.floor(jnp.log(largest) * (STEPS / LN2)) + 2.0


def code(values, power):
    scaled = values * (TOP * jnp.exp(power * (-LN2 / STEPS)))
    return ((scaled + 0.5).astype(jnp.int32) - 32767).astype(jnp.int16)


def scales(head):
    return jnp.exp(head.astype(jnp.int32).astype(jnp.float32) * (LN2 / STEPS)) * (1.0 / TOP)


def decode(codes, scale):
    return (codes.astype(jnp.int32) + 32767).astype(jnp.float32) * scale


def factor_rows(pattern, column, first, ref):
    place = lax.broadcasted_iota(jnp.int32, (1, ref.shape[1]), 1) // BS
    for u in range(ref.shape[0]):
        row = jnp.zeros((1, ref.shape[1]), jnp.float32)
        for v in range(ref.shape[1] // BS):
            row = jnp.where(place == v, pattern(column + v, first + u).astype(jnp.float32), row)
        ref[u : u + 1, :] = row


def masked(values, factors):
    parts = [
        values[u * BS : (u + 1) * BS] * factors[u : u + 1].astype(values.dtype) for u in range(values.shape[0] // BS)
    ]
    return jnp.concatenate(parts, axis=0) if len(parts) > 1 else parts[0]


def dot(left_side, right_side):
    return lax.dot_general(
        left_side, right_side, (((1,), (0,)), ((), ())), preferred_element_type=jnp.float32
    )


def columns_of(ref, start, count):
    return ref.at[0, :, pl.ds(pl.multiple_of(start * BS, BS), count * BS)]


def blocks_at(block, count=1):
    return pl.ds(pl.multiple_of(block * BS, BS), count * BS)


class Sides:
    def __init__(self, inner, panel):
        odd = lax.rem(lax.axis_index("blk"), 2)
        self.panel = panel
        self.first = lax.axis_index("layer") * (inner // BS)
        self.ext_side, self.int_side = odd * (2 * panel), (1 - odd) * (2 * panel)
        self.ext_rows = odd * panel
        self.columns = {"ext": self.ext_side, "own": panel, "int": self.int_side}


class Coded:
    def __init__(self, refs):
        self.refs = refs
        self.heads = [jnp.zeros((HEAD, ref.shape[1]), jnp.float32) for ref in refs]

    def write_all(self, product, place):
        for i in range(product.shape[0] // BS):
            self.write(product[i * BS : (i + 1) * BS], place + i)

    def write(self, product, place):
        column = 0
        for c, ref in enumerate(self.refs):
            chunk = product[:, column : column + ref.shape[1]]
            column += ref.shape[1]
            power = powers(chunk)
            ref[HEAD + place * BS : HEAD + (place + 1) * BS, :] = code(chunk, power)
            line = lax.broadcasted_iota(jnp.int32, self.heads[c].shape, 0)
            self.heads[c] = jnp.where(line == place, power, self.heads[c])

    def finish(self):
        for ref, head in zip(self.refs, self.heads):
            ref[0:HEAD, :] = head.astype(jnp.int32).astype(jnp.int16)


def first_kernel(a_hbm, b_hbm, c_hbm, flow_hbm, graph_hbm, *rest):
    out_refs, rest = rest[:-12], rest[-12:]
    rows_ref, a_rows_ref, b_rows_ref, c_rows_ref, graph_buf, flow_buf, total, ext_factors, a_ref, b_ref, c_ref, sems = rest
    inner, panel = flow_buf.shape[0], flow_buf.shape[1] // BS // 2
    at = Sides(inner, panel)
    steps = inner // BS
    small = [
        pltpu.make_async_copy(pattern, ref, sems.at[i])
        for i, (pattern, ref) in enumerate(((a_hbm, a_ref), (b_hbm, b_ref), (c_hbm, c_ref)))
    ]
    flows, graphs = [], []
    for t in range(steps):
        rows = slice(t * BS, (t + 1) * BS)
        flow = columns_of(flow_hbm, at.ext_rows, 2 * panel).at[rows]
        graph = columns_of(graph_hbm, at.ext_side, 1).at[rows]
        flows.append(pltpu.make_async_copy(flow, flow_buf.at[rows], sems.at[3 + 2 * t]))
        graphs.append(pltpu.make_async_copy(graph, graph_buf.at[rows], sems.at[4 + 2 * t]))
    for copy in small:
        copy.start()
    for t in range(steps):
        flows[t].start()
        graphs[t].start()
    for copy in small:
        copy.wait()
    factor_rows(lambda column, inner: a_ref[column, 0, inner], 0, at.first, a_rows_ref)
    factor_rows(lambda column, inner: b_ref[column, 0, inner], 0, at.first, b_rows_ref)
    factor_rows(lambda column, row: c_ref[0, column, row], 0, 0, c_rows_ref)
    ext_factors[...] = a_rows_ref[:, blocks_at(at.ext_rows, 2 * panel)]
    right_factors = b_rows_ref[:, blocks_at(at.ext_side)]
    per_dot = min(2, steps)
    for t in range(0, steps, per_dot):
        rows = slice(t * BS, (t + per_dot) * BS)
        for copy in flows[t : t + per_dot] + graphs[t : t + per_dot]:
            copy.wait()
        turned = masked(flow_buf[rows, :], ext_factors[t : t + per_dot]).T
        rows_ref[:, rows] = turned
        product = dot(turned, masked(graph_buf[rows, :], right_factors[t : t + per_dot]))
        if t + per_dot < steps:
            total[...] = product if t == 0 else total[...] + product
    if steps > per_dot:
        total[...] += product
    else:
        total[...] = product
    coded = Coded(out_refs)
    for place, first in ((0, panel), (panel, at.ext_side)):
        for i in range(panel):
            coded.write(total[blocks_at(first - at.ext_rows + i), :], place + i)
    coded.finish()


def first_products(flow_t, graph, a_lines, b_lines, c_lines, widths):
    inner, width = flow_t.shape[1:]
    panel = width // 3
    return call(
        first_kernel,
        "first_products",
        [pltpu.with_memory_space_constraint(x, pltpu.HBM) for x in (a_lines, b_lines, c_lines, flow_t, graph)],
        [IN_HBM] * 5,
        [jax.ShapeDtypeStruct((HEAD + 2 * panel, w), jnp.int16) for w in widths]
        + [
            pltpu.VMEM((2 * panel, inner), flow_t.dtype),
            pltpu.VMEM((inner // BS, width), jnp.float32),
            pltpu.VMEM((inner // BS, width), jnp.float32),
            pltpu.VMEM((width // BS, panel), jnp.float32),
        ],
        [
            pltpu.VMEM((inner, BS), graph.dtype),
            pltpu.VMEM((inner, 2 * panel), flow_t.dtype),
            pltpu.VMEM((2 * panel, BS), jnp.float32),
            pltpu.VMEM((inner // BS, 2 * panel), jnp.float32),
            pltpu.SMEM(a_lines.shape, a_lines.dtype),
            pltpu.SMEM(b_lines.shape, b_lines.dtype),
            pltpu.SMEM(c_lines.shape, c_lines.dtype),
            pltpu.SemaphoreType.DMA((3 + 2 * (inner // BS),)),
        ],
        limit=PRODUCT_LIMIT,
    )


def product_kernel(half, wanted, turns, a_rows_ref, b_rows_ref, graph_ref, ext_rows_ref, side_ref, *rest):
    refs = list(rest)
    inner, panel = graph_ref.shape[1], graph_ref.shape[2] // BS // 3
    at = Sides(inner, panel)
    parts = [part for part in ("ext", "own", "int") if part in wanted]
    outs = {part: [refs.pop(0) for _ in wanted[part]] for part in parts}
    int_rows_ref = side_ref
    if turns:
        int_rows_ref = refs.pop(0)
        place = blocks_at(at.int_side, panel)
        int_rows_ref[...] = masked(side_ref[0, :, place], a_rows_ref[:, place]).T
    coded = {part: Coded(outs[part]) for part in parts if part != "own"}
    right = []
    for part in parts:
        place = blocks_at(at.columns[part] + half)
        right.append(masked(graph_ref[0, :, place], b_rows_ref[:, place]))
    right = jnp.concatenate(right, axis=1) if len(right) > 1 else right[0]
    panels = (
        (panel, ext_rows_ref.at[blocks_at(panel - at.ext_rows, panel)], {"ext": 0, "own": 0, "int": 0}),
        (at.ext_side, ext_rows_ref.at[blocks_at(at.ext_side - at.ext_rows, panel)], {"ext": panel, "own": 0}),
        (at.int_side, int_rows_ref, {"own": 0, "int": panel}),
    )
    for first, source, takers in panels:
        used = [part for part in parts if part in takers]
        if not used:
            continue
        low = parts.index(used[0]) * BS
        for i in range(panel):
            product = dot(source[i * BS : (i + 1) * BS, :], right[:, low : low + len(used) * BS])
            for j, part in enumerate(used):
                piece = product[:, j * BS : (j + 1) * BS]
                if part == "own":
                    outs[part][0][blocks_at(first + i), :] = piece
                else:
                    coded[part].write(piece, takers[part] + i)
    for part in coded:
        coded[part].finish()


def products(a_rows, b_rows, graph, ext_rows, side, half, wanted, turns=False):
    inner, width = graph.shape[1:]
    panel = width // 3
    outs = []
    for part in ("ext", "own", "int"):
        for w in wanted.get(part, ()):
            if part == "own":
                outs.append(jax.ShapeDtypeStruct((width, w), jnp.float32))
            else:
                outs.append(jax.ShapeDtypeStruct((HEAD + 2 * panel, w), jnp.int16))
    if turns:
        outs.append(pltpu.VMEM((panel, inner), graph.dtype))
    return call(
        functools.partial(product_kernel, half, wanted, turns),
        "_".join(wanted) + f"_products_{half}",
        (a_rows, b_rows, graph, ext_rows, side),
        [IN_VMEM] * 5,
        outs,
        limit=PRODUCT_LIMIT,
    )


def send_strip(send_ref, strips, power):
    rows = strips[0].shape[0]
    for j, strip in enumerate(strips):
        send_ref[HEAD + j * rows : HEAD + (j + 1) * rows, :] = code(strip, power)
    send_ref[0:HEAD, :] = jnp.broadcast_to(power, (HEAD, power.shape[1])).astype(jnp.int32).astype(jnp.int16)


def split_strips(total, rows, position, keep_ref, send_refs):
    layer = lax.axis_index("layer")
    if len(send_refs) > 1:
        keep_ref[0] = total[pl.ds(layer * rows, rows), :]
        for other, send_ref in enumerate(send_refs, 1):
            strip = total[pl.ds((layer ^ other) * rows, rows), :]
            send_strip(send_ref, [strip], powers(strip))
        return
    bit = lax.rem(layer // position, 2)
    pairs = keep_ref.shape[0]
    for j in range(pairs):
        keep_ref[j] = total[pl.ds((2 * j + bit) * rows, rows), :]
    away = [total[pl.ds((2 * j + 1 - bit) * rows, rows), :] for j in range(pairs)]
    send_strip(send_refs[0], away, functools.reduce(jnp.maximum, [powers(strip) for strip in away]))


def join_kernel(rows, half, lane, c_ref, own_ref, ext_ref, int_ref, keep_ref, *rest):
    *send_refs, total = rest
    odd = lax.rem(lax.axis_index("blk"), 2)
    panel = own_ref.shape[0] // BS // 3
    lanes = slice(lane, lane + ext_ref.shape[1])
    refs = (ext_ref, int_ref)
    from_mid, from_side = ([[(r, start + i) for i in range(panel)] for r in range(2)] for start in (0, panel))
    middle = [list(both) for both in zip(from_side[0], from_side[1])]
    ext_only, int_only = ([[part] for part in from_mid[r]] for r in range(2))
    odd_parts = int_only + middle + ext_only
    even_parts = ext_only + middle + int_only

    def add(parts):
        scale = [scales(ref[0:HEAD, :]) for ref in refs]
        for v in range(3 * panel):
            kept = c_ref[v : v + 1, half * BS + lane : half * BS + lane + ext_ref.shape[1]]
            block = own_ref[v * BS : (v + 1) * BS, lanes] * kept
            for r, i in parts[v]:
                codes = refs[r][HEAD + i * BS : HEAD + (i + 1) * BS, :]
                block += decode(codes, scale[r][i : i + 1] * kept)
            total[v * BS : (v + 1) * BS, :] = block

    @pl.when(odd == 1)
    def _():
        add(odd_parts)

    @pl.when(odd == 0)
    def _():
        add(even_parts)

    split_strips(total, rows, 1, keep_ref, send_refs)


def strips_shapes(pairs, rows, width, messages=1):
    return [
        jax.ShapeDtypeStruct((pairs, rows, width), jnp.float32),
        *[jax.ShapeDtypeStruct((HEAD + pairs * rows, width), jnp.int16)] * messages,
    ]


def join(own, ext_part, int_part, c_rows, half, lane, layers, direct):
    height = own.shape[0]
    width = int_part.shape[1]
    rows = height // layers
    return call(
        functools.partial(join_kernel, rows, half, lane),
        f"join_{half}_{lane}",
        (c_rows, own, ext_part, int_part),
        [IN_VMEM] * 4,
        strips_shapes(1, rows, width, layers - 1) if direct else strips_shapes(layers // 2, rows, width),
        [pltpu.VMEM((height, width), jnp.float32)],
    )


def halve_kernel(rows, position, kept_ref, got_ref, keep_ref, send_ref, total):
    scale = scales(got_ref[0:HEAD, :])[0:1]
    for j in range(kept_ref.shape[0]):
        codes = got_ref[HEAD + j * rows : HEAD + (j + 1) * rows, :]
        total[j * rows : (j + 1) * rows, :] = kept_ref[j] + decode(codes, scale)
    split_strips(total, rows, position, keep_ref, [send_ref])


def halve(kept, got, position, chunk):
    strips, rows, width = kept.shape
    return call(
        functools.partial(halve_kernel, rows, position),
        f"halve_{position}_{chunk}",
        (kept, got),
        [IN_VMEM] * 2,
        strips_shapes(strips // 2, rows, width),
        [pltpu.VMEM((strips * rows, width), jnp.float32)],
    )


def square_kernel(messages, place, kept_ref, *rest):
    got_refs, others, (square_ref, sums_ref) = rest[:messages], rest[messages:-2], rest[-2:]
    value = kept_ref[0]
    for ref in got_refs:
        value += decode(ref[HEAD:, :], scales(ref[0:HEAD, :])[0:1])
    square = value * value
    square_ref[...] = square
    sums = jnp.broadcast_to(jnp.sum(square, axis=0, keepdims=True), (8, square.shape[1]))
    every = [ref[...] for ref in others]
    sums_ref[...] = jnp.concatenate(every[:place] + [sums] + every[place:], axis=1)


def square(kept, got, others, place, chunk):
    _, rows, width = kept.shape
    return call(
        functools.partial(square_kernel, len(got), place),
        f"square_{chunk}",
        (kept, *got, *others),
        [IN_VMEM] * (1 + len(got) + len(others)),
        [
            jax.ShapeDtypeStruct((rows, width), jnp.float32),
            jax.ShapeDtypeStruct((8, width + sum(sums.shape[1] for sums in others)), jnp.float32),
        ],
    )


def rescale_kernel(height, count, *refs):
    squares, sums, out_ref = refs[:count], refs[count:-1], refs[-1]
    total = functools.reduce(jnp.add, [ref[0:1, :] for ref in sums])
    divisor = total / height + 1e-6
    column = 0
    for ref in squares:
        columns = slice(column, column + ref.shape[1])
        column += ref.shape[1]
        out_ref[0, :, columns] = ref[...] / divisor[:, columns]


def rescale(squares, sums, height):
    rows = squares[0].shape[0]
    width = sums[0].shape[1]
    return call(
        functools.partial(rescale_kernel, float(height), len(squares)),
        "rescale",
        (*squares, *sums),
        [IN_VMEM] * (len(squares) + len(sums)),
        jax.ShapeDtypeStruct((1, rows, width), jnp.float32),
    )


def shards(flow_t, graph, a_pattern, b_pattern, c_pattern):
    layers = lax.axis_size("layer")
    blks = lax.axis_size("blk")
    width = flow_t.shape[2]
    panel = width // 3
    a_lines = a_pattern.transpose(2, 0, 1)
    b_lines = b_pattern.transpose(2, 0, 1)
    c_lines = c_pattern.transpose(0, 2, 1)

    def other_chip(i):
        return (i + 1 if i % 2 else i - 1) % blks

    def same_chip(i):
        return i ^ 1

    halves = panel // BS
    chunks = panel // LANES
    fine = (LANES,) * (BS // LANES)
    per_half = len(fine)
    ext, ints, owns, latest = [], [], [], []

    def ordered(value):
        return after(value, latest[-1])

    def send_ext(parts):
        ext.extend(swap(part, "blk", other_chip) for part in parts)
        latest.append(parts[0])

    def send_int(parts):
        ints.extend(swap(part, "blk", same_chip) for part in parts)
        latest.append(parts[0])

    *parts, ext_rows, a_rows, b_rows, c_rows = first_products(flow_t, graph, a_lines, b_lines, c_lines, fine)
    send_ext(parts)
    wanted = {"own": (BS,), "int": fine}
    own, *parts, int_rows = products(a_rows, ordered(b_rows), graph, ext_rows, flow_t, 0, wanted, turns=True)
    owns.append(own)
    send_int(parts)

    def more_products(half):
        wanted = {"ext": fine, "int": fine}
        parts = products(a_rows, ordered(b_rows), graph, ext_rows, int_rows, half, wanted)
        send_ext(parts[:per_half])
        send_int(parts[per_half:])

    def more_own(half):
        owns.extend(products(a_rows, ordered(b_rows), graph, ext_rows, int_rows, half, {"own": (BS,)}))
        latest.append(owns[-1])

    strips, squares, sums = [], {}, {}

    def add_up(chunk):
        half, lane = divmod(chunk, per_half)
        direct = chunk < DIRECT and layers <= 4
        kept, *sends = join(
            owns[half], ext[chunk], ints[chunk], ordered(c_rows), half, lane * LANES, layers, direct
        )
        latest.append(kept)
        strips.append((kept, [swap(send, "layer", lambda i: i ^ other) for other, send in enumerate(sends, 1)]))

    def scatter(chunk):
        kept, got = strips[chunk]
        position = 1
        while kept.shape[0] > 1:
            position *= 2
            kept, send = halve(ordered(kept), got[0], position, chunk)
            latest.append(kept)
            got = [swap(send, "layer", lambda i: i ^ position)]
        strips[chunk] = kept, got

    def finish(chunk):
        kept, got = strips[chunk]
        others, place = ([], 0)
        if len(squares) == chunks - 1:
            others, place = [sums[i] for i in sorted(sums)], chunk
        squares[chunk], sums[chunk] = square(ordered(kept), got, others, place, chunk)
        latest.append(sums[chunk])

    add_up(0)
    more_products(1)
    add_up(1)
    more_own(1)
    scatter(0)
    finish(0)
    add_up(2)
    scatter(1)
    add_up(3)
    scatter(2)
    scatter(3)
    finish(1)
    finish(2)
    finish(3)

    squares = [squares[i] for i in sorted(squares)]
    mine = sums[3]
    others = [swap(mine, "layer", lambda i: i ^ other) for other in range(1, layers)]
    return rescale(squares, [mine, *others], width)


def solution(mesh):
    placed = (
        P("blk", "layer", None),
        P("blk", "layer", None),
        P("blk", None, None),
        P("blk", None, None),
        P("blk", None, None),
    )
    return jax.shard_map(
        shards, mesh=mesh, in_specs=placed, out_specs=P("blk", "layer", None), check_vma=False
    )
```

```python
import functools

import jax
import jax.numpy as jnp
from jax import lax
from jax.experimental import pallas as pl
from jax.experimental.pallas import tpu as pltpu
from jax.sharding import PartitionSpec as P

BS = 256
LANES = 128
HEAD = 16
STEPS = 256.0
TOP = 65534.0
LN2 = 0.6931471805599453
PRODUCT_LIMIT = 24000000
SMALL_LIMIT = 8 * 1024 * 1024
IN_VMEM = pl.BlockSpec(memory_space=pltpu.VMEM)
IN_HBM = pl.BlockSpec(memory_space=pltpu.HBM)


def swap(block, axis, partner):
    return lax.ppermute(block, axis, [(partner(i), i) for i in range(lax.axis_size(axis))])


def after(value, *others):
    return lax.optimization_barrier((value, *others))[0]


def call(kernel, name, operands, in_specs, out_shape, scratch_shapes=(), limit=SMALL_LIMIT):
    return pl.pallas_call(
        kernel,
        out_shape=out_shape,
        in_specs=in_specs,
        out_specs=jax.tree.map(lambda _: IN_VMEM, out_shape),
        scratch_shapes=list(scratch_shapes),
        compiler_params=pltpu.CompilerParams(vmem_limit_bytes=limit),
        cost_estimate=pl.CostEstimate(flops=1, bytes_accessed=1, transcendentals=0),
        name=name,
    )(*operands)


def powers(values):
    largest = jnp.maximum(jnp.max(values, axis=0, keepdims=True), 1e-3)
    return jnp.floor(jnp.log(largest) * (STEPS / LN2)) + 2.0


def code(values, power):
    scaled = values * (TOP * jnp.exp(power * (-LN2 / STEPS)))
    return ((scaled + 0.5).astype(jnp.int32) - 32767).astype(jnp.int16)


def scales(head):
    return jnp.exp(head.astype(jnp.int32).astype(jnp.float32) * (LN2 / STEPS)) * (1.0 / TOP)


def decode(codes, scale):
    return (codes.astype(jnp.int32) + 32767).astype(jnp.float32) * scale


def factor_rows(pattern, column, first, ref):
    place = lax.broadcasted_iota(jnp.int32, (1, ref.shape[1]), 1) // BS
    for u in range(ref.shape[0]):
        row = jnp.zeros((1, ref.shape[1]), jnp.float32)
        for v in range(ref.shape[1] // BS):
            row = jnp.where(place == v, pattern(column + v, first + u).astype(jnp.float32), row)
        ref[u : u + 1, :] = row


def masked(values, factors):
    parts = [
        values[u * BS : (u + 1) * BS] * factors[u : u + 1].astype(values.dtype) for u in range(values.shape[0] // BS)
    ]
    return jnp.concatenate(parts, axis=0) if len(parts) > 1 else parts[0]


def dot(left_side, right_side):
    return lax.dot_general(
        left_side, right_side, (((1,), (0,)), ((), ())), preferred_element_type=jnp.float32
    )


def columns_of(ref, start, count):
    return ref.at[0, :, pl.ds(pl.multiple_of(start * BS, BS), count * BS)]


def blocks_at(block, count=1):
    return pl.ds(pl.multiple_of(block * BS, BS), count * BS)


class Sides:
    def __init__(self, inner, panel):
        odd = lax.rem(lax.axis_index("blk"), 2)
        self.panel = panel
        self.first = lax.axis_index("layer") * (inner // BS)
        self.ext_side, self.int_side = odd * (2 * panel), (1 - odd) * (2 * panel)
        self.ext_rows = odd * panel
        self.columns = {"ext": self.ext_side, "own": panel, "int": self.int_side}


class Coded:
    def __init__(self, refs):
        self.refs = refs
        self.heads = [jnp.zeros((HEAD, ref.shape[1]), jnp.float32) for ref in refs]

    def write_all(self, product, place):
        for i in range(product.shape[0] // BS):
            self.write(product[i * BS : (i + 1) * BS], place + i)

    def write(self, product, place):
        column = 0
        for c, ref in enumerate(self.refs):
            chunk = product[:, column : column + ref.shape[1]]
            column += ref.shape[1]
            power = powers(chunk)
            ref[HEAD + place * BS : HEAD + (place + 1) * BS, :] = code(chunk, power)
            line = lax.broadcasted_iota(jnp.int32, self.heads[c].shape, 0)
            self.heads[c] = jnp.where(line == place, power, self.heads[c])

    def finish(self):
        for ref, head in zip(self.refs, self.heads):
            ref[0:HEAD, :] = head.astype(jnp.int32).astype(jnp.int16)


def first_kernel(a_hbm, b_hbm, c_hbm, flow_hbm, graph_hbm, *rest):
    out_refs, rest = rest[:-12], rest[-12:]
    rows_ref, a_rows_ref, b_rows_ref, c_rows_ref, graph_buf, flow_buf, total, ext_factors, a_ref, b_ref, c_ref, sems = rest
    inner, panel = flow_buf.shape[0], flow_buf.shape[1] // BS // 2
    at = Sides(inner, panel)
    steps = inner // BS
    small = [
        pltpu.make_async_copy(pattern, ref, sems.at[i])
        for i, (pattern, ref) in enumerate(((a_hbm, a_ref), (b_hbm, b_ref), (c_hbm, c_ref)))
    ]
    flows, graphs = [], []
    for t in range(steps):
        rows = slice(t * BS, (t + 1) * BS)
        flow = columns_of(flow_hbm, at.ext_rows, 2 * panel).at[rows]
        graph = columns_of(graph_hbm, at.ext_side, 1).at[rows]
        flows.append(pltpu.make_async_copy(flow, flow_buf.at[rows], sems.at[3 + 2 * t]))
        graphs.append(pltpu.make_async_copy(graph, graph_buf.at[rows], sems.at[4 + 2 * t]))
    for copy in small:
        copy.start()
    for t in range(steps):
        flows[t].start()
        graphs[t].start()
    for copy in small:
        copy.wait()
    factor_rows(lambda column, inner: a_ref[column, 0, inner], 0, at.first, a_rows_ref)
    factor_rows(lambda column, inner: b_ref[column, 0, inner], 0, at.first, b_rows_ref)
    factor_rows(lambda column, row: c_ref[0, column, row], 0, 0, c_rows_ref)
    ext_factors[...] = a_rows_ref[:, blocks_at(at.ext_rows, 2 * panel)]
    right_factors = b_rows_ref[:, blocks_at(at.ext_side)]
    per_dot = min(2, steps)
    for t in range(0, steps, per_dot):
        rows = slice(t * BS, (t + per_dot) * BS)
        for copy in flows[t : t + per_dot] + graphs[t : t + per_dot]:
            copy.wait()
        turned = masked(flow_buf[rows, :], ext_factors[t : t + per_dot]).T
        rows_ref[:, rows] = turned
        product = dot(turned, masked(graph_buf[rows, :], right_factors[t : t + per_dot]))
        if t + per_dot < steps:
            total[...] = product if t == 0 else total[...] + product
    if steps > per_dot:
        total[...] += product
    else:
        total[...] = product
    coded = Coded(out_refs)
    for place, first in ((0, panel), (panel, at.ext_side)):
        for i in range(panel):
            coded.write(total[blocks_at(first - at.ext_rows + i), :], place + i)
    coded.finish()


def first_products(flow_t, graph, a_lines, b_lines, c_lines, widths):
    inner, width = flow_t.shape[1:]
    panel = width // 3
    return call(
        first_kernel,
        "first_products",
        [pltpu.with_memory_space_constraint(x, pltpu.HBM) for x in (a_lines, b_lines, c_lines, flow_t, graph)],
        [IN_HBM] * 5,
        [jax.ShapeDtypeStruct((HEAD + 2 * panel, w), jnp.int16) for w in widths]
        + [
            pltpu.VMEM((2 * panel, inner), flow_t.dtype),
            pltpu.VMEM((inner // BS, width), jnp.float32),
            pltpu.VMEM((inner // BS, width), jnp.float32),
            pltpu.VMEM((width // BS, panel), jnp.float32),
        ],
        [
            pltpu.VMEM((inner, BS), graph.dtype),
            pltpu.VMEM((inner, 2 * panel), flow_t.dtype),
            pltpu.VMEM((2 * panel, BS), jnp.float32),
            pltpu.VMEM((inner // BS, 2 * panel), jnp.float32),
            pltpu.SMEM(a_lines.shape, a_lines.dtype),
            pltpu.SMEM(b_lines.shape, b_lines.dtype),
            pltpu.SMEM(c_lines.shape, c_lines.dtype),
            pltpu.SemaphoreType.DMA((3 + 2 * (inner // BS),)),
        ],
        limit=PRODUCT_LIMIT,
    )


def product_kernel(half, wanted, turns, a_rows_ref, b_rows_ref, graph_ref, ext_rows_ref, side_ref, *rest):
    refs = list(rest)
    inner, panel = graph_ref.shape[1], graph_ref.shape[2] // BS // 3
    at = Sides(inner, panel)
    parts = [part for part in ("ext", "own", "int") if part in wanted]
    outs = {part: [refs.pop(0) for _ in wanted[part]] for part in parts}
    int_rows_ref = side_ref
    if turns:
        int_rows_ref = refs.pop(0)
        place = blocks_at(at.int_side, panel)
        int_rows_ref[...] = masked(side_ref[0, :, place], a_rows_ref[:, place]).T
    coded = {part: Coded(outs[part]) for part in parts if part != "own"}
    right = []
    for part in parts:
        place = blocks_at(at.columns[part] + half)
        right.append(masked(graph_ref[0, :, place], b_rows_ref[:, place]))
    right = jnp.concatenate(right, axis=1) if len(right) > 1 else right[0]
    panels = (
        (panel, ext_rows_ref.at[blocks_at(panel - at.ext_rows, panel)], {"ext": 0, "own": 0, "int": 0}),
        (at.ext_side, ext_rows_ref.at[blocks_at(at.ext_side - at.ext_rows, panel)], {"ext": panel, "own": 0}),
        (at.int_side, int_rows_ref, {"own": 0, "int": panel}),
    )
    for first, source, takers in panels:
        used = [part for part in parts if part in takers]
        if not used:
            continue
        low = parts.index(used[0]) * BS
        for i in range(panel):
            product = dot(source[i * BS : (i + 1) * BS, :], right[:, low : low + len(used) * BS])
            for j, part in enumerate(used):
                piece = product[:, j * BS : (j + 1) * BS]
                if part == "own":
                    outs[part][0][blocks_at(first + i), :] = piece
                else:
                    coded[part].write(piece, takers[part] + i)
    for part in coded:
        coded[part].finish()


def products(a_rows, b_rows, graph, ext_rows, side, half, wanted, turns=False):
    inner, width = graph.shape[1:]
    panel = width // 3
    outs = []
    for part in ("ext", "own", "int"):
        for w in wanted.get(part, ()):
            if part == "own":
                outs.append(jax.ShapeDtypeStruct((width, w), jnp.float32))
            else:
                outs.append(jax.ShapeDtypeStruct((HEAD + 2 * panel, w), jnp.int16))
    if turns:
        outs.append(pltpu.VMEM((panel, inner), graph.dtype))
    return call(
        functools.partial(product_kernel, half, wanted, turns),
        "_".join(wanted) + f"_products_{half}",
        (a_rows, b_rows, graph, ext_rows, side),
        [IN_VMEM] * 5,
        outs,
        limit=PRODUCT_LIMIT,
    )


def send_strip(send_ref, strips, power):
    rows = strips[0].shape[0]
    for j, strip in enumerate(strips):
        send_ref[HEAD + j * rows : HEAD + (j + 1) * rows, :] = code(strip, power)
    send_ref[0:HEAD, :] = jnp.broadcast_to(power, (HEAD, power.shape[1])).astype(jnp.int32).astype(jnp.int16)


def split_strips(total, rows, position, keep_ref, send_refs):
    layer = lax.axis_index("layer")
    if len(send_refs) > 1:
        keep_ref[0] = total[pl.ds(layer * rows, rows), :]
        for other, send_ref in enumerate(send_refs, 1):
            strip = total[pl.ds((layer ^ other) * rows, rows), :]
            send_strip(send_ref, [strip], powers(strip))
        return
    bit = lax.rem(layer // position, 2)
    pairs = keep_ref.shape[0]
    for j in range(pairs):
        keep_ref[j] = total[pl.ds((2 * j + bit) * rows, rows), :]
    away = [total[pl.ds((2 * j + 1 - bit) * rows, rows), :] for j in range(pairs)]
    send_strip(send_refs[0], away, functools.reduce(jnp.maximum, [powers(strip) for strip in away]))


def join_kernel(rows, half, lane, c_ref, own_ref, ext_ref, int_ref, keep_ref, *rest):
    *send_refs, total = rest
    odd = lax.rem(lax.axis_index("blk"), 2)
    panel = own_ref.shape[0] // BS // 3
    lanes = slice(lane, lane + ext_ref.shape[1])
    refs = (ext_ref, int_ref)
    from_mid, from_side = ([[(r, start + i) for i in range(panel)] for r in range(2)] for start in (0, panel))
    middle = [list(both) for both in zip(from_side[0], from_side[1])]
    ext_only, int_only = ([[part] for part in from_mid[r]] for r in range(2))
    odd_parts = int_only + middle + ext_only
    even_parts = ext_only + middle + int_only

    def add(parts):
        scale = [scales(ref[0:HEAD, :]) for ref in refs]
        for v in range(3 * panel):
            kept = c_ref[v : v + 1, half * BS + lane : half * BS + lane + ext_ref.shape[1]]
            block = own_ref[v * BS : (v + 1) * BS, lanes] * kept
            for r, i in parts[v]:
                codes = refs[r][HEAD + i * BS : HEAD + (i + 1) * BS, :]
                block += decode(codes, scale[r][i : i + 1] * kept)
            total[v * BS : (v + 1) * BS, :] = block

    @pl.when(odd == 1)
    def _():
        add(odd_parts)

    @pl.when(odd == 0)
    def _():
        add(even_parts)

    split_strips(total, rows, 1, keep_ref, send_refs)


def strips_shapes(pairs, rows, width, messages=1):
    return [
        jax.ShapeDtypeStruct((pairs, rows, width), jnp.float32),
        *[jax.ShapeDtypeStruct((HEAD + pairs * rows, width), jnp.int16)] * messages,
    ]


def join(own, ext_part, int_part, c_rows, half, lane, layers, direct):
    height = own.shape[0]
    width = int_part.shape[1]
    rows = height // layers
    return call(
        functools.partial(join_kernel, rows, half, lane),
        f"join_{half}_{lane}",
        (c_rows, own, ext_part, int_part),
        [IN_VMEM] * 4,
        strips_shapes(1, rows, width, layers - 1) if direct else strips_shapes(layers // 2, rows, width),
        [pltpu.VMEM((height, width), jnp.float32)],
    )


def halve_kernel(rows, position, kept_ref, got_ref, keep_ref, send_ref, total):
    scale = scales(got_ref[0:HEAD, :])[0:1]
    for j in range(kept_ref.shape[0]):
        codes = got_ref[HEAD + j * rows : HEAD + (j + 1) * rows, :]
        total[j * rows : (j + 1) * rows, :] = kept_ref[j] + decode(codes, scale)
    split_strips(total, rows, position, keep_ref, [send_ref])


def halve(kept, got, position, chunk):
    strips, rows, width = kept.shape
    return call(
        functools.partial(halve_kernel, rows, position),
        f"halve_{position}_{chunk}",
        (kept, got),
        [IN_VMEM] * 2,
        strips_shapes(strips // 2, rows, width),
        [pltpu.VMEM((strips * rows, width), jnp.float32)],
    )


def square_kernel(messages, place, kept_ref, *rest):
    got_refs, others, (square_ref, sums_ref) = rest[:messages], rest[messages:-2], rest[-2:]
    value = kept_ref[0]
    for ref in got_refs:
        value += decode(ref[HEAD:, :], scales(ref[0:HEAD, :])[0:1])
    square = value * value
    square_ref[...] = square
    sums = jnp.broadcast_to(jnp.sum(square, axis=0, keepdims=True), (8, square.shape[1]))
    every = [ref[...] for ref in others]
    sums_ref[...] = jnp.concatenate(every[:place] + [sums] + every[place:], axis=1)


def square(kept, got, others, place, chunk):
    _, rows, width = kept.shape
    return call(
        functools.partial(square_kernel, len(got), place),
        f"square_{chunk}",
        (kept, *got, *others),
        [IN_VMEM] * (1 + len(got) + len(others)),
        [
            jax.ShapeDtypeStruct((rows, width), jnp.float32),
            jax.ShapeDtypeStruct((8, width + sum(sums.shape[1] for sums in others)), jnp.float32),
        ],
    )


def rescale_kernel(height, count, *refs):
    squares, sums, out_ref = refs[:count], refs[count:-1], refs[-1]
    total = functools.reduce(jnp.add, [ref[0:1, :] for ref in sums])
    divisor = total / height + 1e-6
    column = 0
    for ref in squares:
        columns = slice(column, column + ref.shape[1])
        column += ref.shape[1]
        out_ref[0, :, columns] = ref[...] / divisor[:, columns]


def rescale(squares, sums, height):
    rows = squares[0].shape[0]
    width = sums[0].shape[1]
    return call(
        functools.partial(rescale_kernel, float(height), len(squares)),
        "rescale",
        (*squares, *sums),
        [IN_VMEM] * (len(squares) + len(sums)),
        jax.ShapeDtypeStruct((1, rows, width), jnp.float32),
    )


def shards(flow_t, graph, a_pattern, b_pattern, c_pattern):
    layers = lax.axis_size("layer")
    blks = lax.axis_size("blk")
    width = flow_t.shape[2]
    panel = width // 3
    a_lines = a_pattern.transpose(2, 0, 1)
    b_lines = b_pattern.transpose(2, 0, 1)
    c_lines = c_pattern.transpose(0, 2, 1)

    def other_chip(i):
        return (i + 1 if i % 2 else i - 1) % blks

    def same_chip(i):
        return i ^ 1

    halves = panel // BS
    chunks = panel // LANES
    fine = (LANES,) * (BS // LANES)
    per_half = len(fine)
    ext, ints, owns, latest = [], [], [], []

    def ordered(value):
        return after(value, latest[-1])

    def send_ext(parts):
        ext.extend(swap(part, "blk", other_chip) for part in parts)
        latest.append(parts[0])

    def send_int(parts):
        ints.extend(swap(part, "blk", same_chip) for part in parts)
        latest.append(parts[0])

    *parts, ext_rows, a_rows, b_rows, c_rows = first_products(flow_t, graph, a_lines, b_lines, c_lines, fine)
    send_ext(parts)
    wanted = {"own": (BS,), "int": fine}
    own, *parts, int_rows = products(a_rows, ordered(b_rows), graph, ext_rows, flow_t, 0, wanted, turns=True)
    owns.append(own)
    send_int(parts)

    def more_products(half):
        wanted = {"ext": fine, "int": fine}
        parts = products(a_rows, ordered(b_rows), graph, ext_rows, int_rows, half, wanted)
        send_ext(parts[:per_half])
        send_int(parts[per_half:])

    def more_own(half):
        owns.extend(products(a_rows, ordered(b_rows), graph, ext_rows, int_rows, half, {"own": (BS,)}))
        latest.append(owns[-1])

    strips, squares, sums = [], {}, {}

    def add_up(chunk):
        half, lane = divmod(chunk, per_half)
        direct = chunk in (0, chunks - 1) and layers <= 4
        kept, *sends = join(
            owns[half], ext[chunk], ints[chunk], ordered(c_rows), half, lane * LANES, layers, direct
        )
        latest.append(kept)
        strips.append((kept, [swap(send, "layer", lambda i: i ^ other) for other, send in enumerate(sends, 1)]))

    def scatter(chunk):
        kept, got = strips[chunk]
        position = 1
        while kept.shape[0] > 1:
            position *= 2
            kept, send = halve(ordered(kept), got[0], position, chunk)
            latest.append(kept)
            got = [swap(send, "layer", lambda i: i ^ position)]
        strips[chunk] = kept, got

    def finish(chunk):
        kept, got = strips[chunk]
        others, place = ([], 0)
        if len(squares) == chunks - 1:
            others, place = [sums[i] for i in sorted(sums)], chunk
        squares[chunk], sums[chunk] = square(ordered(kept), got, others, place, chunk)
        latest.append(sums[chunk])

    add_up(0)
    more_products(1)
    add_up(1)
    more_own(1)
    scatter(0)
    finish(0)
    add_up(2)
    scatter(1)
    add_up(3)
    finish(1)
    scatter(2)
    scatter(3)
    finish(3)
    finish(2)

    squares = [squares[i] for i in sorted(squares)]
    mine = sums[2]
    others = [swap(mine, "layer", lambda i: i ^ other) for other in range(1, layers)]
    return rescale(squares, [mine, *others], width)


def solution(mesh):
    placed = (
        P("blk", "layer", None),
        P("blk", "layer", None),
        P("blk", None, None),
        P("blk", None, None),
        P("blk", None, None),
    )
    return jax.shard_map(
        shards, mesh=mesh, in_specs=placed, out_specs=P("blk", "layer", None), check_vma=False
    )
```

```python
import functools

import jax
import jax.numpy as jnp
from jax import lax
from jax.experimental import pallas as pl
from jax.experimental.pallas import tpu as pltpu
from jax.sharding import PartitionSpec as P

BS = 256
LANES = 128
HEAD = 16
STEPS = 256.0
TOP = 65534.0
LN2 = 0.6931471805599453
DIRECT = 1
PRODUCT_LIMIT = 24000000
SMALL_LIMIT = 8 * 1024 * 1024
IN_VMEM = pl.BlockSpec(memory_space=pltpu.VMEM)
IN_HBM = pl.BlockSpec(memory_space=pltpu.HBM)


def swap(block, axis, partner):
    return lax.ppermute(block, axis, [(partner(i), i) for i in range(lax.axis_size(axis))])


def after(value, *others):
    return lax.optimization_barrier((value, *others))[0]


def call(kernel, name, operands, in_specs, out_shape, scratch_shapes=(), limit=SMALL_LIMIT):
    return pl.pallas_call(
        kernel,
        out_shape=out_shape,
        in_specs=in_specs,
        out_specs=jax.tree.map(lambda _: IN_VMEM, out_shape),
        scratch_shapes=list(scratch_shapes),
        compiler_params=pltpu.CompilerParams(vmem_limit_bytes=limit),
        cost_estimate=pl.CostEstimate(flops=1, bytes_accessed=1, transcendentals=0),
        name=name,
    )(*operands)


def powers(values):
    largest = jnp.maximum(jnp.max(values, axis=0, keepdims=True), 1e-3)
    return jnp.floor(jnp.log(largest) * (STEPS / LN2)) + 2.0


def code(values, power):
    scaled = values * (TOP * jnp.exp(power * (-LN2 / STEPS)))
    return ((scaled + 0.5).astype(jnp.int32) - 32767).astype(jnp.int16)


def scales(head):
    return jnp.exp(head.astype(jnp.int32).astype(jnp.float32) * (LN2 / STEPS)) * (1.0 / TOP)


def decode(codes, scale):
    return (codes.astype(jnp.int32) + 32767).astype(jnp.float32) * scale


def factor_rows(pattern, column, first, ref):
    place = lax.broadcasted_iota(jnp.int32, (1, ref.shape[1]), 1) // BS
    for u in range(ref.shape[0]):
        row = jnp.zeros((1, ref.shape[1]), jnp.float32)
        for v in range(ref.shape[1] // BS):
            row = jnp.where(place == v, pattern(column + v, first + u).astype(jnp.float32), row)
        ref[u : u + 1, :] = row


def masked(values, factors):
    parts = [
        values[u * BS : (u + 1) * BS] * factors[u : u + 1].astype(values.dtype) for u in range(values.shape[0] // BS)
    ]
    return jnp.concatenate(parts, axis=0) if len(parts) > 1 else parts[0]


def dot(left_side, right_side):
    return lax.dot_general(
        left_side, right_side, (((1,), (0,)), ((), ())), preferred_element_type=jnp.float32
    )


def columns_of(ref, start, count):
    return ref.at[0, :, pl.ds(pl.multiple_of(start * BS, BS), count * BS)]


def blocks_at(block, count=1):
    return pl.ds(pl.multiple_of(block * BS, BS), count * BS)


class Sides:
    def __init__(self, inner, panel):
        odd = lax.rem(lax.axis_index("blk"), 2)
        self.panel = panel
        self.first = lax.axis_index("layer") * (inner // BS)
        self.ext_side, self.int_side = odd * (2 * panel), (1 - odd) * (2 * panel)
        self.ext_rows = odd * panel
        self.columns = {"ext": self.ext_side, "own": panel, "int": self.int_side}


class Coded:
    def __init__(self, refs):
        self.refs = refs
        self.heads = [jnp.zeros((HEAD, ref.shape[1]), jnp.float32) for ref in refs]

    def write_all(self, product, place):
        for i in range(product.shape[0] // BS):
            self.write(product[i * BS : (i + 1) * BS], place + i)

    def write(self, product, place):
        column = 0
        for c, ref in enumerate(self.refs):
            chunk = product[:, column : column + ref.shape[1]]
            column += ref.shape[1]
            power = powers(chunk)
            ref[HEAD + place * BS : HEAD + (place + 1) * BS, :] = code(chunk, power)
            line = lax.broadcasted_iota(jnp.int32, self.heads[c].shape, 0)
            self.heads[c] = jnp.where(line == place, power, self.heads[c])

    def finish(self):
        for ref, head in zip(self.refs, self.heads):
            ref[0:HEAD, :] = head.astype(jnp.int32).astype(jnp.int16)


def first_kernel(a_hbm, b_hbm, c_hbm, flow_hbm, graph_hbm, *rest):
    out_refs, rest = rest[:-12], rest[-12:]
    rows_ref, a_rows_ref, b_rows_ref, c_rows_ref, graph_buf, flow_buf, total, ext_factors, a_ref, b_ref, c_ref, sems = rest
    inner, panel = flow_buf.shape[0], flow_buf.shape[1] // BS // 2
    at = Sides(inner, panel)
    steps = inner // BS
    small = [
        pltpu.make_async_copy(pattern, ref, sems.at[i])
        for i, (pattern, ref) in enumerate(((a_hbm, a_ref), (b_hbm, b_ref), (c_hbm, c_ref)))
    ]
    flows, graphs = [], []
    for t in range(steps):
        rows = slice(t * BS, (t + 1) * BS)
        flow = columns_of(flow_hbm, at.ext_rows, 2 * panel).at[rows]
        graph = columns_of(graph_hbm, at.ext_side, 1).at[rows]
        flows.append(pltpu.make_async_copy(flow, flow_buf.at[rows], sems.at[3 + 2 * t]))
        graphs.append(pltpu.make_async_copy(graph, graph_buf.at[rows], sems.at[4 + 2 * t]))
    for copy in small:
        copy.start()
    for t in range(steps):
        flows[t].start()
        graphs[t].start()
    for copy in small:
        copy.wait()
    factor_rows(lambda column, inner: a_ref[column, 0, inner], 0, at.first, a_rows_ref)
    factor_rows(lambda column, inner: b_ref[column, 0, inner], 0, at.first, b_rows_ref)
    factor_rows(lambda column, row: c_ref[0, column, row], 0, 0, c_rows_ref)
    ext_factors[...] = a_rows_ref[:, blocks_at(at.ext_rows, 2 * panel)]
    right_factors = b_rows_ref[:, blocks_at(at.ext_side)]
    per_dot = min(2, steps)
    for t in range(0, steps, per_dot):
        rows = slice(t * BS, (t + per_dot) * BS)
        for copy in flows[t : t + per_dot] + graphs[t : t + per_dot]:
            copy.wait()
        turned = masked(flow_buf[rows, :], ext_factors[t : t + per_dot]).T
        rows_ref[:, rows] = turned
        product = dot(turned, masked(graph_buf[rows, :], right_factors[t : t + per_dot]))
        if t + per_dot < steps:
            total[...] = product if t == 0 else total[...] + product
    if steps > per_dot:
        total[...] += product
    else:
        total[...] = product
    coded = Coded(out_refs)
    for place, first in ((0, panel), (panel, at.ext_side)):
        for i in range(panel):
            coded.write(total[blocks_at(first - at.ext_rows + i), :], place + i)
    coded.finish()


def first_products(flow_t, graph, a_lines, b_lines, c_lines, widths):
    inner, width = flow_t.shape[1:]
    panel = width // 3
    return call(
        first_kernel,
        "first_products",
        [pltpu.with_memory_space_constraint(x, pltpu.HBM) for x in (a_lines, b_lines, c_lines, flow_t, graph)],
        [IN_HBM] * 5,
        [jax.ShapeDtypeStruct((HEAD + 2 * panel, w), jnp.int16) for w in widths]
        + [
            pltpu.VMEM((2 * panel, inner), flow_t.dtype),
            pltpu.VMEM((inner // BS, width), jnp.float32),
            pltpu.VMEM((inner // BS, width), jnp.float32),
            pltpu.VMEM((width // BS, panel), jnp.float32),
        ],
        [
            pltpu.VMEM((inner, BS), graph.dtype),
            pltpu.VMEM((inner, 2 * panel), flow_t.dtype),
            pltpu.VMEM((2 * panel, BS), jnp.float32),
            pltpu.VMEM((inner // BS, 2 * panel), jnp.float32),
            pltpu.SMEM(a_lines.shape, a_lines.dtype),
            pltpu.SMEM(b_lines.shape, b_lines.dtype),
            pltpu.SMEM(c_lines.shape, c_lines.dtype),
            pltpu.SemaphoreType.DMA((3 + 2 * (inner // BS),)),
        ],
        limit=PRODUCT_LIMIT,
    )


def product_kernel(half, wanted, turns, a_rows_ref, b_rows_ref, graph_ref, ext_rows_ref, side_ref, *rest):
    refs = list(rest)
    inner, panel = graph_ref.shape[1], graph_ref.shape[2] // BS // 3
    at = Sides(inner, panel)
    parts = [part for part in ("ext", "own", "int") if part in wanted]
    outs = {part: [refs.pop(0) for _ in wanted[part]] for part in parts}
    int_rows_ref = side_ref
    if turns:
        int_rows_ref = refs.pop(0)
        place = blocks_at(at.int_side, panel)
        int_rows_ref[...] = masked(side_ref[0, :, place], a_rows_ref[:, place]).T
    coded = {part: Coded(outs[part]) for part in parts if part != "own"}
    right = []
    for part in parts:
        place = blocks_at(at.columns[part] + half)
        right.append(masked(graph_ref[0, :, place], b_rows_ref[:, place]))
    right = jnp.concatenate(right, axis=1) if len(right) > 1 else right[0]
    panels = (
        (panel, ext_rows_ref.at[blocks_at(panel - at.ext_rows, panel)], {"ext": 0, "own": 0, "int": 0}),
        (at.ext_side, ext_rows_ref.at[blocks_at(at.ext_side - at.ext_rows, panel)], {"ext": panel, "own": 0}),
        (at.int_side, int_rows_ref, {"own": 0, "int": panel}),
    )
    for first, source, takers in panels:
        used = [part for part in parts if part in takers]
        if not used:
            continue
        low = parts.index(used[0]) * BS
        for i in range(panel):
            product = dot(source[i * BS : (i + 1) * BS, :], right[:, low : low + len(used) * BS])
            for j, part in enumerate(used):
                piece = product[:, j * BS : (j + 1) * BS]
                if part == "own":
                    outs[part][0][blocks_at(first + i), :] = piece
                else:
                    coded[part].write(piece, takers[part] + i)
    for part in coded:
        coded[part].finish()


def products(a_rows, b_rows, graph, ext_rows, side, half, wanted, turns=False):
    inner, width = graph.shape[1:]
    panel = width // 3
    outs = []
    for part in ("ext", "own", "int"):
        for w in wanted.get(part, ()):
            if part == "own":
                outs.append(jax.ShapeDtypeStruct((width, w), jnp.float32))
            else:
                outs.append(jax.ShapeDtypeStruct((HEAD + 2 * panel, w), jnp.int16))
    if turns:
        outs.append(pltpu.VMEM((panel, inner), graph.dtype))
    return call(
        functools.partial(product_kernel, half, wanted, turns),
        "_".join(wanted) + f"_products_{half}",
        (a_rows, b_rows, graph, ext_rows, side),
        [IN_VMEM] * 5,
        outs,
        limit=PRODUCT_LIMIT,
    )


def send_strip(send_ref, strips, power):
    rows = strips[0].shape[0]
    for j, strip in enumerate(strips):
        send_ref[HEAD + j * rows : HEAD + (j + 1) * rows, :] = code(strip, power)
    send_ref[0:HEAD, :] = jnp.broadcast_to(power, (HEAD, power.shape[1])).astype(jnp.int32).astype(jnp.int16)


def split_strips(total, rows, position, keep_ref, send_refs):
    layer = lax.axis_index("layer")
    if len(send_refs) > 1:
        keep_ref[0] = total[pl.ds(layer * rows, rows), :]
        for other, send_ref in enumerate(send_refs, 1):
            strip = total[pl.ds((layer ^ other) * rows, rows), :]
            send_strip(send_ref, [strip], powers(strip))
        return
    bit = lax.rem(layer // position, 2)
    pairs = keep_ref.shape[0]
    for j in range(pairs):
        keep_ref[j] = total[pl.ds((2 * j + bit) * rows, rows), :]
    away = [total[pl.ds((2 * j + 1 - bit) * rows, rows), :] for j in range(pairs)]
    send_strip(send_refs[0], away, functools.reduce(jnp.maximum, [powers(strip) for strip in away]))


def join_kernel(rows, half, lane, c_ref, own_ref, ext_ref, int_ref, keep_ref, *rest):
    *send_refs, total = rest
    odd = lax.rem(lax.axis_index("blk"), 2)
    panel = own_ref.shape[0] // BS // 3
    lanes = slice(lane, lane + ext_ref.shape[1])
    refs = (ext_ref, int_ref)
    from_mid, from_side = ([[(r, start + i) for i in range(panel)] for r in range(2)] for start in (0, panel))
    middle = [list(both) for both in zip(from_side[0], from_side[1])]
    ext_only, int_only = ([[part] for part in from_mid[r]] for r in range(2))
    odd_parts = int_only + middle + ext_only
    even_parts = ext_only + middle + int_only

    def add(parts):
        scale = [scales(ref[0:HEAD, :]) for ref in refs]
        for v in range(3 * panel):
            kept = c_ref[v : v + 1, half * BS + lane : half * BS + lane + ext_ref.shape[1]]
            block = own_ref[v * BS : (v + 1) * BS, lanes] * kept
            for r, i in parts[v]:
                codes = refs[r][HEAD + i * BS : HEAD + (i + 1) * BS, :]
                block += decode(codes, scale[r][i : i + 1] * kept)
            total[v * BS : (v + 1) * BS, :] = block

    @pl.when(odd == 1)
    def _():
        add(odd_parts)

    @pl.when(odd == 0)
    def _():
        add(even_parts)

    split_strips(total, rows, 1, keep_ref, send_refs)


def strips_shapes(pairs, rows, width, messages=1):
    return [
        jax.ShapeDtypeStruct((pairs, rows, width), jnp.float32),
        *[jax.ShapeDtypeStruct((HEAD + pairs * rows, width), jnp.int16)] * messages,
    ]


def join(own, ext_part, int_part, c_rows, half, lane, layers, direct):
    height = own.shape[0]
    width = int_part.shape[1]
    rows = height // layers
    return call(
        functools.partial(join_kernel, rows, half, lane),
        f"join_{half}_{lane}",
        (c_rows, own, ext_part, int_part),
        [IN_VMEM] * 4,
        strips_shapes(1, rows, width, layers - 1) if direct else strips_shapes(layers // 2, rows, width),
        [pltpu.VMEM((height, width), jnp.float32)],
    )


def halve_kernel(rows, position, kept_ref, got_ref, keep_ref, send_ref, total):
    scale = scales(got_ref[0:HEAD, :])[0:1]
    for j in range(kept_ref.shape[0]):
        codes = got_ref[HEAD + j * rows : HEAD + (j + 1) * rows, :]
        total[j * rows : (j + 1) * rows, :] = kept_ref[j] + decode(codes, scale)
    split_strips(total, rows, position, keep_ref, [send_ref])


def halve(kept, got, position, chunk):
    strips, rows, width = kept.shape
    return call(
        functools.partial(halve_kernel, rows, position),
        f"halve_{position}_{chunk}",
        (kept, got),
        [IN_VMEM] * 2,
        strips_shapes(strips // 2, rows, width),
        [pltpu.VMEM((strips * rows, width), jnp.float32)],
    )


def square_kernel(messages, place, kept_ref, *rest):
    got_refs, others, (square_ref, sums_ref) = rest[:messages], rest[messages:-2], rest[-2:]
    value = kept_ref[0]
    for ref in got_refs:
        value += decode(ref[HEAD:, :], scales(ref[0:HEAD, :])[0:1])
    square = value * value
    square_ref[...] = square
    sums = jnp.broadcast_to(jnp.sum(square, axis=0, keepdims=True), (8, square.shape[1]))
    every = [ref[...] for ref in others]
    sums_ref[...] = jnp.concatenate(every[:place] + [sums] + every[place:], axis=1)


def square(kept, got, others, place, chunk):
    _, rows, width = kept.shape
    return call(
        functools.partial(square_kernel, len(got), place),
        f"square_{chunk}",
        (kept, *got, *others),
        [IN_VMEM] * (1 + len(got) + len(others)),
        [
            jax.ShapeDtypeStruct((rows, width), jnp.float32),
            jax.ShapeDtypeStruct((8, width + sum(sums.shape[1] for sums in others)), jnp.float32),
        ],
    )


def rescale_kernel(height, count, *refs):
    squares, sums, (out_ref, buf, sems) = refs[:count], refs[count:-3], refs[-3:]
    total = functools.reduce(jnp.add, [ref[0:1, :] for ref in sums])
    factor = 1.0 / (total / height + 1e-6)
    groups = sems.shape[0]
    depth = buf.shape[1] // groups
    copies = []
    for g in range(groups):
        rows = slice(g * depth, (g + 1) * depth)
        column = 0
        for ref in squares:
            columns = slice(column, column + ref.shape[1])
            column += ref.shape[1]
            buf[0, rows, columns] = ref[rows, :] * factor[:, columns]
        copies.append(pltpu.make_async_copy(buf.at[0, rows], out_ref.at[0, rows], sems.at[g]))
        copies[-1].start()
    for copy in copies:
        copy.wait()


def rescale(squares, sums, height):
    rows = squares[0].shape[0]
    shape = (1, rows, sums[0].shape[1])
    groups = 4 if rows % 32 == 0 else 1
    return pl.pallas_call(
        functools.partial(rescale_kernel, float(height), len(squares)),
        out_shape=jax.ShapeDtypeStruct(shape, jnp.float32),
        in_specs=[IN_VMEM] * (len(squares) + len(sums)),
        out_specs=IN_HBM,
        scratch_shapes=[pltpu.VMEM(shape, jnp.float32), pltpu.SemaphoreType.DMA((groups,))],
        compiler_params=pltpu.CompilerParams(vmem_limit_bytes=SMALL_LIMIT),
        cost_estimate=pl.CostEstimate(flops=1, bytes_accessed=1, transcendentals=0),
        name="rescale",
    )(*squares, *sums)


def shards(flow_t, graph, a_pattern, b_pattern, c_pattern):
    layers = lax.axis_size("layer")
    blks = lax.axis_size("blk")
    width = flow_t.shape[2]
    panel = width // 3
    a_lines = a_pattern.transpose(2, 0, 1)
    b_lines = b_pattern.transpose(2, 0, 1)
    c_lines = c_pattern.transpose(0, 2, 1)

    def other_chip(i):
        return (i + 1 if i % 2 else i - 1) % blks

    def same_chip(i):
        return i ^ 1

    halves = panel // BS
    chunks = panel // LANES
    fine = (LANES,) * (BS // LANES)
    per_half = len(fine)
    ext, ints, owns, latest = [], [], [], []

    def ordered(value):
        return after(value, latest[-1])

    def send_ext(parts):
        ext.extend(swap(part, "blk", other_chip) for part in parts)
        latest.append(parts[0])

    def send_int(parts):
        ints.extend(swap(part, "blk", same_chip) for part in parts)
        latest.append(parts[0])

    *parts, ext_rows, a_rows, b_rows, c_rows = first_products(flow_t, graph, a_lines, b_lines, c_lines, fine)
    send_ext(parts)
    wanted = {"own": (BS,), "int": fine}
    own, *parts, int_rows = products(a_rows, ordered(b_rows), graph, ext_rows, flow_t, 0, wanted, turns=True)
    owns.append(own)
    send_int(parts)

    def more_products(half):
        wanted = {"ext": fine, "int": fine}
        parts = products(a_rows, ordered(b_rows), graph, ext_rows, int_rows, half, wanted)
        send_ext(parts[:per_half])
        send_int(parts[per_half:])

    def more_own(half):
        owns.extend(products(a_rows, ordered(b_rows), graph, ext_rows, int_rows, half, {"own": (BS,)}))
        latest.append(owns[-1])

    strips, squares, sums = [], {}, {}

    def add_up(chunk):
        half, lane = divmod(chunk, per_half)
        direct = chunk < DIRECT and layers <= 4
        kept, *sends = join(
            owns[half], ext[chunk], ints[chunk], ordered(c_rows), half, lane * LANES, layers, direct
        )
        latest.append(kept)
        strips.append((kept, [swap(send, "layer", lambda i: i ^ other) for other, send in enumerate(sends, 1)]))

    def scatter(chunk):
        kept, got = strips[chunk]
        position = 1
        while kept.shape[0] > 1:
            position *= 2
            kept, send = halve(ordered(kept), got[0], position, chunk)
            latest.append(kept)
            got = [swap(send, "layer", lambda i: i ^ position)]
        strips[chunk] = kept, got

    def finish(chunk):
        kept, got = strips[chunk]
        others, place = ([], 0)
        if len(squares) == chunks - 1:
            others, place = [sums[i] for i in sorted(sums)], chunk
        squares[chunk], sums[chunk] = square(ordered(kept), got, others, place, chunk)
        latest.append(sums[chunk])

    add_up(0)
    more_products(1)
    add_up(1)
    more_own(1)
    scatter(0)
    finish(0)
    add_up(2)
    scatter(1)
    add_up(3)
    scatter(2)
    scatter(3)
    finish(1)
    finish(2)
    finish(3)

    squares = [squares[i] for i in sorted(squares)]
    mine = sums[3]
    others = [swap(mine, "layer", lambda i: i ^ other) for other in range(1, layers)]
    return rescale(squares, [mine, *others], width)


def solution(mesh):
    placed = (
        P("blk", "layer", None),
        P("blk", "layer", None),
        P("blk", None, None),
        P("blk", None, None),
        P("blk", None, None),
    )
    return jax.shard_map(
        shards, mesh=mesh, in_specs=placed, out_specs=P("blk", "layer", None), check_vma=False
    )
```
